32 devices in a mesh: groups: 2 (over y), tm: 4 (over z), space: 2 (over x), chan: 2 (over core).
Axes of the slice: x: 2, y: 2, z: 4, core: 2. Of those that a mesh axis runs over, the one named last changes fastest.
Arguments:
- activations: bfloat16 [256, 8, 16, 256], P(('groups', 'chan'), 'tm', 'space'), parts along dimension 0
- frame_clip: int32 [16], P(('groups', 'tm')), parts along dimension 0, may hold values from 0 to 3, as said below
- conv_weight: bfloat16 [3, 3, 3, 128, 128], replicated, may hold values from -0.109375 to 0.109375
- norm_gain: float32 [128], replicated, may hold values from 0.25 to 1.75
- norm_bias: float32 [128], replicated, may hold values from -3 to 3
- out_weight: bfloat16 [2, 2, 128, 32], replicated, may hold values from -0.25 to 0.25
- owner: int32 [4, 32, 1], P(('groups', 'space'), 'tm'), parts along dimension 0, may hold values from 0 to 3; in each aligned block of 8 rows (0 to 7, 8 to 15, ..., all dimensions but the last counted through in order) at most 4 rows name the same one
Outputs:
- owned: bfloat16 [4, 64, 32, 128], P(('groups', 'space'), 'tm', 'chan'), parts along dimension 0
The draws below stay inside these ranges and needn't reach their ends.
There are 2 independent parts, one for each index of `groups`. The reference program is written for one: setup_inputs(seed, part) draws one part's arguments, and reference() takes and returns one part's arrays. A program takes and returns all parts, laid end to end along the dimension named above; an argument that names none is the same for every part. Nothing has to cross between parts.
Inputs may be any that keep to these rules, and one draw needn't show every extreme that they name: `frame_clip`: clip numbers never fall along the frames; each clip has 1 to 4 frames and one has exactly 4. Among the 8 rows of one tm index (aligned blocks), no owner is named more than 4 times; some owner is named exactly 4 times in some block.
All inputs are finite; a program needn't handle non-finite values.
Results may differ from the reference program's by a relative error of at most 0.012.
Values may be sent and summed in bfloat16 or wider, within the bound.
No kernel may reach another device: no remote copies, remote signals or barrier semaphores. Data moves between devices by JAX's collectives and lax.ppermute only.
A program may use at most 64 MiB of HBM per device.

```python
import math
import jax
import jax.numpy as jnp
import numpy as np
from jax import lax

CHANNELS = 128
GROUPS = 32
COLUMNS = 256
CLIPS = 4
MOMENTS = 32
HALF_ROWS = 4
HALF_COLS = 128
SEND_ROWS = 8
FRAMES = 8
HEIGHT = 16
LONGEST = 4
CAPACITY = 4
N_TM = 4
N_SPACE = 2


def draw_activations(key, part):
    key_base, key_rows, key_chan = jax.random.split(key, 3)
    frame_pos = jnp.arange(FRAMES, dtype=jnp.float32) / max(FRAMES - 1, 1)
    frame_scale = jnp.exp(jnp.log(3.0) * frame_pos)
    shape = (CHANNELS, FRAMES, HEIGHT, COLUMNS)
    base = jnp.clip(jax.random.normal(key_base, shape, jnp.float32), -6.0, 6.0)
    row_scale = jnp.exp(jax.random.uniform(key_rows, (1, FRAMES, HEIGHT, 1), jnp.float32, jnp.log(0.5), jnp.log(5.0)))
    chan_scale = jnp.exp(jax.random.uniform(key_chan, (CHANNELS, 1, 1, 1), jnp.float32, jnp.log(0.5), jnp.log(2.0)))
    return (base * row_scale * chan_scale * frame_scale[None, :, None, None]).astype(jnp.bfloat16)


def draw_frame_clip(key, part):
    key_cuts, key_place = jax.random.split(jax.random.fold_in(key, 7), 2)
    remain = FRAMES - LONGEST
    picked = jax.random.permutation(key_cuts, remain - 1)[:CLIPS - 2] + 1
    cuts = jnp.sort(picked).astype(jnp.int32)
    bounds = jnp.concatenate([jnp.zeros((1,), jnp.int32), cuts, jnp.full((1,), remain, jnp.int32)])
    others = bounds[1:] - bounds[:-1]
    place = jax.random.randint(key_place, (), 0, CLIPS, dtype=jnp.int32)
    index = jnp.arange(CLIPS, dtype=jnp.int32)
    other_index = jnp.clip(index - (index > place).astype(jnp.int32), 0, CLIPS - 2)
    lengths = jnp.where(index == place, LONGEST, others[other_index]).astype(jnp.int32)
    ends = jnp.cumsum(lengths).astype(jnp.int32)
    frames = jnp.arange(FRAMES, dtype=jnp.int32)
    return jnp.sum((frames[:, None] >= ends[None, :CLIPS - 1]).astype(jnp.int32), axis=1).astype(jnp.int32)


def shared_out(rng, own, number, rows, count, top, bound, slope):
    ranking = jax.random.permutation(rng, count)
    heavy_load, usual = load_shares(count, rows * top, bound, slope, True), load_shares(count, rows * top, bound, slope, False)
    places = jnp.arange(count)

    def named(sizes, turn):
        used = int((sizes > 0).sum())
        fixed = max(1, used // 4)
        shifted = fixed + (places - fixed + turn * (used - fixed)) % max(1, count - fixed)
        return jnp.zeros((count,), jnp.int32).at[ranking[jnp.where(places < fixed, places, shifted)]].set(jnp.asarray(sizes, jnp.int32))

    sizes = jnp.where(number % 4 == 0, named(heavy_load, number // 4), named(usual, number - number // 4 - 1))
    mixed = jax.random.permutation(jax.random.fold_in(own, 3), count)
    giver, receiver = mixed[0:count // 2 * 2:2], mixed[1:count // 2 * 2:2]
    margin = jnp.minimum(sizes[giver] - 1, bound - sizes[receiver]) // 2
    margin = jnp.where((giver == ranking[0]) | (receiver == ranking[0]) | (sizes[receiver] == 0), 0, jnp.maximum(margin, 0))
    shifted = jax.random.randint(jax.random.fold_in(own, 4), (count // 2,), 0, 1 << 20) % (margin + 1)
    sizes = sizes.at[giver].add(-shifted).at[receiver].add(shifted)
    items = jnp.searchsorted(jnp.cumsum(sizes), jnp.arange(rows * top), side="right").astype(jnp.int32)
    grid = items.reshape(top, rows).T
    grid = grid[jax.random.permutation(jax.random.fold_in(own, 1), rows)]
    turn = jax.random.randint(jax.random.fold_in(own, 2), (rows, 1), 0, top)
    return jnp.take_along_axis(grid, (jnp.arange(top)[None, :] + turn) % top, axis=1)


def load_shares(amount, total, reach, slope, full):
    loads = [(1 << 20) // math.isqrt(standing ** slope) + 1 for standing in range(1, amount + 1)]
    largest = reach if full else min(reach, max(-(-total // amount), total * loads[0] // sum(loads)))
    least = 1 if total - largest >= amount - 1 else 0
    given, rest = [largest] + [least] * (amount - 1), total - largest - least * (amount - 1)
    while rest > 0:
        movable = [i for i in range(1, amount) if given[i] < largest] or [i for i in range(1, amount) if given[i] < reach]
        whole, budget = sum([loads[i] for i in movable]), rest
        for i in movable:
            more = min(reach - given[i], max(1, budget * loads[i] // whole), rest)
            given[i] = given[i] + more
            rest = rest - more
    return np.array(given)


def noise(rng, shape, spread, bound, kind=jnp.bfloat16):
    drawn = jax.random.normal(rng, shape, jnp.float32) * spread
    return jnp.minimum(jnp.maximum(drawn, -bound), bound).astype(kind)


def setup_inputs(seed: int = 0, part: int = 0) -> dict:
    key_list = jax.random.split(jax.random.key(seed), 8)
    part_splits = jax.random.split(jax.random.fold_in(key_list[7], part), 8)
    activations = draw_activations(jax.random.fold_in(jax.random.fold_in(key_list[7], part), 71), part)
    frame_clip = draw_frame_clip(jax.random.fold_in(jax.random.fold_in(key_list[7], part), 71), part)
    conv_weight = noise(key_list[2], (3, 3, 3, CHANNELS, CHANNELS), (27 * CHANNELS) ** -0.5, 0.109375)
    norm_gain = jnp.clip(1.0 + 0.15 * jax.random.normal(key_list[3], (CHANNELS,), jnp.float32), 0.25, 1.75)
    norm_bias = noise(key_list[4], (CHANNELS,), 0.5, 3.0, jnp.float32)
    out_weight = noise(key_list[5], (2, 2, CHANNELS, MOMENTS), (4 * CHANNELS) ** -0.5, 0.25)
    owner_keys = jax.random.split(jax.random.fold_in(part_splits[6], 1), N_SPACE * (FRAMES * HALF_ROWS) // SEND_ROWS)
    owner_turns = jax.random.permutation(jax.random.fold_in(part_splits[6], 3), N_SPACE * (FRAMES * HALF_ROWS) // SEND_ROWS)
    owner = jax.vmap(lambda own, number: shared_out(jax.random.fold_in(part_splits[6], 2), own, number, SEND_ROWS, N_TM, 1, CAPACITY, 2))(owner_keys, owner_turns).reshape((N_SPACE, FRAMES * HALF_ROWS, 1))
    return dict(activations=activations, frame_clip=frame_clip, conv_weight=conv_weight, norm_gain=norm_gain, norm_bias=norm_bias, out_weight=out_weight, owner=owner)


def tap_list(clip_ids):
    frame_total = clip_ids.shape[0]
    position = jnp.arange(frame_total, dtype=jnp.int32)
    padded_ids = jnp.concatenate([jnp.full((2,), -1, jnp.int32), clip_ids])
    matches = [(padded_ids[m:m + frame_total] == clip_ids).astype(jnp.int32) for m in range(3)]
    result = []
    for k in range(3):
        number = matches[k]
        for m in range(k + 1, 3):
            number = number + matches[m]
        result.append(position + 1 - number)
    return result

def plane_conv(frames, kernel):
    return lax.conv_general_dilated(frames, kernel, (1, 1), ((1, 1), (1, 1)), dimension_numbers=('CNHW', 'HWIO', 'CNHW'), precision=lax.Precision.HIGHEST)

def reference(activations, frame_clip, conv_weight, norm_gain, norm_bias, out_weight, owner):
    source = activations.astype(jnp.float32)
    kernels = conv_weight.astype(jnp.float32)
    conv = jnp.zeros(activations.shape, jnp.float32)
    for k, tap_index in enumerate(tap_list(frame_clip)):
        conv = conv + plane_conv(jnp.take(source, tap_index, axis=1), kernels[k])
    conv = conv.astype(jnp.bfloat16).astype(jnp.float32)
    group_size = CHANNELS // GROUPS
    onehot = (frame_clip[:, None] == jnp.arange(CLIPS, dtype=jnp.int32)[None, :]).astype(jnp.float32)
    sums_one = lax.optimization_barrier(jnp.sum(conv, axis=(2, 3))).reshape(GROUPS, group_size, FRAMES).sum(1)
    sums_two = lax.optimization_barrier(jnp.sum(conv * conv, axis=(2, 3))).reshape(GROUPS, group_size, FRAMES).sum(1)
    sums_one = jnp.dot(sums_one, onehot, precision=lax.Precision.HIGHEST)
    sums_two = jnp.dot(sums_two, onehot, precision=lax.Precision.HIGHEST)
    counts = lax.optimization_barrier(jnp.sum(onehot, axis=0)) * (HEIGHT * COLUMNS * group_size)
    mean = sums_one / counts
    rstd = lax.rsqrt(sums_two / counts - mean * mean + 1e-06)
    mean_frame = jnp.repeat(jnp.dot(mean, onehot.T, precision=lax.Precision.HIGHEST), group_size, axis=0)
    rstd_frame = jnp.repeat(jnp.dot(rstd, onehot.T, precision=lax.Precision.HIGHEST), group_size, axis=0)
    scaled = (conv - mean_frame[:, :, None, None]) * rstd_frame[:, :, None, None]
    normed = jax.nn.silu(scaled * norm_gain[:, None, None, None] + norm_bias[:, None, None, None]).astype(jnp.bfloat16)
    patches = normed.astype(jnp.float32).reshape(CHANNELS, FRAMES, HEIGHT // 2, 2, HALF_COLS, 2)
    latent = jnp.einsum('cfrizj,ijco->ofrz', patches, out_weight.astype(jnp.float32), precision=lax.Precision.HIGHEST).astype(jnp.bfloat16)
    row_block = latent.reshape(MOMENTS, FRAMES, N_SPACE, HALF_ROWS, HALF_COLS)
    row_block = row_block.transpose(2, 1, 3, 0, 4).reshape(N_SPACE, FRAMES * HALF_ROWS, MOMENTS, HALF_COLS)
    blocks = owner[:, :, 0].reshape(N_SPACE, N_TM, SEND_ROWS)
    earlier = jnp.arange(SEND_ROWS)[None, :] < jnp.arange(SEND_ROWS)[:, None]
    equal = blocks[:, :, :, None] == blocks[:, :, None, :]
    order_rank = lax.optimization_barrier(jnp.sum((equal & earlier[None, None]).astype(jnp.int32), axis=3))
    target = blocks * (N_TM * CAPACITY) + jnp.arange(N_TM, dtype=jnp.int32)[None, :, None] * CAPACITY + order_rank
    target = target.reshape(N_SPACE, FRAMES * HALF_ROWS)
    owned = jnp.zeros((N_SPACE, N_TM * N_TM * CAPACITY, MOMENTS, HALF_COLS), jnp.bfloat16)
    owned = owned.at[jnp.arange(N_SPACE)[:, None], target].set(row_block)
    return owned
```

```python
import jax
import jax.numpy as jnp
from jax import lax
from jax.sharding import PartitionSpec as P

CHANNELS = 128
GROUPS = 32
CLIPS = 4
MOMENTS = 32


def shifted(value, axis, steps):
    count = lax.axis_size(axis)
    leading, last = (max(0, -steps), min(count, count - steps))
    return lax.ppermute(value, axis, [(source, source + steps) for source in range(leading, last)])


def with_halo(block, sides, width):
    for axis, dim in sides:
        count = lax.axis_size(axis)
        forward = [(i, i + 1) for i in range(count - 1)]
        backward = [(target, source) for source, target in forward]
        low = lax.ppermute(
            lax.slice_in_dim(block, block.shape[dim] - width, None, axis=dim), axis, forward
        )
        high = lax.ppermute(lax.slice_in_dim(block, 0, width, axis=dim), axis, backward)
        block = jnp.concatenate([low, block, high], axis=dim)
    return block


def plane_conv(frames, kernel):
    return lax.conv_general_dilated(
        frames,
        kernel,
        (1, 1),
        ((0, 0), (1, 1)),
        dimension_numbers=("CNHW", "HWIO", "CNHW"),
        preferred_element_type=jnp.float32,
    )


def shards(activations, frame_clip, conv_weight, norm_gain, norm_bias, out_weight, owner):
    c_local, frames_here, rows_here, columns = activations.shape
    chan_index = lax.axis_index("chan")
    chan_first = chan_index * c_local
    trailing_ids = (frame_clip + 1).astype(jnp.bfloat16)
    previous, previous_ids = shifted((activations, trailing_ids), "tm", 1)
    extended = jnp.concatenate([previous, activations], axis=1)
    extended_ids = jnp.concatenate(
        [previous_ids.astype(jnp.float32), (frame_clip + 1).astype(jnp.float32)]
    )
    padded = with_halo(extended, (("space", 2),), 1)
    own_ids = extended_ids[2:]
    matches = [(extended_ids[m : m + frames_here] == own_ids).astype(jnp.int32) for m in range(3)]
    position = jnp.arange(frames_here, dtype=jnp.int32)
    tap_index = []
    for k in range(3):
        number = matches[k]
        for m in range(k + 1, 3):
            number = number + matches[m]
        tap_index.append(position + 3 - number)
    chan_count = lax.axis_size("chan")
    window = frames_here // chan_count
    windows = jnp.stack(
        [padded[:, w * window : w * window + window + 2] for w in range(chan_count)], axis=1
    )
    whole_window = lax.all_to_all(windows, "chan", split_axis=1, concat_axis=0, tiled=True)[:, 0]
    window_start = chan_index * window
    running = None
    for k in range(3):
        local_taps = lax.dynamic_slice_in_dim(tap_index[k], window_start, window) - window_start
        term = plane_conv(jnp.take(whole_window, local_taps, axis=1), conv_weight[k])
        running = term if running is None else running + term
    conv_value = running.astype(jnp.bfloat16).astype(jnp.float32)
    tm_size = lax.axis_size("tm")
    parts = tm_size * lax.axis_size("space") * chan_count
    group_size = CHANNELS // GROUPS
    send_rows = frames_here * (rows_here // 2)
    sums_one = jnp.sum(conv_value, axis=(2, 3)).reshape(GROUPS, group_size, window).sum(1)
    sums_two = jnp.sum(conv_value * conv_value, axis=(2, 3)).reshape(GROUPS, group_size, window).sum(1)
    own_clip = lax.dynamic_slice_in_dim(frame_clip, window_start, window).astype(jnp.float32)
    pieces = [sums_one.reshape(-1), sums_two.reshape(-1), own_clip, owner.reshape(-1).astype(jnp.float32)]
    message = jnp.concatenate(pieces)
    size = message.shape[0]
    message = jnp.pad(message, (0, -size % 128)).reshape(1, -1, 128)
    gathered = lax.all_to_all(
        jnp.broadcast_to(message, (parts,) + message.shape[1:]),
        ("tm", "space", "chan"),
        split_axis=0,
        concat_axis=0,
        tiled=True,
    ).reshape(parts, -1)
    first = GROUPS * window
    all_one = gathered[:, :first].reshape(parts, GROUPS, window)
    all_two = gathered[:, first : 2 * first].reshape(parts, GROUPS, window)
    all_clip = gathered[:, 2 * first : 2 * first + window]
    all_owner = gathered[:, 2 * first + window : 2 * first + window + send_rows].astype(jnp.int32)
    same = (all_clip[:, None, :] == own_clip[None, :, None]).astype(jnp.float32)
    total_one = jnp.einsum("pgw,pvw->gv", all_one, same, precision=lax.Precision.HIGHEST)
    total_two = jnp.einsum("pgw,pvw->gv", all_two, same, precision=lax.Precision.HIGHEST)
    counts = jnp.sum(same, axis=(0, 2)) * (rows_here * columns * group_size)
    mean = total_one / counts
    rstd = lax.rsqrt(total_two / counts - mean * mean + 1e-06)
    mean_frame = jnp.repeat(mean, group_size, axis=0)
    rstd_frame = jnp.repeat(rstd, group_size, axis=0)
    scaled = (conv_value - mean_frame[:, :, None, None]) * rstd_frame[:, :, None, None]
    normed = jax.nn.silu(
        scaled * norm_gain[:, None, None, None] + norm_bias[:, None, None, None]
    ).astype(jnp.bfloat16)
    patches = normed.reshape(CHANNELS, window, rows_here // 2, 2, columns // 2, 2)
    latent = jnp.einsum(
        "cfrizj,ijco->froz",
        patches,
        out_weight,
        preferred_element_type=jnp.float32,
    ).astype(jnp.bfloat16)
    half = MOMENTS // chan_count
    rows = latent.reshape(window * (rows_here // 2), chan_count, half, columns // 2)
    outgoing = jnp.broadcast_to(
        rows.transpose(1, 0, 2, 3)[None], (tm_size,) + (chan_count, rows.shape[0], half, columns // 2)
    ).reshape((tm_size * chan_count,) + (rows.shape[0], half, columns // 2))
    arrived = lax.all_to_all(outgoing, ("tm", "chan"), split_axis=0, concat_axis=0, tiled=True)
    arrived = arrived.reshape(tm_size * send_rows, half * (columns // 2))
    capacity = max(2, 2 * send_rows // tm_size)
    own_space = all_owner.reshape(tm_size, -1, chan_count, send_rows)
    own_space = lax.dynamic_index_in_dim(own_space, lax.axis_index("space"), 1, keepdims=False)[:, 0]
    earlier = jnp.arange(send_rows)[None, :] < jnp.arange(send_rows)[:, None]
    equal = own_space[:, :, None] == own_space[:, None, :]
    rank = jnp.sum((equal & earlier[None]).astype(jnp.int32), axis=2)
    slot = jnp.arange(tm_size)[:, None] * capacity + rank
    slot = jnp.where(own_space == lax.axis_index("tm"), slot, -1).reshape(-1)
    selector = (slot[None, :] == jnp.arange(tm_size * capacity)[:, None]).astype(jnp.bfloat16)
    owned = jnp.dot(selector, arrived, preferred_element_type=jnp.float32).astype(jnp.bfloat16)
    return owned.reshape(1, tm_size * capacity, half, columns // 2)


def solution(mesh):
    placed = (
        P(("groups", "chan"), "tm", "space", None),
        P(("groups", "tm")),
        P(),
        P(),
        P(),
        P(),
        P(("groups", "space"), "tm", None),
    )
    return jax.shard_map(
        shards,
        mesh=mesh,
        in_specs=placed,
        out_specs=P(("groups", "space"), "tm", "chan", None),
        check_vma=False,
    )
```

```python
import jax
import jax.numpy as jnp
import numpy as np
from jax import lax
from jax.experimental import pallas as pl
from jax.experimental.pallas import tpu as pltpu
from jax.sharding import PartitionSpec as P

CHANNELS = 128
GROUPS = 32
MOMENTS = 32
ID_ROWS = 16
BF16 = jnp.bfloat16
F32 = jnp.float32
VMEM = pl.BlockSpec(memory_space=pltpu.VMEM)
SMEM = pl.BlockSpec(memory_space=pltpu.SMEM)
PARAMS = pltpu.CompilerParams(vmem_limit_bytes=40 * 1024 * 1024)
PART = ("tm", "space", "chan")


def flat_pairs(sizes, pairs):
    _, spaces, chans = sizes
    return [
        ((a[0] * spaces + a[1]) * chans + a[2], (b[0] * spaces + b[1]) * chans + b[2])
        for a, b in pairs
    ]


def space_swap(value, sizes, odd):
    slabs, spaces, chans = sizes
    pairs = []
    for low in range(odd, spaces - 1, 2):
        for t in range(slabs):
            for c in range(chans):
                pairs += [((t, low, c), (t, low + 1, c)), ((t, low + 1, c), (t, low, c))]
    return lax.ppermute(value, PART, flat_pairs(sizes, pairs))


def slab_swap(value, sizes, cross):
    slabs, spaces, _ = sizes
    pairs = []
    for t in range(slabs - 1):
        for s in range(spaces):
            if cross:
                pairs += [((t, s, 0), (t + 1, s, 1)), ((t + 1, s, 1), (t, s, 0))]
            else:
                pairs += [((t, s, 1), (t + 1, s, 1)), ((t + 1, s, 0), (t, s, 0))]
    return lax.ppermute(value, PART, flat_pairs(sizes, pairs))


def whole_call(kernel, out_shape, specs, args):
    return pl.pallas_call(
        kernel,
        out_shape=out_shape,
        in_specs=specs,
        out_specs=jax.tree.map(lambda _: VMEM, out_shape),
        compiler_params=PARAMS,
    )(*args)


def pack_kernel(halos, where_ref, ids_ref, frames_ref, *refs):
    halo_refs, (cross_ref, same_ref) = refs[:halos], refs[halos:]
    chan = where_ref[2]
    _, rows, half, columns = frames_ref.shape
    source = lax.broadcasted_iota(jnp.int32, (columns, columns), 0)
    target = lax.broadcasted_iota(jnp.int32, (columns, columns), 1)
    wanted = jnp.where(target < columns // 2, 2 * target, 2 * target - columns + 1)
    split = jnp.where(source == wanted, 1.0, 0.0).astype(BF16)

    def parted(value):
        return jnp.dot(value, split, preferred_element_type=F32).astype(BF16)

    for out_ref, frame in ((cross_ref, 1 - chan), (same_ref, chan)):
        for r in range(rows):
            out_ref[r * half : (r + 1) * half, :] = parted(frames_ref[frame, r])
        for h in range(halos):
            first = (rows + h) * half
            out_ref[first : first + half, :] = parted(halo_refs[h][frame])
        number = (ids_ref[frame] + 1).astype(F32)
        out_ref[(rows + halos) * half :, :] = jnp.full((ID_ROWS, columns), number, F32).astype(BF16)


def weights_kernel(where_ref, ids_ref, weight_ref, local_ref, late_ref, sum_ref):
    chan = where_ref[2]
    half = CHANNELS // 2
    zero = jnp.float32(0.0)
    one = jnp.float32(1.0)
    first = chan == 0
    joined = ids_ref[0] == ids_ref[1]
    flag = jnp.where(joined, one, zero)
    on_first = jnp.where(first, one, zero)
    on_second = one - on_first
    near = (
        on_first * (one - flag),
        on_first + on_second * flag,
        zero,
    )
    far = (
        on_first * flag + on_second * (one - flag),
        on_second * (one - flag),
        on_second,
    )
    late_same = (on_second * flag, zero, on_first)
    late_apart = (on_first + on_second * flag, on_first, on_first)
    own = pl.multiple_of(chan * half, half)
    other = pl.multiple_of((1 - chan) * half, half)
    for j in range(3):
        for i in range(3):
            taps = []
            for k in range(3):
                block = jnp.concatenate(
                    [weight_ref[k, i, j, pl.ds(own, half), :], weight_ref[k, i, j, pl.ds(other, half), :]],
                    axis=0,
                )
                taps.append(block.astype(F32).T)

            def mixed(scale):
                return (taps[0] * scale[0] + taps[1] * scale[1] + taps[2] * scale[2]).astype(BF16)

            rows = slice(j * CHANNELS, (j + 1) * CHANNELS)
            columns = slice(i * CHANNELS, (i + 1) * CHANNELS)
            shifted = slice((3 + i) * CHANNELS, (4 + i) * CHANNELS)
            local_ref[rows, columns] = mixed(near)
            local_ref[rows, shifted] = mixed(far)
            late_ref[0, rows, columns] = mixed(late_same)
            late_ref[1, rows, columns] = mixed(late_apart)
            sum_ref[rows, columns] = mixed((one, one, one))


def image_row(own_ref, other_ref, rows, halos, odd, r):
    half = CHANNELS // 2

    def slab(ref, n):
        return ref[n * half : (n + 1) * half, :]

    pieces = []
    for ref in (own_ref, other_ref):
        if 0 <= r < rows:
            pieces.append(slab(ref, r))
            continue
        first = slab(ref, rows)
        second = slab(ref, rows + 1) if halos > 1 else jnp.zeros_like(first)
        on_first = odd if r < 0 else jnp.logical_not(odd)
        pieces.append(jnp.where(on_first, first, second))
    return jnp.concatenate(pieces, axis=0)


def joined_columns(product):
    half = product.shape[1] // 2
    left = product[:CHANNELS, :]
    middle = product[CHANNELS : 2 * CHANNELS, :]
    right = product[2 * CHANNELS :, :]
    lane = lax.broadcasted_iota(jnp.int32, (CHANNELS, half), 1)
    from_left = jnp.where(lane == 0, 0.0, pltpu.roll(left[:, half:], 1, 1))
    from_right = jnp.where(lane == half - 1, 0.0, pltpu.roll(right[:, :half], half - 1, 1))
    even = from_left + middle[:, :half] + right[:, half:]
    odd = left[:, :half] + middle[:, half:] + from_right
    return even, odd


def lane_totals(first, second):
    rows = [jnp.sum(value.T, axis=0, keepdims=True) for value in (first, second)]
    return rows


def local_kernel(
    rows, halos, where_ref, weight_ref, sum_ref, cross_ref, same_ref, cross_other_ref, same_other_ref,
    conv_ref, extra_ref, sums_ref,
):
    odd = lax.rem(where_ref[1], 2) == 1
    chan = where_ref[2]
    near = [image_row(cross_ref, same_other_ref, rows, halos, odd, r) for r in range(-1, rows + 1)]
    far = [image_row(same_ref, cross_other_ref, rows, halos, odd, r) for r in range(-1, rows + 1)]
    half = near[0].shape[1] // 2
    for r in range(rows):
        image = jnp.concatenate(near[r : r + 3] + far[r : r + 3], axis=0)
        product = jnp.dot(weight_ref[...], image, preferred_element_type=F32)
        even, late = joined_columns(product)
        conv_ref[r, :, :half] = even
        conv_ref[r, :, half:] = late
    sums_ref[...] = jnp.zeros_like(sums_ref)

    @pl.when(where_ref[0] > 0)
    def _():
        extra_ref[...] = jnp.zeros_like(extra_ref)

    for c in range(2):

        @pl.when((where_ref[0] == 0) & (chan == c))
        def _():
            totals = [jnp.zeros((CHANNELS, half), F32)] * 2
            start = c * (rows // 2)
            for r in range(rows // 2):
                images = far if c == 0 else near
                image = jnp.concatenate(images[start + r : start + r + 3], axis=0)
                product = jnp.dot(sum_ref[...], image, preferred_element_type=F32)
                for side, value in enumerate(joined_columns(product)):
                    value = value.astype(BF16)
                    extra_ref[r, :, side * half : (side + 1) * half] = value
                    value = value.astype(F32)
                    totals = [totals[0] + value, totals[1] + value * value]
            one, two = lane_totals(*totals)
            sums_ref[0:1, :] = one
            sums_ref[1:2, :] = two


def late_kernel(
    rows, halos, slabs, where_ref, ids_ref, owner_ref, weight_ref, part_ref, cross_ref, same_other_ref,
    late_own_ref, late_other_ref, sums_ref, conv_ref, message_ref,
):
    odd = lax.rem(where_ref[1], 2) == 1
    slab = where_ref[0]
    chan = where_ref[2]
    half = part_ref.shape[2] // 2
    tail = (rows + halos) * (CHANNELS // 2)
    number = jnp.max(late_own_ref[tail:, :].astype(F32)).astype(jnp.int32) - 1
    first = chan == 0
    same = jnp.where(first, number == ids_ref[1], number == ids_ref[0])
    keep = jnp.where(jnp.logical_or(same, jnp.logical_not(first)), 1.0, 0.0)
    use_late = jnp.logical_or(same, first)
    choice = jnp.where(same, 0, 1)
    weight = weight_ref[choice]
    images = []
    for r in range(-1, rows + 1):
        late = image_row(late_own_ref, late_other_ref, rows, halos, odd, r)
        here = image_row(cross_ref, same_other_ref, rows, halos, odd, r)
        images.append(jnp.where(use_late, late, here))
    totals = [jnp.zeros((CHANNELS, half), F32)] * 2
    for r in range(rows):
        image = jnp.concatenate(images[r : r + 3], axis=0)
        product = jnp.dot(weight, image, preferred_element_type=F32)
        for side, value in enumerate(joined_columns(product)):
            lanes = slice(side * half, (side + 1) * half)
            value = (value + keep * part_ref[r, :, lanes]).astype(BF16)
            conv_ref[r, :, lanes] = value
            value = value.astype(F32)
            totals = [totals[0] + value, totals[1] + value * value]
    one, two = lane_totals(*totals)
    absent = jnp.logical_and(first, slab == slabs - 1)
    main_id = jnp.where(first, jnp.where(absent, -1, number), ids_ref[1]).astype(F32)
    extra_id = jnp.where(slab == 0, ids_ref[0], -1).astype(F32)
    line = lax.broadcasted_iota(jnp.int32, (8, CHANNELS), 0)
    message = jnp.where(line == 0, one, 0.0)
    message = jnp.where(line == 1, two, message)
    message = jnp.where(line == 2, sums_ref[0:1, :], message)
    message = jnp.where(line == 3, sums_ref[1:2, :], message)
    message = jnp.where(line == 4, main_id, message)
    message = jnp.where(line == 5, extra_id, message)
    message = jnp.where(line == 6, owner_ref[0:1, :], message)
    for p in range(message_ref.shape[0]):
        message_ref[p] = message


def norm_kernel(
    count, where_ref, message_ref, gathered_ref, affine_ref, out_weight_ref, conv_ref, extra_ref, latent_ref
):
    rows, _, columns = conv_ref.shape
    half = columns // 2
    main = gathered_ref[:, 4, :]
    extra = gathered_ref[:, 5, :]
    lines = []
    for number in (message_ref[0, 4:5, :], message_ref[0, 5:6, :]):
        on_main = main == number
        on_extra = extra == number
        for n in range(2):
            picked = jnp.where(on_main, gathered_ref[:, n, :], 0.0) + jnp.where(
                on_extra, gathered_ref[:, 2 + n, :], 0.0
            )
            lines.append(jnp.sum(picked, axis=0, keepdims=True))
        held = jnp.where(on_main, float(count), 0.0) + jnp.where(on_extra, float(count // 2), 0.0)
        lines.append(jnp.sum(held, axis=0, keepdims=True))
    lines += [jnp.zeros((1, CHANNELS), F32)] * 2
    size = CHANNELS // GROUPS
    group_row = lax.broadcasted_iota(jnp.int32, (CHANNELS, CHANNELS), 0) // size
    group_column = lax.broadcasted_iota(jnp.int32, (CHANNELS, CHANNELS), 1) // size
    member = jnp.where(group_row == group_column, 1.0, 0.0)
    totals = jnp.dot(
        jnp.concatenate(lines, axis=0), member, preferred_element_type=F32, precision=lax.Precision.HIGHEST
    )

    def factors(first):
        counts = totals[first + 2 : first + 3, :]
        mean = totals[first : first + 1, :] / counts
        var = totals[first + 1 : first + 2, :] / counts - mean * mean
        scale = lax.rsqrt(var + 1e-06) * affine_ref[0:1, :]
        offset = affine_ref[1:2, :] - mean * scale
        return [jnp.broadcast_to(value, (CHANNELS, CHANNELS)).T for value in (scale, offset)]

    def project(source_ref, scale, offset):
        images = []
        for r in range(source_ref.shape[0] // 2):
            pieces = []
            for i in range(2):
                for j in range(2):
                    value = source_ref[2 * r + i, :, j * half : (j + 1) * half].astype(F32)
                    value = value * scale + offset
                    pieces.append((value / (1.0 + jnp.exp(-value))).astype(BF16))
            images.append(jnp.concatenate(pieces, axis=0))
        image = jnp.concatenate(images, axis=1)
        return jnp.dot(out_weight_ref[...], image, preferred_element_type=F32).astype(BF16)

    places, chans = latent_ref.shape[0] // 2, 2
    part = MOMENTS // chans

    def store(latent, first):
        for r in range(latent.shape[1] // half):
            for c in range(chans):
                block = latent[c * part : (c + 1) * part, r * half : (r + 1) * half]
                for t in range(places):
                    latent_ref[t * chans + c, first + r] = block

    store(project(conv_ref, *factors(0)), 0)

    @pl.when(where_ref[0] == 0)
    def _():
        store(project(extra_ref, *factors(3)), rows // 2)

    @pl.when(where_ref[0] > 0)
    def _():
        for r in range(rows // 4):
            for p in range(latent_ref.shape[0]):
                latent_ref[p, rows // 2 + r] = jnp.zeros((part, half), BF16)


def shards(activations, frame_clip, conv_weight, norm_gain, norm_bias, out_weight, owner):
    half, frames, rows, columns = activations.shape
    sizes = tuple(lax.axis_size(name) for name in PART)
    slabs, spaces, chans = sizes
    assert (frames, chans, half * chans) == (2, 2, CHANNELS)
    parts = slabs * spaces * chans
    halos = 1 if spaces <= 2 else 2
    space = lax.axis_index("space")
    where = jnp.stack([lax.axis_index(name) for name in PART]).astype(jnp.int32)
    edge_low = activations[:, :, 0, :].transpose(1, 0, 2)
    edge_high = activations[:, :, rows - 1, :].transpose(1, 0, 2)
    odd = space % 2 == 1
    swapped = [space_swap(jnp.where(odd, edge_low, edge_high), sizes, 0)]
    if halos > 1:
        swapped.append(space_swap(jnp.where(odd, edge_high, edge_low), sizes, 1))
    planes = activations.transpose(1, 2, 0, 3)
    depth = (rows + halos) * half + ID_ROWS
    payload = jax.ShapeDtypeStruct((depth, columns), BF16)
    cross, same = whole_call(
        lambda *refs: pack_kernel(halos, *refs),
        (payload, payload),
        [SMEM, SMEM] + [VMEM] * (1 + halos),
        (where, frame_clip, planes, *swapped),
    )
    late_other = slab_swap(cross, sizes, True)
    late_own = slab_swap(same, sizes, False)
    turn = [(0, 1), (1, 0)]
    cross_other = lax.ppermute(cross, "chan", turn)
    same_other = lax.ppermute(same, "chan", turn)
    local_weight, late_weight, sum_weight = whole_call(
        weights_kernel,
        (
            jax.ShapeDtypeStruct((3 * CHANNELS, 6 * CHANNELS), BF16),
            jax.ShapeDtypeStruct((2, 3 * CHANNELS, 3 * CHANNELS), BF16),
            jax.ShapeDtypeStruct((3 * CHANNELS, 3 * CHANNELS), BF16),
        ),
        [SMEM, SMEM, VMEM],
        (where, frame_clip, conv_weight),
    )
    part, extra, extra_sums = whole_call(
        lambda *refs: local_kernel(rows, halos, *refs),
        (
            jax.ShapeDtypeStruct((rows, CHANNELS, columns), F32),
            jax.ShapeDtypeStruct((rows // 2, CHANNELS, columns), BF16),
            jax.ShapeDtypeStruct((8, CHANNELS), F32),
        ),
        [SMEM] + [VMEM] * 6,
        (where, local_weight, sum_weight, cross, same, cross_other, same_other),
    )
    send_rows = frames * (rows // 2)
    owner_line = jnp.pad(owner.reshape(1, send_rows).astype(F32), ((0, 0), (0, CHANNELS - send_rows)))
    conv, message = whole_call(
        lambda *refs: late_kernel(rows, halos, slabs, *refs),
        (
            jax.ShapeDtypeStruct((rows, CHANNELS, columns), BF16),
            jax.ShapeDtypeStruct((parts, 8, CHANNELS), F32),
        ),
        [SMEM, SMEM] + [VMEM] * 8,
        (where, frame_clip, owner_line, late_weight, part, cross, same_other, late_own, late_other, extra_sums),
    )
    gathered = lax.all_to_all(message, PART, split_axis=0, concat_axis=0, tiled=True)
    affine = jnp.stack([norm_gain, norm_bias])
    out_matrix = out_weight.reshape(4 * CHANNELS, MOMENTS).T
    kept = rows // 2 + rows // 4
    latent = whole_call(
        lambda *refs: norm_kernel(rows * columns, *refs),
        jax.ShapeDtypeStruct((slabs * chans, kept, MOMENTS // chans, columns // 2), BF16),
        [SMEM] + [VMEM] * 6,
        (where, message, gathered, affine, out_matrix, conv, extra),
    )
    arrived = lax.all_to_all(latent, ("tm", "chan"), split_axis=0, concat_axis=0, tiled=True)
    owners = gathered.reshape(slabs, spaces, chans, 8, CHANNELS)[:, :, 0, 6, :send_rows]
    owners = lax.dynamic_index_in_dim(owners, space, 1, keepdims=False).astype(jnp.int32)
    capacity = max(2, 2 * send_rows // slabs)
    earlier = jnp.arange(send_rows)[None, :] < jnp.arange(send_rows)[:, None]
    equal = owners[:, :, None] == owners[:, None, :]
    rank = jnp.sum((equal & earlier[None]).astype(jnp.int32), axis=2)
    slot = jnp.arange(slabs)[:, None] * capacity + rank
    slot = jnp.where(owners == lax.axis_index("tm"), slot, -1)
    by_frame = slot.reshape(slabs * frames, rows // 2)
    none = jnp.full((1, rows // 2), -1, jnp.int32)
    main_slot = jnp.stack([jnp.concatenate([by_frame[2::2], none]), by_frame[1::2]], axis=1)
    extra_slot = jnp.concatenate(
        [by_frame[0].reshape(1, chans, rows // 4), jnp.full((slabs - 1, chans, rows // 4), -1, jnp.int32)]
    )
    slots = jnp.concatenate([main_slot, extra_slot], axis=2).reshape(-1)
    selector = (slots[None, :] == jnp.arange(slabs * capacity)[:, None]).astype(BF16)
    block = arrived.reshape(slots.shape[0], -1)
    owned = jnp.dot(selector, block, preferred_element_type=F32).astype(BF16)
    return owned.reshape(1, slabs * capacity, MOMENTS // chans, columns // 2)


def solution(mesh):
    placed = (
        P(("groups", "chan"), "tm", "space", None),
        P(("groups", "tm")),
        P(),
        P(),
        P(),
        P(),
        P(("groups", "space"), "tm", None),
    )
    return jax.shard_map(
        shards,
        mesh=mesh,
        in_specs=placed,
        out_specs=P(("groups", "space"), "tm", "chan", None),
        check_vma=False,
    )
```

```python
import jax
import jax.numpy as jnp
import numpy as np
from jax import lax
from jax.experimental import pallas as pl
from jax.experimental.pallas import tpu as pltpu
from jax.sharding import PartitionSpec as P

CHANNELS = 128
GROUPS = 32
MOMENTS = 32
SEND_ROWS = 8
ID_ROWS = 16
BF16 = jnp.bfloat16
F32 = jnp.float32
VMEM = pl.BlockSpec(memory_space=pltpu.VMEM)
PARAMS = pltpu.CompilerParams(vmem_limit_bytes=40 * 1024 * 1024)
PART = ("tm", "space", "chan")


def flat_pairs(sizes, pairs):
    _, spaces, chans = sizes
    return [
        ((a[0] * spaces + a[1]) * chans + a[2], (b[0] * spaces + b[1]) * chans + b[2])
        for a, b in pairs
    ]


def space_swap(value, sizes, start):
    slabs, spaces, chans = sizes
    pairs = []
    for low in range(start, spaces - 1, 2):
        for t in range(slabs):
            for c in range(chans):
                pairs += [((t, low, c), (t, low + 1, c)), ((t, low + 1, c), (t, low, c))]
    return lax.ppermute(value, PART, flat_pairs(sizes, pairs))


def slab_swap(value, sizes, cross):
    slabs, spaces, _ = sizes
    last = slabs - 1
    pairs = []
    for s in range(spaces):
        for t in range(last):
            if cross:
                pairs += [((t, s, 0), (t + 1, s, 1)), ((t + 1, s, 1), (t, s, 0))]
            else:
                pairs += [((t, s, 1), (t + 1, s, 1)), ((t + 1, s, 0), (t, s, 0))]
        if spaces % 2 == 0 and cross:
            pairs += [((0, s, 1), (0, s ^ 1, 1)), ((last, s, 0), (last, s ^ 1, 0))]
        elif spaces % 2 == 0:
            pairs += [((last, s, 1), (last, s, 0)), ((0, s, 0), (0, s, 1))]
    return lax.ppermute(value, PART, flat_pairs(sizes, pairs))


def whole_call(kernel, out_shape, args, scratch=(), specs=None, flops=0):
    return pl.pallas_call(
        kernel,
        out_shape=out_shape,
        in_specs=specs or [VMEM] * len(args),
        out_specs=jax.tree.map(lambda _: VMEM, out_shape),
        scratch_shapes=scratch,
        compiler_params=PARAMS,
        cost_estimate=pl.CostEstimate(flops=flops, bytes_accessed=flops // 400, transcendentals=0),
    )(*args)


def number_at(small_ref, n):
    lane = lax.broadcasted_iota(jnp.int32, (1, CHANNELS), 1)
    return jnp.sum(jnp.where(lane == n, small_ref[2:3, :], 0.0))


def edge_kernel(frames_ref, split_ref, *edge_refs):
    chan = lax.axis_index("chan")
    odd = lax.axis_index("space") % 2 == 1
    _, rows, half, columns = frames_ref.shape
    source = lax.broadcasted_iota(jnp.int32, (columns, columns), 0)
    target = lax.broadcasted_iota(jnp.int32, (1, columns), 1)
    wanted = jnp.where(target < columns // 2, 2 * target, 2 * target - columns + 1)
    split_ref[...] = jnp.where(source == wanted, 1.0, 0.0).astype(BF16)
    for h, edge_ref in enumerate(edge_refs):
        to_low = odd if h == 0 else jnp.logical_not(odd)
        line = jnp.where(to_low, 0, rows - 1)
        image = jnp.concatenate([frames_ref[1 - chan, line], frames_ref[chan, line]], axis=0)
        edge_ref[...] = jnp.dot(image, split_ref[...], preferred_element_type=F32).astype(BF16)


def interior_kernel(frames_ref, split_ref, cross_ref, same_ref, both_ref):
    chan = lax.axis_index("chan")
    _, rows, half, columns = frames_ref.shape
    inside = rows * half
    for out_ref, frame, n in ((cross_ref, 1 - chan, 0), (same_ref, chan, 1)):
        image = frames_ref[frame].reshape(inside, columns)
        value = jnp.dot(image, split_ref[...], preferred_element_type=F32).astype(BF16)
        out_ref[...] = value
        both_ref[n * inside : (n + 1) * inside, :] = value


def halo_kernel(halos, capacity, small_ref, *refs):
    halo_refs, kept_refs, (cross_ref, same_ref) = refs[:halos], refs[halos : 2 * halos], refs[2 * halos :]
    for halo_ref, kept_ref in zip(halo_refs, kept_refs):
        kept_ref[...] = halo_ref[...]
    chan = lax.axis_index("chan")
    half, columns = CHANNELS // 2, cross_ref.shape[1]
    count = SEND_ROWS
    line = lax.broadcasted_iota(jnp.int32, (ID_ROWS, CHANNELS), 0)
    lane = lax.broadcasted_iota(jnp.int32, (ID_ROWS, CHANNELS), 1)
    owners = jnp.broadcast_to(small_ref[3:4, :], (ID_ROWS, CHANNELS))
    mine = jnp.sum(jnp.where(line == lane, owners, 0.0), axis=1, keepdims=True)
    rank = jnp.sum(jnp.where((owners == mine) & (lane < line), 1.0, 0.0), axis=1, keepdims=True)
    keys = mine * float(capacity) + rank + 1.0
    place = lax.broadcasted_iota(jnp.int32, (ID_ROWS, columns), 0)
    tail = jnp.where(place < count, keys, 0.0)
    ids = [number_at(small_ref, n) for n in range(2)]
    for n, (out_ref, frame) in enumerate(((cross_ref, 1 - chan), (same_ref, chan))):
        for h in range(halos):
            out_ref[h * half : (h + 1) * half, :] = halo_refs[h][n * half : (n + 1) * half, :]
        number = jnp.where(frame == 0, ids[0], ids[1])
        out_ref[halos * half :, :] = jnp.where(place == count, number + 1.0, tail).astype(BF16)


def weights_kernel(
    ids_any, owner_any, gain_any, bias_any, out_weight_any, weight_ref, _, local_ref, late_ref, sum_ref, small_ref,
    out_matrix_ref, ids_ref, owner_ref, gain_ref, bias_ref, out_weight_ref, taps_ref, copies
):
    chan = lax.axis_index("chan")
    fetched = [
        pltpu.make_async_copy(source, target, copies.at[n])
        for n, (source, target) in enumerate(
            (
                (ids_any, ids_ref),
                (owner_any, owner_ref),
                (gain_any, gain_ref),
                (bias_any, bias_ref),
                (out_weight_any, out_weight_ref),
            )
        )
    ]
    for copy in fetched:
        copy.start()
    half = CHANNELS // 2
    own = pl.multiple_of(chan * half, half)
    other = pl.multiple_of((1 - chan) * half, half)
    for j in range(3):
        for i in range(3):
            for k in range(3):
                block = jnp.concatenate(
                    [weight_ref[k, i, j, pl.ds(own, half), :], weight_ref[k, i, j, pl.ds(other, half), :]],
                    axis=0,
                )
                taps_ref[k, i, j] = block.T
    for copy in fetched:
        copy.wait()
    small_ref[...] = jnp.zeros_like(small_ref)
    small_ref[0:1, :] = gain_ref[...]
    small_ref[1:2, :] = bias_ref[...]
    small_ref[2:3, : ids_ref.shape[1]] = ids_ref[...].astype(F32)
    small_ref[3:4, :SEND_ROWS] = owner_ref[...].astype(F32)
    for i in range(2):
        for j in range(2):
            first = (2 * i + j) * CHANNELS
            out_matrix_ref[:, first : first + CHANNELS] = out_weight_ref[i, j]
    zero = jnp.float32(0.0)
    one = jnp.float32(1.0)
    first = chan == 0
    joined = number_at(small_ref, 0) == number_at(small_ref, 1)
    flag = jnp.where(joined, one, zero)
    on_first = jnp.where(first, one, zero)
    on_second = one - on_first
    near = (
        on_first * (one - flag),
        on_first + on_second * flag,
        zero,
    )
    far = (
        on_first * flag + on_second * (one - flag),
        on_second * (one - flag),
        on_second,
    )
    late_same = (on_second * flag, zero, on_first)
    late_apart = (on_first + on_second * flag, on_first, on_first)
    for j in range(3):
        for i in range(3):
            taps = [taps_ref[k, i, j].astype(F32) for k in range(3)]

            def mixed(scale):
                return (taps[0] * scale[0] + taps[1] * scale[1] + taps[2] * scale[2]).astype(BF16)

            rows = slice(j * CHANNELS, (j + 1) * CHANNELS)
            columns = slice(i * CHANNELS, (i + 1) * CHANNELS)
            shifted = slice((3 + i) * CHANNELS, (4 + i) * CHANNELS)
            local_ref[rows, columns] = mixed(near)
            local_ref[rows, shifted] = mixed(far)
            late_ref[0, rows, columns] = mixed(late_same)
            late_ref[1, rows, columns] = mixed(late_apart)
            sum_ref[rows, columns] = mixed((one, one, one))


def image_row(sources, rows, odd, r):
    half = CHANNELS // 2
    pieces = []
    for ref, start, halos in sources:
        if 0 <= r < rows:
            pieces.append(ref[start + r * half : start + (r + 1) * half, :])
            continue
        edges = [halo_ref[first : first + half, :] for halo_ref, first in halos]
        edges.append(jnp.zeros_like(edges[0]))
        on_first = odd if r < 0 else jnp.logical_not(odd)
        pieces.append(jnp.where(on_first, edges[0], edges[1]))
    return jnp.concatenate(pieces, axis=0)


def local_sources(rows, cross_ref, same_ref, other_ref, own_halos, other_halos):
    half = CHANNELS // 2
    inside = rows * half
    near = (
        (cross_ref, 0, [(ref, 0) for ref in own_halos]),
        (other_ref, inside, [(ref, half) for ref in other_halos]),
    )
    far = (
        (same_ref, 0, [(ref, half) for ref in own_halos]),
        (other_ref, 0, [(ref, 0) for ref in other_halos]),
    )
    return near, far


def joined_columns(product):
    half = product.shape[1] // 2
    left = product[:CHANNELS, :]
    middle = product[CHANNELS : 2 * CHANNELS, :]
    right = product[2 * CHANNELS :, :]
    lane = lax.broadcasted_iota(jnp.int32, (CHANNELS, half), 1)
    from_left = jnp.where(lane == 0, 0.0, pltpu.roll(left[:, half:], 1, 1))
    from_right = jnp.where(lane == half - 1, 0.0, pltpu.roll(right[:, :half], half - 1, 1))
    even = from_left + middle[:, :half] + right[:, half:]
    odd = left[:, :half] + middle[:, half:] + from_right
    return even, odd


def lane_totals(first, second):
    rows = [jnp.sum(value.T, axis=0, keepdims=True) for value in (first, second)]
    return rows


def local_kernel(rows, halos, weight_ref, sum_ref, *refs):
    conv_ref, extra_ref, sums_ref, images_ref = refs[3 + 2 * halos :]
    near, far = local_sources(rows, *refs[:3], refs[3 : 3 + halos], refs[3 + halos : 3 + 2 * halos])
    odd = lax.axis_index("space") % 2 == 1
    chan = lax.axis_index("chan")
    half = conv_ref.shape[2] // 2
    for r in range(rows):
        image = jnp.concatenate(
            [image_row(frame, rows, odd, r + i) for frame in (near, far) for i in (-1, 0, 1)], axis=0
        )
        product = jnp.dot(weight_ref[...], image, preferred_element_type=F32)
        for side, value in enumerate(joined_columns(product)):
            conv_ref[r, :, side * half : (side + 1) * half] = value
    sums_ref[...] = jnp.zeros_like(sums_ref)

    @pl.when(lax.axis_index("tm") == 0)
    def _():
        rows_here = rows // 2
        for n in range(rows_here + 2):
            upper = image_row(far, rows, odd, n - 1)
            lower = image_row(near, rows, odd, rows_here + n - 1)
            images_ref[n] = jnp.where(chan == 0, upper, lower)
        totals = [jnp.zeros((CHANNELS, half), F32)] * 2
        for r in range(rows_here):
            image = jnp.concatenate([images_ref[r + i] for i in range(3)], axis=0)
            product = jnp.dot(sum_ref[...], image, preferred_element_type=F32)
            for side, value in enumerate(joined_columns(product)):
                value = value.astype(BF16)
                extra_ref[r, :, side * half : (side + 1) * half] = value
                value = value.astype(F32)
                totals = [totals[0] + value, totals[1] + value * value]
        one, two = lane_totals(*totals)
        sums_ref[0:1, :] = one
        sums_ref[1:2, :] = two


def late_kernel(rows, halos, slabs, small_ref, weight_ref, part_ref, sums_ref, own_edge_ref, *refs):
    near, _ = local_sources(rows, *refs[:3], refs[3 : 3 + halos], refs[3 + halos : 3 + 2 * halos])
    refs = refs[3 + 2 * halos :]
    late_own_ref, late_other_ref, own_halo_ref, other_halo_ref = refs[:4]
    conv_ref, message_ref, keys_ref, images_ref = refs[4:]
    extent = CHANNELS // 2
    arrived = (
        (late_own_ref, 0, [(own_halo_ref, h * extent) for h in range(halos)]),
        (late_other_ref, 0, [(other_halo_ref, h * extent) for h in range(halos)]),
    )
    odd = lax.axis_index("space") % 2 == 1
    slab = lax.axis_index("tm")
    first = lax.axis_index("chan") == 0
    half = part_ref.shape[2] // 2
    kept = rows // 2
    tail = halos * extent
    absent = slab == jnp.where(first, slabs - 1, 0)
    late_tail = jnp.where(absent, 0.0, own_halo_ref[tail:, :CHANNELS].astype(F32))
    own_tail = own_edge_ref[tail:, :CHANNELS].astype(F32)
    number = jnp.max(late_tail[2 * kept : 2 * kept + 1, :]) - 1.0
    ids = [number_at(small_ref, n) for n in range(2)]
    same = number == jnp.where(first, ids[1], ids[0])
    keep = jnp.where(jnp.logical_or(same, jnp.logical_not(first)), 1.0, 0.0)
    use_late = jnp.logical_or(same, first)
    choice = jnp.where(same, 0, 1)
    for r in range(-1, rows + 1):
        late = image_row(arrived, rows, odd, r)
        here = image_row(near, rows, odd, r)
        images_ref[r + 1] = jnp.where(use_late, late, here)
    totals = [jnp.zeros((CHANNELS, half), F32)] * 2
    for r in range(rows):
        image = jnp.concatenate([images_ref[r + i] for i in range(3)], axis=0)
        product = jnp.dot(weight_ref[choice], image, preferred_element_type=F32)
        for side, value in enumerate(joined_columns(product)):
            lanes = slice(side * half, (side + 1) * half)
            value = (value + keep * part_ref[r, :, lanes]).astype(BF16)
            conv_ref[r, :, lanes] = value
            value = value.astype(F32)
            totals = [totals[0] + value, totals[1] + value * value]
    one, two = lane_totals(*totals)
    main_id = jnp.where(first, number, ids[1])
    extra_id = jnp.where(slab == 0, ids[0], -1.0)
    line = lax.broadcasted_iota(jnp.int32, (8, CHANNELS), 0)
    message = jnp.where(line == 0, one, 0.0)
    message = jnp.where(line == 1, two, message)
    message = jnp.where(line == 2, sums_ref[0:1, :], message)
    message = jnp.where(line == 3, sums_ref[1:2, :], message)
    message = jnp.where(line == 4, main_id, message)
    message = jnp.where(line == 5, extra_id, message)
    for p in range(message_ref.shape[0]):
        message_ref[p] = message
    keys = jnp.zeros((8, CHANNELS), F32)
    for n in range(kept):
        main_key = jnp.where(first, late_tail[n : n + 1, :], own_tail[kept + n : kept + n + 1, :])
        keys = jnp.where(line == n, main_key, keys)
    quarter = kept // 2
    for n in range(quarter):
        extra_key = jnp.where(first, own_tail[n : n + 1, :], own_tail[quarter + n : quarter + n + 1, :])
        keys = jnp.where(line == kept + n, jnp.where(slab == 0, extra_key, 0.0), keys)
    keys_ref[...] = keys


def norm_kernel(
    count, capacity, message_ref, keys_ref, gathered_ref, small_ref, out_matrix_ref, conv_ref, extra_ref, latent_ref
):
    rows, _, columns = conv_ref.shape
    half = columns // 2
    main = gathered_ref[:, 4, :]
    extra = gathered_ref[:, 5, :]
    lines = []
    for number in (message_ref[0, 4:5, :], message_ref[0, 5:6, :]):
        on_main = main == number
        on_extra = extra == number
        for n in range(2):
            picked = jnp.where(on_main, gathered_ref[:, n, :], 0.0) + jnp.where(
                on_extra, gathered_ref[:, 2 + n, :], 0.0
            )
            lines.append(jnp.sum(picked, axis=0, keepdims=True))
        held = jnp.where(on_main, float(count), 0.0) + jnp.where(on_extra, float(count // 2), 0.0)
        lines.append(jnp.sum(held, axis=0, keepdims=True))
    lines += [jnp.zeros((1, CHANNELS), F32)] * 2
    size = CHANNELS // GROUPS
    group_row = lax.broadcasted_iota(jnp.int32, (CHANNELS, CHANNELS), 0) // size
    group_column = lax.broadcasted_iota(jnp.int32, (CHANNELS, CHANNELS), 1) // size
    member = jnp.where(group_row == group_column, 1.0, 0.0)
    totals = jnp.dot(
        jnp.concatenate(lines, axis=0), member, preferred_element_type=F32, precision=lax.Precision.HIGHEST
    )

    def factors(first):
        counts = totals[first + 2 : first + 3, :]
        mean = totals[first : first + 1, :] / counts
        var = totals[first + 1 : first + 2, :] / counts - mean * mean
        scale = lax.rsqrt(var + 1e-06) * small_ref[0:1, :]
        offset = small_ref[1:2, :] - mean * scale
        return [jnp.broadcast_to(value, (CHANNELS, CHANNELS)).T for value in (scale, offset)]

    def project(source_ref, scale, offset):
        images = []
        for r in range(source_ref.shape[0] // 2):
            pieces = []
            for i in range(2):
                for j in range(2):
                    value = source_ref[2 * r + i, :, j * half : (j + 1) * half].astype(F32)
                    value = value * scale + offset
                    pieces.append((value / (1.0 + jnp.exp(-value))).astype(BF16))
            images.append(jnp.concatenate(pieces, axis=0))
        image = jnp.concatenate(images, axis=1)
        return jnp.dot(out_matrix_ref[...], image, preferred_element_type=F32)

    slots, places, chans = latent_ref.shape[1], latent_ref.shape[0] // 2, 2
    part = MOMENTS // chans

    def place(latent, first_key, wanted, slot):
        for c in range(chans):
            blocks = [
                latent[c * part : (c + 1) * part, r * half : (r + 1) * half] for r in range(latent.shape[1] // half)
            ]
            for t in range(places):
                for j in range(wanted):
                    value = jnp.zeros((part, half), F32)
                    for n, block in enumerate(blocks):
                        key = keys_ref[first_key + n : first_key + n + 1, :]
                        value = jnp.where(key == float(t * capacity + j + 1), block, value)
                    yield t * chans + c, slot + j, value

    kept = rows // 2
    for p, j, value in place(project(conv_ref, *factors(0)), 0, capacity, 0):
        latent_ref[p, j] = value.astype(BF16)
    for p in range(latent_ref.shape[0]):
        for j in range(capacity, slots):
            latent_ref[p, j] = jnp.zeros((part, half), BF16)

    @pl.when(lax.axis_index("tm") == 0)
    def _():
        latent = project(extra_ref, *factors(3))

        @pl.when(lax.axis_index("chan") == 0)
        def _():
            for p, j, value in place(latent, kept, slots - capacity, capacity):
                latent_ref[p, j] = value.astype(BF16)

        @pl.when(lax.axis_index("chan") == 1)
        def _():
            for p, j, value in place(latent, kept, capacity, 0):
                latent_ref[p, j] = (latent_ref[p, j].astype(F32) + value).astype(BF16)


def shards(activations, frame_clip, conv_weight, norm_gain, norm_bias, out_weight, owner):
    half, frames, rows, columns = activations.shape
    sizes = tuple(lax.axis_size(name) for name in PART)
    slabs, spaces, chans = sizes
    assert (frames, chans, half * chans) == (2, 2, CHANNELS)
    parts = slabs * spaces * chans
    halos = 1 if spaces <= 2 else 2
    send_rows = frames * (rows // 2)
    capacity = max(2, 2 * send_rows // slabs)
    kept = rows // 2
    assert send_rows == SEND_ROWS
    payload = jax.ShapeDtypeStruct((rows * half, columns), BF16)
    pair = jax.ShapeDtypeStruct((2 * half, columns), BF16)
    planes = activations.transpose(1, 2, 0, 3)
    split, *edges = whole_call(
        edge_kernel, (jax.ShapeDtypeStruct((columns, columns), BF16),) + (pair,) * halos, (planes,)
    )
    own_halos = [space_swap(edge, sizes, start) for start, edge in enumerate(edges)]
    cross, same, both = whole_call(
        interior_kernel,
        (payload, payload, jax.ShapeDtypeStruct((2 * rows * half, columns), BF16)),
        (planes, split),
        flops=300_000_000,
    )
    late_own = slab_swap(same, sizes, False)
    late_other = slab_swap(cross, sizes, True)
    turn = [(0, 1), (1, 0)]
    other = lax.ppermute(both, "chan", turn)
    local_weight, late_weight, sum_weight, small, out_matrix = whole_call(
        weights_kernel,
        (
            jax.ShapeDtypeStruct((3 * CHANNELS, 6 * CHANNELS), BF16),
            jax.ShapeDtypeStruct((2, 3 * CHANNELS, 3 * CHANNELS), BF16),
            jax.ShapeDtypeStruct((3 * CHANNELS, 3 * CHANNELS), BF16),
            jax.ShapeDtypeStruct((8, CHANNELS), F32),
            jax.ShapeDtypeStruct((MOMENTS, 4 * CHANNELS), BF16),
        ),
        (
            frame_clip.reshape(1, frames), owner.reshape(1, send_rows), norm_gain.reshape(1, CHANNELS),
            norm_bias.reshape(1, CHANNELS), out_weight.transpose(0, 1, 3, 2), conv_weight, both,
        ),
        [
            pltpu.VMEM((1, frames), jnp.int32),
            pltpu.VMEM((1, send_rows), jnp.int32),
            pltpu.VMEM((1, CHANNELS), F32),
            pltpu.VMEM((1, CHANNELS), F32),
            pltpu.VMEM((2, 2, MOMENTS, CHANNELS), BF16),
            pltpu.VMEM((3, 3, 3, CHANNELS, CHANNELS), BF16),
            pltpu.SemaphoreType.DMA((5,)),
        ],
        [pl.BlockSpec(memory_space=pl.ANY)] * 5 + [VMEM] * 2,
        1_200_000_000,
    )
    message_halo = jax.ShapeDtypeStruct((halos * half + ID_ROWS, columns), BF16)
    *own_halos, cross_halo, same_halo = whole_call(
        lambda *refs: halo_kernel(halos, capacity, *refs),
        (pair,) * halos + (message_halo, message_halo),
        (small, *own_halos),
    )
    other_halos = [lax.ppermute(halo, "chan", turn) for halo in own_halos]
    late_own_halo = slab_swap(same_halo, sizes, False)
    late_other_halo = slab_swap(cross_halo, sizes, True)
    here = (cross, same, other, *own_halos, *other_halos)
    part, extra, extra_sums = whole_call(
        lambda *refs: local_kernel(rows, halos, *refs),
        (
            jax.ShapeDtypeStruct((rows, CHANNELS, columns), F32),
            jax.ShapeDtypeStruct((rows // 2, CHANNELS, columns), BF16),
            jax.ShapeDtypeStruct((8, CHANNELS), F32),
        ),
        (local_weight, sum_weight, *here),
        [pltpu.VMEM((rows // 2 + 2, CHANNELS, columns), BF16)],
        flops=1_800_000_000,
    )
    conv, message, keys = whole_call(
        lambda *refs: late_kernel(rows, halos, slabs, *refs),
        (
            jax.ShapeDtypeStruct((rows, CHANNELS, columns), BF16),
            jax.ShapeDtypeStruct((parts, 8, CHANNELS), F32),
            jax.ShapeDtypeStruct((8, CHANNELS), F32),
        ),
        (
            small, late_weight, part, extra_sums, cross_halo, *here, late_own, late_other, late_own_halo, late_other_halo,
        ),
        [pltpu.VMEM((rows + 2, CHANNELS, columns), BF16)],
        flops=1_500_000_000,
    )
    gathered = lax.all_to_all(message, PART, split_axis=0, concat_axis=0, tiled=True)
    slots = capacity + kept // 2
    latent = whole_call(
        lambda *refs: norm_kernel(rows * columns, capacity, *refs),
        jax.ShapeDtypeStruct((slabs * chans, slots, MOMENTS // chans, columns // 2), BF16),
        (message, keys, gathered, small, out_matrix, conv, extra),
    )
    arrived = lax.all_to_all(latent, ("tm", "chan"), split_axis=0, concat_axis=0, tiled=True)
    arrived = arrived.reshape((slabs, chans) + arrived.shape[1:])
    later = arrived[:, 1, :capacity]
    begin = jnp.pad(arrived[:1, 0, capacity:], ((0, 0), (0, 2 * capacity - slots), (0, 0), (0, 0)))
    sooner = jnp.concatenate([begin, arrived[:-1, 0, :capacity]])
    return (later + sooner).reshape(1, slabs * capacity, MOMENTS // chans, columns // 2)


def solution(mesh):
    placed = (
        P(("groups", "chan"), "tm", "space", None),
        P(("groups", "tm")),
        P(),
        P(),
        P(),
        P(),
        P(("groups", "space"), "tm", None),
    )
    return jax.shard_map(
        shards,
        mesh=mesh,
        in_specs=placed,
        out_specs=P(("groups", "space"), "tm", "chan", None),
        check_vma=False,
    )
```

```python
import jax
import jax.numpy as jnp
import numpy as np
from jax import lax
from jax.experimental import pallas as pl
from jax.experimental.pallas import tpu as pltpu
from jax.sharding import PartitionSpec as P

CHANNELS = 128
GROUPS = 32
MOMENTS = 32
SEND_ROWS = 8
ID_ROWS = 16
BLOCK = 16
BF16 = jnp.bfloat16
F32 = jnp.float32
VMEM = pl.BlockSpec(memory_space=pltpu.VMEM)
PARAMS = pltpu.CompilerParams(vmem_limit_bytes=40 * 1024 * 1024)
PART = ("tm", "space", "chan")


def flat_pairs(sizes, pairs):
    _, spaces, chans = sizes
    return [
        ((a[0] * spaces + a[1]) * chans + a[2], (b[0] * spaces + b[1]) * chans + b[2])
        for a, b in pairs
    ]


def space_swap(value, sizes, start):
    slabs, spaces, chans = sizes
    pairs = []
    for low in range(start, spaces - 1, 2):
        for t in range(slabs):
            for c in range(chans):
                pairs += [((t, low, c), (t, low + 1, c)), ((t, low + 1, c), (t, low, c))]
    return lax.ppermute(value, PART, flat_pairs(sizes, pairs))


def slab_swap(value, sizes, cross):
    slabs, spaces, _ = sizes
    last = slabs - 1
    pairs = []
    for s in range(spaces):
        for t in range(last):
            if cross:
                pairs += [((t, s, 0), (t + 1, s, 1)), ((t + 1, s, 1), (t, s, 0))]
            else:
                pairs += [((t, s, 1), (t + 1, s, 1)), ((t + 1, s, 0), (t, s, 0))]
        if spaces % 2 == 0 and cross:
            pairs += [((0, s, 1), (0, s ^ 1, 1)), ((last, s, 0), (last, s ^ 1, 0))]
        elif spaces % 2 == 0:
            pairs += [((last, s, 1), (last, s, 0)), ((0, s, 0), (0, s, 1))]
    return lax.ppermute(value, PART, flat_pairs(sizes, pairs))


def whole_call(kernel, out_shape, args, scratch=(), specs=None, flops=0):
    return pl.pallas_call(
        kernel,
        out_shape=out_shape,
        in_specs=specs or [VMEM] * len(args),
        out_specs=jax.tree.map(lambda _: VMEM, out_shape),
        scratch_shapes=scratch,
        compiler_params=PARAMS,
        cost_estimate=None if flops is None else pl.CostEstimate(flops=flops, bytes_accessed=flops // 400, transcendentals=0),
    )(*args)


def number_at(small_ref, n):
    lane = lax.broadcasted_iota(jnp.int32, (1, CHANNELS), 1)
    return jnp.sum(jnp.where(lane == n, small_ref[2:3, :], 0.0))


def front_kernel(rows, pixels_ref, cross_ref, same_ref, both_ref, *edge_refs):
    chan = lax.axis_index("chan")
    odd = lax.axis_index("space") % 2 == 1
    half, columns = CHANNELS // 2, pixels_ref.shape[1]
    size = 2 * rows * BLOCK
    source = lax.broadcasted_iota(jnp.int32, (columns, columns), 0)
    target = lax.broadcasted_iota(jnp.int32, (1, columns), 1)
    wanted = jnp.where(target < columns // 2, 2 * target, 2 * target - columns + 1)
    split = jnp.where(source == wanted, 1.0, 0.0).astype(BF16)
    placed = lax.broadcasted_iota(jnp.int32, (size, size), 1)
    line = lax.broadcasted_iota(jnp.int32, (size, 1), 0)
    second = line // (rows * BLOCK)
    frame = jnp.where(second == 0, 1 - chan, chan)
    row = line // BLOCK % rows
    origin = line % BLOCK * (2 * rows) + frame * rows + row
    turn = jnp.where(placed == origin, 1.0, 0.0).astype(BF16)
    inside = rows * half
    for n in range(half // BLOCK):
        image = pixels_ref[n * size : (n + 1) * size, :]
        image = jnp.dot(turn, image, preferred_element_type=F32).astype(BF16)
        image = jnp.dot(image, split, preferred_element_type=F32).astype(BF16)
        for f, out_ref in enumerate((cross_ref, same_ref)):
            for r in range(rows):
                first = (f * rows + r) * BLOCK
                block = image[first : first + BLOCK, :]
                first = r * half + n * BLOCK
                out_ref[first : first + BLOCK, :] = block
                both_ref[f * inside + first : f * inside + first + BLOCK, :] = block
    for f, out_ref in enumerate((cross_ref, same_ref)):
        low, high = out_ref[:half, :], out_ref[(rows - 1) * half :, :]
        for h, edge_ref in enumerate(edge_refs):
            to_low = odd if h == 0 else jnp.logical_not(odd)
            edge_ref[f * half : (f + 1) * half, :] = jnp.where(to_low, low, high)


def halo_kernel(halos, capacity, small_ref, *refs):
    halo_refs, kept_refs, (cross_ref, same_ref) = refs[:halos], refs[halos : 2 * halos], refs[2 * halos :]
    for halo_ref, kept_ref in zip(halo_refs, kept_refs):
        kept_ref[...] = halo_ref[...]
    chan = lax.axis_index("chan")
    half, columns = CHANNELS // 2, cross_ref.shape[1]
    count = SEND_ROWS
    line = lax.broadcasted_iota(jnp.int32, (ID_ROWS, CHANNELS), 0)
    lane = lax.broadcasted_iota(jnp.int32, (ID_ROWS, CHANNELS), 1)
    owners = jnp.broadcast_to(small_ref[3:4, :], (ID_ROWS, CHANNELS))
    mine = jnp.sum(jnp.where(line == lane, owners, 0.0), axis=1, keepdims=True)
    rank = jnp.sum(jnp.where((owners == mine) & (lane < line), 1.0, 0.0), axis=1, keepdims=True)
    keys = mine * float(capacity) + rank + 1.0
    place = lax.broadcasted_iota(jnp.int32, (ID_ROWS, columns), 0)
    tail = jnp.where(place < count, keys, 0.0)
    ids = [number_at(small_ref, n) for n in range(2)]
    for n, (out_ref, frame) in enumerate(((cross_ref, 1 - chan), (same_ref, chan))):
        for h in range(halos):
            out_ref[h * half : (h + 1) * half, :] = halo_refs[h][n * half : (n + 1) * half, :]
        number = jnp.where(frame == 0, ids[0], ids[1])
        out_ref[halos * half :, :] = jnp.where(place == count, number + 1.0, tail).astype(BF16)


def weights_kernel(
    ids_any, owner_any, gain_any, bias_any, out_weight_any, weight_ref, _, local_ref, late_ref, sum_ref, small_ref,
    out_matrix_ref, ids_ref, owner_ref, gain_ref, bias_ref, out_weight_ref, taps_ref, copies
):
    chan = lax.axis_index("chan")
    fetched = [
        pltpu.make_async_copy(source, target, copies.at[n])
        for n, (source, target) in enumerate(
            (
                (ids_any, ids_ref),
                (owner_any, owner_ref),
                (gain_any, gain_ref),
                (bias_any, bias_ref),
                (out_weight_any, out_weight_ref),
            )
        )
    ]
    for copy in fetched:
        copy.start()
    half = CHANNELS // 2
    own = pl.multiple_of(chan * half, half)
    other = pl.multiple_of((1 - chan) * half, half)
    for j in range(3):
        for i in range(3):
            for k in range(3):
                block = jnp.concatenate(
                    [weight_ref[k, i, j, pl.ds(own, half), :], weight_ref[k, i, j, pl.ds(other, half), :]],
                    axis=0,
                )
                taps_ref[k, i, j] = block.T
    for copy in fetched:
        copy.wait()
    small_ref[...] = jnp.zeros_like(small_ref)
    small_ref[0:1, :] = gain_ref[...]
    small_ref[1:2, :] = bias_ref[...]
    small_ref[2:3, : ids_ref.shape[1]] = ids_ref[...].astype(F32)
    small_ref[3:4, :SEND_ROWS] = owner_ref[...].astype(F32)
    for i in range(2):
        for j in range(2):
            first = (2 * i + j) * CHANNELS
            out_matrix_ref[:, first : first + CHANNELS] = out_weight_ref[i, j]
    zero = jnp.float32(0.0)
    one = jnp.float32(1.0)
    first = chan == 0
    joined = number_at(small_ref, 0) == number_at(small_ref, 1)
    flag = jnp.where(joined, one, zero)
    on_first = jnp.where(first, one, zero)
    on_second = one - on_first
    near = (
        on_first * (one - flag),
        on_first + on_second * flag,
        zero,
    )
    far = (
        on_first * flag + on_second * (one - flag),
        on_second * (one - flag),
        on_second,
    )
    late_same = (on_second * flag, zero, on_first)
    late_apart = (on_first + on_second * flag, on_first, on_first)
    for j in range(3):
        for i in range(3):
            taps = [taps_ref[k, i, j].astype(F32) for k in range(3)]

            def mixed(scale):
                return (taps[0] * scale[0] + taps[1] * scale[1] + taps[2] * scale[2]).astype(BF16)

            rows = slice(j * CHANNELS, (j + 1) * CHANNELS)
            columns = slice(i * CHANNELS, (i + 1) * CHANNELS)
            shifted = slice((3 + i) * CHANNELS, (4 + i) * CHANNELS)
            local_ref[rows, columns] = mixed(near)
            local_ref[rows, shifted] = mixed(far)
            late_ref[0, rows, columns] = mixed(late_same)
            late_ref[1, rows, columns] = mixed(late_apart)
            sum_ref[rows, columns] = mixed((one, one, one))


def image_row(sources, rows, odd, r):
    half = CHANNELS // 2
    pieces = []
    for ref, start, halos in sources:
        if 0 <= r < rows:
            pieces.append(ref[start + r * half : start + (r + 1) * half, :])
            continue
        edges = [halo_ref[first : first + half, :] for halo_ref, first in halos]
        edges.append(jnp.zeros_like(edges[0]))
        on_first = odd if r < 0 else jnp.logical_not(odd)
        pieces.append(jnp.where(on_first, edges[0], edges[1]))
    return jnp.concatenate(pieces, axis=0)


def local_sources(rows, cross_ref, same_ref, other_ref, own_halos, other_halos):
    half = CHANNELS // 2
    inside = rows * half
    near = (
        (cross_ref, 0, [(ref, 0) for ref in own_halos]),
        (other_ref, inside, [(ref, half) for ref in other_halos]),
    )
    far = (
        (same_ref, 0, [(ref, half) for ref in own_halos]),
        (other_ref, 0, [(ref, 0) for ref in other_halos]),
    )
    return near, far


def joined_columns(product):
    half = product.shape[1] // 2
    left = product[:CHANNELS, :]
    middle = product[CHANNELS : 2 * CHANNELS, :]
    right = product[2 * CHANNELS :, :]
    lane = lax.broadcasted_iota(jnp.int32, (CHANNELS, half), 1)
    from_left = jnp.where(lane == 0, 0.0, pltpu.roll(left[:, half:], 1, 1))
    from_right = jnp.where(lane == half - 1, 0.0, pltpu.roll(right[:, :half], half - 1, 1))
    even = from_left + middle[:, :half] + right[:, half:]
    odd = left[:, :half] + middle[:, half:] + from_right
    return even, odd


def lane_totals(first, second):
    rows = [jnp.sum(value.T, axis=0, keepdims=True) for value in (first, second)]
    return rows


def local_kernel(rows, halos, weight_ref, sum_ref, *refs):
    conv_ref, extra_ref, sums_ref, images_ref = refs[3 + 2 * halos :]
    near, far = local_sources(rows, *refs[:3], refs[3 : 3 + halos], refs[3 + halos : 3 + 2 * halos])
    odd = lax.axis_index("space") % 2 == 1
    chan = lax.axis_index("chan")
    half = conv_ref.shape[2] // 2
    for r in range(rows):
        image = jnp.concatenate(
            [image_row(frame, rows, odd, r + i) for frame in (near, far) for i in (-1, 0, 1)], axis=0
        )
        product = jnp.dot(weight_ref[...], image, preferred_element_type=F32)
        for side, value in enumerate(joined_columns(product)):
            conv_ref[r, :, side * half : (side + 1) * half] = value
    sums_ref[...] = jnp.zeros_like(sums_ref)

    @pl.when(lax.axis_index("tm") == 0)
    def _():
        rows_here = rows // 2
        for n in range(rows_here + 2):
            upper = image_row(far, rows, odd, n - 1)
            lower = image_row(near, rows, odd, rows_here + n - 1)
            images_ref[n] = jnp.where(chan == 0, upper, lower)
        totals = [jnp.zeros((CHANNELS, half), F32)] * 2
        for r in range(rows_here):
            image = jnp.concatenate([images_ref[r + i] for i in range(3)], axis=0)
            product = jnp.dot(sum_ref[...], image, preferred_element_type=F32)
            for side, value in enumerate(joined_columns(product)):
                value = value.astype(BF16)
                extra_ref[r, :, side * half : (side + 1) * half] = value
                value = value.astype(F32)
                totals = [totals[0] + value, totals[1] + value * value]
        one, two = lane_totals(*totals)
        sums_ref[0:1, :] = one
        sums_ref[1:2, :] = two


def late_kernel(rows, halos, slabs, small_ref, weight_ref, part_ref, sums_ref, own_edge_ref, *refs):
    near, _ = local_sources(rows, *refs[:3], refs[3 : 3 + halos], refs[3 + halos : 3 + 2 * halos])
    refs = refs[3 + 2 * halos :]
    late_own_ref, late_other_ref, own_halo_ref, other_halo_ref = refs[:4]
    conv_ref, message_ref, keys_ref, images_ref = refs[4:]
    extent = CHANNELS // 2
    arrived = (
        (late_own_ref, 0, [(own_halo_ref, h * extent) for h in range(halos)]),
        (late_other_ref, 0, [(other_halo_ref, h * extent) for h in range(halos)]),
    )
    odd = lax.axis_index("space") % 2 == 1
    slab = lax.axis_index("tm")
    first = lax.axis_index("chan") == 0
    half = part_ref.shape[2] // 2
    kept = rows // 2
    tail = halos * extent
    absent = slab == jnp.where(first, slabs - 1, 0)
    late_tail = jnp.where(absent, 0.0, own_halo_ref[tail:, :CHANNELS].astype(F32))
    own_tail = own_edge_ref[tail:, :CHANNELS].astype(F32)
    number = jnp.max(late_tail[2 * kept : 2 * kept + 1, :]) - 1.0
    ids = [number_at(small_ref, n) for n in range(2)]
    same = number == jnp.where(first, ids[1], ids[0])
    keep = jnp.where(jnp.logical_or(same, jnp.logical_not(first)), 1.0, 0.0)
    use_late = jnp.logical_or(same, first)
    choice = jnp.where(same, 0, 1)
    for r in range(-1, rows + 1):
        late = image_row(arrived, rows, odd, r)
        here = image_row(near, rows, odd, r)
        images_ref[r + 1] = jnp.where(use_late, late, here)
    totals = [jnp.zeros((CHANNELS, half), F32)] * 2
    for r in range(rows):
        image = jnp.concatenate([images_ref[r + i] for i in range(3)], axis=0)
        product = jnp.dot(weight_ref[choice], image, preferred_element_type=F32)
        for side, value in enumerate(joined_columns(product)):
            lanes = slice(side * half, (side + 1) * half)
            value = (value + keep * part_ref[r, :, lanes]).astype(BF16)
            conv_ref[r, :, lanes] = value
            value = value.astype(F32)
            totals = [totals[0] + value, totals[1] + value * value]
    one, two = lane_totals(*totals)
    main_id = jnp.where(first, number, ids[1])
    extra_id = jnp.where(slab == 0, ids[0], -1.0)
    line = lax.broadcasted_iota(jnp.int32, (8, CHANNELS), 0)
    message = jnp.where(line == 0, one, 0.0)
    message = jnp.where(line == 1, two, message)
    message = jnp.where(line == 2, sums_ref[0:1, :], message)
    message = jnp.where(line == 3, sums_ref[1:2, :], message)
    message = jnp.where(line == 4, main_id, message)
    message = jnp.where(line == 5, extra_id, message)
    for p in range(message_ref.shape[0]):
        message_ref[p] = message
    keys = jnp.zeros((8, CHANNELS), F32)
    for n in range(kept):
        main_key = jnp.where(first, late_tail[n : n + 1, :], own_tail[kept + n : kept + n + 1, :])
        keys = jnp.where(line == n, main_key, keys)
    quarter = kept // 2
    for n in range(quarter):
        extra_key = jnp.where(first, own_tail[n : n + 1, :], own_tail[quarter + n : quarter + n + 1, :])
        keys = jnp.where(line == kept + n, jnp.where(slab == 0, extra_key, 0.0), keys)
    keys_ref[...] = keys


def norm_kernel(
    count, message_ref, keys_ref, gathered_ref, small_ref, out_matrix_ref, conv_ref, extra_ref, mine_ref, theirs_ref
):
    rows, _, columns = conv_ref.shape
    half = columns // 2
    main = gathered_ref[:, 4, :]
    extra = gathered_ref[:, 5, :]
    lines = []
    for number in (message_ref[0, 4:5, :], message_ref[0, 5:6, :]):
        on_main = main == number
        on_extra = extra == number
        for n in range(2):
            picked = jnp.where(on_main, gathered_ref[:, n, :], 0.0) + jnp.where(
                on_extra, gathered_ref[:, 2 + n, :], 0.0
            )
            lines.append(jnp.sum(picked, axis=0, keepdims=True))
        held = jnp.where(on_main, float(count), 0.0) + jnp.where(on_extra, float(count // 2), 0.0)
        lines.append(jnp.sum(held, axis=0, keepdims=True))
    lines += [jnp.zeros((1, CHANNELS), F32)] * 2
    size = CHANNELS // GROUPS
    group_row = lax.broadcasted_iota(jnp.int32, (CHANNELS, CHANNELS), 0) // size
    group_column = lax.broadcasted_iota(jnp.int32, (CHANNELS, CHANNELS), 1) // size
    member = jnp.where(group_row == group_column, 1.0, 0.0)
    totals = jnp.dot(
        jnp.concatenate(lines, axis=0), member, preferred_element_type=F32, precision=lax.Precision.HIGHEST
    )

    def factors(first):
        counts = totals[first + 2 : first + 3, :]
        mean = totals[first : first + 1, :] / counts
        var = totals[first + 1 : first + 2, :] / counts - mean * mean
        scale = lax.rsqrt(var + 1e-06) * small_ref[0:1, :]
        offset = small_ref[1:2, :] - mean * scale
        return [jnp.broadcast_to(0.5 * value, (CHANNELS, CHANNELS)).T for value in (scale, offset)]

    def project(source_ref, scale, offset):
        images = []
        for r in range(source_ref.shape[0] // 2):
            pieces = []
            for i in range(2):
                for j in range(2):
                    value = source_ref[2 * r + i, :, j * half : (j + 1) * half].astype(F32)
                    value = value * scale + offset
                    pieces.append((value + value * jnp.tanh(value)).astype(BF16))
            images.append(jnp.concatenate(pieces, axis=0))
        image = jnp.concatenate(images, axis=1)
        return jnp.dot(out_matrix_ref[...], image, preferred_element_type=F32)

    chan = lax.axis_index("chan")
    kept = rows // 2
    part = MOMENTS // 2

    def store(latent, first):
        for n in range(latent.shape[1] // half):
            blocks = [latent[c * part : (c + 1) * part, n * half : (n + 1) * half].astype(BF16) for c in range(2)]
            mine_ref[first + n] = jnp.where(chan == 0, blocks[0], blocks[1])
            theirs_ref[first + n] = jnp.where(chan == 0, blocks[1], blocks[0])

    store(project(conv_ref, *factors(0)), 0)
    theirs_ref[kept + kept // 2] = jnp.concatenate([keys_ref[...]] * 2, axis=0).astype(BF16)

    @pl.when(lax.axis_index("tm") == 0)
    def _():
        store(project(extra_ref, *factors(3)), kept)

    @pl.when(lax.axis_index("tm") > 0)
    def _():
        for n in range(kept // 2):
            mine_ref[kept + n] = jnp.zeros((part, half), BF16)
            theirs_ref[kept + n] = jnp.zeros((part, half), BF16)


def crossed(slabs):
    return slabs in (2, 4)


def place_kernel(slabs, capacity, kept, keys_ref, mine_ref, other_ref, *send_refs):
    slab = lax.axis_index("tm")
    second = lax.axis_index("chan") == 1
    count = kept + kept // 2
    other_keys = other_ref[count].astype(F32)
    rows = []
    for n in range(count):
        mine = (keys_ref[n : n + 1, :], mine_ref[n].astype(F32))
        other = (other_keys[n : n + 1, :], other_ref[n].astype(F32))
        if n < kept:
            picked = [[jnp.where(second, x, y) for x, y in pair] for pair in (zip(mine, other), zip(other, mine))]
            rows.append(((picked[0],), picked[1]))
        else:
            rows.append(((mine, other), None))
    now = [row for group, _ in rows for row in group]
    following = [row for _, row in rows if row is not None]
    for d in range(slabs):
        owner = (slab ^ d if crossed(slabs) else jnp.int32(d)).astype(F32)
        for j in range(capacity):
            wanted = owner * float(capacity) + float(j + 1)
            for first, group in ((0, now), (capacity, following)):
                value = jnp.zeros(mine_ref.shape[1:], F32)
                for key, block in group:
                    value = jnp.where(key == wanted, block, value)
                if crossed(slabs):
                    send_refs[d][first + j] = value.astype(BF16)
                else:
                    send_refs[0][d, first + j] = value.astype(BF16)


def merge_kernel(slabs, capacity, *refs):
    sources, owned_ref = refs[:-1], refs[-1]
    slab = lax.axis_index("tm")

    def source(d):
        if crossed(slabs):
            return slab ^ d, sources[d]
        return d, sources[0].at[d]

    for d in range(slabs):
        block, ref = source(d)
        for j in range(capacity):
            owned_ref[block * capacity + j] = ref[j]
    for d in range(slabs):
        block, ref = source(d)

        @pl.when(block + 1 < slabs)
        def _():
            for j in range(capacity):
                n = (block + 1) * capacity + j
                owned_ref[n] = (owned_ref[n].astype(F32) + ref[capacity + j].astype(F32)).astype(BF16)


def shards(activations, frame_clip, conv_weight, norm_gain, norm_bias, out_weight, owner):
    half, frames, rows, columns = activations.shape
    sizes = tuple(lax.axis_size(name) for name in PART)
    slabs, spaces, chans = sizes
    assert (frames, chans, half * chans) == (2, 2, CHANNELS)
    parts = slabs * spaces * chans
    halos = 1 if spaces <= 2 else 2
    send_rows = frames * (rows // 2)
    capacity = max(2, 2 * send_rows // slabs)
    kept = rows // 2
    assert send_rows == SEND_ROWS
    payload = jax.ShapeDtypeStruct((rows * half, columns), BF16)
    pair = jax.ShapeDtypeStruct((2 * half, columns), BF16)
    cross, same, both, *edges = whole_call(
        lambda *refs: front_kernel(rows, *refs),
        (payload, payload, jax.ShapeDtypeStruct((2 * rows * half, columns), BF16)) + (pair,) * halos,
        (activations.reshape(half * frames * rows, columns),),
        flops=300000000,
    )
    own_halos = [space_swap(edge, sizes, start) for start, edge in enumerate(edges)]
    late_own = slab_swap(same, sizes, False)
    late_other = slab_swap(cross, sizes, True)
    turn = [(0, 1), (1, 0)]
    local_weight, late_weight, sum_weight, small, out_matrix = whole_call(
        weights_kernel,
        (
            jax.ShapeDtypeStruct((3 * CHANNELS, 6 * CHANNELS), BF16),
            jax.ShapeDtypeStruct((2, 3 * CHANNELS, 3 * CHANNELS), BF16),
            jax.ShapeDtypeStruct((3 * CHANNELS, 3 * CHANNELS), BF16),
            jax.ShapeDtypeStruct((8, CHANNELS), F32),
            jax.ShapeDtypeStruct((MOMENTS, 4 * CHANNELS), BF16),
        ),
        (
            frame_clip.reshape(1, frames), owner.reshape(1, send_rows), norm_gain.reshape(1, CHANNELS),
            norm_bias.reshape(1, CHANNELS), out_weight.transpose(0, 1, 3, 2), conv_weight, both,
        ),
        [
            pltpu.VMEM((1, frames), jnp.int32),
            pltpu.VMEM((1, send_rows), jnp.int32),
            pltpu.VMEM((1, CHANNELS), F32),
            pltpu.VMEM((1, CHANNELS), F32),
            pltpu.VMEM((2, 2, MOMENTS, CHANNELS), BF16),
            pltpu.VMEM((3, 3, 3, CHANNELS, CHANNELS), BF16),
            pltpu.SemaphoreType.DMA((5,)),
        ],
        [pl.BlockSpec(memory_space=pl.ANY)] * 5 + [VMEM] * 2,
        1200000000,
    )
    other = lax.ppermute(both, "chan", turn)
    message_halo = jax.ShapeDtypeStruct((halos * half + ID_ROWS, columns), BF16)
    *own_halos, cross_halo, same_halo = whole_call(
        lambda *refs: halo_kernel(halos, capacity, *refs),
        (pair,) * halos + (message_halo, message_halo),
        (small, *own_halos),
    )
    other_halos = [lax.ppermute(halo, "chan", turn) for halo in own_halos]
    late_own_halo = slab_swap(same_halo, sizes, False)
    late_other_halo = slab_swap(cross_halo, sizes, True)
    here = (cross, same, other, *own_halos, *other_halos)
    part, extra, extra_sums = whole_call(
        lambda *refs: local_kernel(rows, halos, *refs),
        (
            jax.ShapeDtypeStruct((rows, CHANNELS, columns), F32),
            jax.ShapeDtypeStruct((rows // 2, CHANNELS, columns), BF16),
            jax.ShapeDtypeStruct((8, CHANNELS), F32),
        ),
        (local_weight, sum_weight, *here),
        [pltpu.VMEM((rows // 2 + 2, CHANNELS, columns), BF16)],
        flops=1800000000,
    )
    conv, message, keys = whole_call(
        lambda *refs: late_kernel(rows, halos, slabs, *refs),
        (
            jax.ShapeDtypeStruct((rows, CHANNELS, columns), BF16),
            jax.ShapeDtypeStruct((parts, 8, CHANNELS), F32),
            jax.ShapeDtypeStruct((8, CHANNELS), F32),
        ),
        (
            small, late_weight, part, extra_sums, cross_halo, *here, late_own, late_other, late_own_halo, late_other_halo,
        ),
        [pltpu.VMEM((rows + 2, CHANNELS, columns), BF16)],
        flops=1500000000,
    )
    gathered = lax.all_to_all(message, PART, split_axis=0, concat_axis=0, tiled=True)
    part = MOMENTS // chans
    width = columns // 2
    count = kept + kept // 2
    mine, theirs = whole_call(
        lambda *refs: norm_kernel(rows * columns, *refs),
        (
            jax.ShapeDtypeStruct((count, part, width), BF16),
            jax.ShapeDtypeStruct((count + 1, part, width), BF16),
        ),
        (message, keys, gathered, small, out_matrix, conv, extra),
    )
    from_other = lax.ppermute(theirs, "chan", turn)
    blocks = (2 * capacity, part, width)
    if crossed(slabs):
        shapes = (jax.ShapeDtypeStruct(blocks, BF16),) * slabs
    else:
        shapes = (jax.ShapeDtypeStruct((slabs,) + blocks, BF16),)
    sends = whole_call(
        lambda *refs: place_kernel(slabs, capacity, kept, *refs), shapes, (keys, mine, from_other)
    )
    if crossed(slabs):
        received = [sends[0]]
        for d in range(1, slabs):
            received.append(lax.ppermute(sends[d], "tm", [(t, t ^ d) for t in range(slabs)]))
    else:
        received = [lax.all_to_all(sends[0], "tm", split_axis=0, concat_axis=0, tiled=True)]
    turns = list((0, 3, 1, 2)) if crossed(slabs) else [0]
    owned = pl.pallas_call(
        lambda *refs: merge_kernel(slabs, capacity, *[refs[turns.index(d)] for d in range(len(turns))], refs[-1]),
        out_shape=jax.ShapeDtypeStruct((slabs * capacity, part, width), BF16),
        in_specs=[VMEM] * len(received),
        out_specs=pl.BlockSpec((slabs * capacity, part, width), lambda: (0, 0, 0)),
        compiler_params=PARAMS,
    )(*[received[d] for d in turns])
    return owned[None]


def solution(mesh):
    placed = (
        P(("groups", "chan"), "tm", "space", None),
        P(("groups", "tm")),
        P(),
        P(),
        P(),
        P(),
        P(("groups", "space"), "tm", None),
    )
    return jax.shard_map(
        shards,
        mesh=mesh,
        in_specs=placed,
        out_specs=P(("groups", "space"), "tm", "chan", None),
        check_vma=False,
    )
```

```python
import jax
import jax.numpy as jnp
import numpy as np
from jax import lax
from jax.experimental import pallas as pl
from jax.experimental.pallas import tpu as pltpu
from jax.sharding import PartitionSpec as P

CHANNELS = 128
GROUPS = 32
MOMENTS = 32
SEND_ROWS = 8
ID_ROWS = 16
BLOCK = 16
BF16 = jnp.bfloat16
F32 = jnp.float32
VMEM = pl.BlockSpec(memory_space=pltpu.VMEM)
PARAMS = pltpu.CompilerParams(vmem_limit_bytes=40 * 1024 * 1024)
PART = ("tm", "space", "chan")


def flat_pairs(sizes, pairs):
    _, spaces, chans = sizes
    return [
        ((a[0] * spaces + a[1]) * chans + a[2], (b[0] * spaces + b[1]) * chans + b[2])
        for a, b in pairs
    ]


def space_swap(value, sizes, start):
    slabs, spaces, chans = sizes
    pairs = []
    for low in range(start, spaces - 1, 2):
        for t in range(slabs):
            for c in range(chans):
                pairs += [((t, low, c), (t, low + 1, c)), ((t, low + 1, c), (t, low, c))]
    return lax.ppermute(value, PART, flat_pairs(sizes, pairs))


def slab_swap(value, sizes, cross):
    slabs, spaces, _ = sizes
    last = slabs - 1
    pairs = []
    for s in range(spaces):
        for t in range(last):
            if cross:
                pairs += [((t, s, 0), (t + 1, s, 1)), ((t + 1, s, 1), (t, s, 0))]
            else:
                pairs += [((t, s, 1), (t + 1, s, 1)), ((t + 1, s, 0), (t, s, 0))]
        if spaces % 2 == 0 and cross:
            pairs += [((0, s, 1), (0, s ^ 1, 1)), ((last, s, 0), (last, s ^ 1, 0))]
        elif spaces % 2 == 0:
            pairs += [((last, s, 1), (last, s, 0)), ((0, s, 0), (0, s, 1))]
    return lax.ppermute(value, PART, flat_pairs(sizes, pairs))


def whole_call(kernel, out_shape, args, scratch=(), specs=None, flops=0):
    return pl.pallas_call(
        kernel,
        out_shape=out_shape,
        in_specs=specs or [VMEM] * len(args),
        out_specs=jax.tree.map(lambda _: VMEM, out_shape),
        scratch_shapes=scratch,
        compiler_params=PARAMS,
        cost_estimate=None if flops is None else pl.CostEstimate(flops=flops, bytes_accessed=flops // 400, transcendentals=0),
    )(*args)


def number_at(small_ref, n):
    lane = lax.broadcasted_iota(jnp.int32, (1, CHANNELS), 1)
    return jnp.sum(jnp.where(lane == n, small_ref[2:3, :], 0.0))


def front_kernel(rows, pixels_ref, cross_ref, same_ref, both_ref, *edge_refs):
    chan = lax.axis_index("chan")
    odd = lax.axis_index("space") % 2 == 1
    half, columns = CHANNELS // 2, pixels_ref.shape[1]
    size = 2 * rows * BLOCK
    source = lax.broadcasted_iota(jnp.int32, (columns, columns), 0)
    target = lax.broadcasted_iota(jnp.int32, (1, columns), 1)
    wanted = jnp.where(target < columns // 2, 2 * target, 2 * target - columns + 1)
    split = jnp.where(source == wanted, 1.0, 0.0).astype(BF16)
    placed = lax.broadcasted_iota(jnp.int32, (size, size), 1)
    line = lax.broadcasted_iota(jnp.int32, (size, 1), 0)
    second = line // (rows * BLOCK)
    frame = jnp.where(second == 0, 1 - chan, chan)
    row = line // BLOCK % rows
    origin = line % BLOCK * (2 * rows) + frame * rows + row
    turn = jnp.where(placed == origin, 1.0, 0.0).astype(BF16)
    inside = rows * half
    for n in range(half // BLOCK):
        image = pixels_ref[n * size : (n + 1) * size, :]
        image = jnp.dot(turn, image, preferred_element_type=F32).astype(BF16)
        image = jnp.dot(image, split, preferred_element_type=F32).astype(BF16)
        for f, out_ref in enumerate((cross_ref, same_ref)):
            for r in range(rows):
                first = (f * rows + r) * BLOCK
                block = image[first : first + BLOCK, :]
                first = r * half + n * BLOCK
                out_ref[first : first + BLOCK, :] = block
                both_ref[f * inside + first : f * inside + first + BLOCK, :] = block
    for f, out_ref in enumerate((cross_ref, same_ref)):
        low, high = out_ref[:half, :], out_ref[(rows - 1) * half :, :]
        for h, edge_ref in enumerate(edge_refs):
            to_low = odd if h == 0 else jnp.logical_not(odd)
            edge_ref[f * half : (f + 1) * half, :] = jnp.where(to_low, low, high)


def halo_kernel(halos, capacity, small_ref, *refs):
    halo_refs, kept_refs, (cross_ref, same_ref) = refs[:halos], refs[halos : 2 * halos], refs[2 * halos :]
    for halo_ref, kept_ref in zip(halo_refs, kept_refs):
        kept_ref[...] = halo_ref[...]
    chan = lax.axis_index("chan")
    half, columns = CHANNELS // 2, cross_ref.shape[1]
    count = SEND_ROWS
    line = lax.broadcasted_iota(jnp.int32, (ID_ROWS, CHANNELS), 0)
    lane = lax.broadcasted_iota(jnp.int32, (ID_ROWS, CHANNELS), 1)
    owners = jnp.broadcast_to(small_ref[3:4, :], (ID_ROWS, CHANNELS))
    mine = jnp.sum(jnp.where(line == lane, owners, 0.0), axis=1, keepdims=True)
    rank = jnp.sum(jnp.where((owners == mine) & (lane < line), 1.0, 0.0), axis=1, keepdims=True)
    keys = mine * float(capacity) + rank + 1.0
    place = lax.broadcasted_iota(jnp.int32, (ID_ROWS, columns), 0)
    tail = jnp.where(place < count, keys, 0.0)
    ids = [number_at(small_ref, n) for n in range(2)]
    for n, (out_ref, frame) in enumerate(((cross_ref, 1 - chan), (same_ref, chan))):
        for h in range(halos):
            out_ref[h * half : (h + 1) * half, :] = halo_refs[h][n * half : (n + 1) * half, :]
        number = jnp.where(frame == 0, ids[0], ids[1])
        out_ref[halos * half :, :] = jnp.where(place == count, number + 1.0, tail).astype(BF16)


def weights_kernel(
    ids_any, owner_any, gain_any, bias_any, out_weight_any, weight_ref, _, local_ref, late_ref, sum_ref, small_ref,
    out_matrix_ref, ids_ref, owner_ref, gain_ref, bias_ref, out_weight_ref, taps_ref, copies
):
    chan = lax.axis_index("chan")
    fetched = [
        pltpu.make_async_copy(source, target, copies.at[n])
        for n, (source, target) in enumerate(
            (
                (ids_any, ids_ref),
                (owner_any, owner_ref),
                (gain_any, gain_ref),
                (bias_any, bias_ref),
                (out_weight_any, out_weight_ref),
            )
        )
    ]
    for copy in fetched:
        copy.start()
    half = CHANNELS // 2
    own = pl.multiple_of(chan * half, half)
    other = pl.multiple_of((1 - chan) * half, half)
    for j in range(3):
        for i in range(3):
            for k in range(3):
                block = jnp.concatenate(
                    [weight_ref[k, i, j, pl.ds(own, half), :], weight_ref[k, i, j, pl.ds(other, half), :]],
                    axis=0,
                )
                taps_ref[k, i, j] = block.T
    for copy in fetched:
        copy.wait()
    small_ref[...] = jnp.zeros_like(small_ref)
    small_ref[0:1, :] = gain_ref[...]
    small_ref[1:2, :] = bias_ref[...]
    small_ref[2:3, : ids_ref.shape[1]] = ids_ref[...].astype(F32)
    small_ref[3:4, :SEND_ROWS] = owner_ref[...].astype(F32)
    for i in range(2):
        for j in range(2):
            first = (2 * i + j) * CHANNELS
            out_matrix_ref[:, first : first + CHANNELS] = out_weight_ref[i, j]
    zero = jnp.float32(0.0)
    one = jnp.float32(1.0)
    first = chan == 0
    joined = number_at(small_ref, 0) == number_at(small_ref, 1)
    flag = jnp.where(joined, one, zero)
    on_first = jnp.where(first, one, zero)
    on_second = one - on_first
    near = (
        on_first * (one - flag),
        on_first + on_second * flag,
        zero,
    )
    far = (
        on_first * flag + on_second * (one - flag),
        on_second * (one - flag),
        on_second,
    )
    late_same = (on_second * flag, zero, on_first)
    late_apart = (on_first + on_second * flag, on_first, on_first)
    for j in range(3):
        for i in range(3):
            taps = [taps_ref[k, i, j].astype(F32) for k in range(3)]

            def mixed(scale):
                return (taps[0] * scale[0] + taps[1] * scale[1] + taps[2] * scale[2]).astype(BF16)

            rows = slice(j * CHANNELS, (j + 1) * CHANNELS)
            columns = slice(i * CHANNELS, (i + 1) * CHANNELS)
            shifted = slice((3 + i) * CHANNELS, (4 + i) * CHANNELS)
            local_ref[rows, columns] = mixed(near)
            local_ref[rows, shifted] = mixed(far)
            late_ref[0, rows, columns] = mixed(late_same)
            late_ref[1, rows, columns] = mixed(late_apart)
            sum_ref[rows, columns] = mixed((one, one, one))


def image_row(sources, rows, odd, r):
    half = CHANNELS // 2
    pieces = []
    for ref, start, halos in sources:
        if 0 <= r < rows:
            pieces.append(ref[start + r * half : start + (r + 1) * half, :])
            continue
        edges = [halo_ref[first : first + half, :] for halo_ref, first in halos]
        edges.append(jnp.zeros_like(edges[0]))
        on_first = odd if r < 0 else jnp.logical_not(odd)
        pieces.append(jnp.where(on_first, edges[0], edges[1]))
    return jnp.concatenate(pieces, axis=0)


def local_sources(rows, cross_ref, same_ref, other_ref, own_halos, other_halos):
    half = CHANNELS // 2
    inside = rows * half
    near = (
        (cross_ref, 0, [(ref, 0) for ref in own_halos]),
        (other_ref, inside, [(ref, half) for ref in other_halos]),
    )
    far = (
        (same_ref, 0, [(ref, half) for ref in own_halos]),
        (other_ref, 0, [(ref, 0) for ref in other_halos]),
    )
    return near, far


def joined_columns(product):
    half = product.shape[1] // 2
    left = product[:CHANNELS, :]
    middle = product[CHANNELS : 2 * CHANNELS, :]
    right = product[2 * CHANNELS :, :]
    lane = lax.broadcasted_iota(jnp.int32, (CHANNELS, half), 1)
    from_left = jnp.where(lane == 0, 0.0, pltpu.roll(left[:, half:], 1, 1))
    from_right = jnp.where(lane == half - 1, 0.0, pltpu.roll(right[:, :half], half - 1, 1))
    even = from_left + middle[:, :half] + right[:, half:]
    odd = left[:, :half] + middle[:, half:] + from_right
    return even, odd


def group_place():
    return lax.broadcasted_iota(jnp.int32, (1, CHANNELS), 1) % (CHANNELS // GROUPS)


def group_totals(lines):
    lane = lax.broadcasted_iota(jnp.int32, lines.shape, 1)
    step = 1
    while step < CHANNELS // GROUPS:
        ahead = pltpu.roll(lines, CHANNELS - step, 1)
        behind = pltpu.roll(lines, step, 1)
        lines = lines + jnp.where(lane // step % 2 == 0, ahead, behind)
        step *= 2
    return lines


def lane_totals(first, second):
    rows = [jnp.sum(value.T, axis=0, keepdims=True) for value in (first, second)]
    return rows


def local_kernel(rows, halos, weight_ref, sum_ref, *refs):
    conv_ref, extra_ref, sums_ref, images_ref = refs[3 + 2 * halos :]
    near, far = local_sources(rows, *refs[:3], refs[3 : 3 + halos], refs[3 + halos : 3 + 2 * halos])
    odd = lax.axis_index("space") % 2 == 1
    chan = lax.axis_index("chan")
    half = conv_ref.shape[2] // 2
    for r in range(rows):
        image = jnp.concatenate(
            [image_row(frame, rows, odd, r + i) for frame in (near, far) for i in (-1, 0, 1)], axis=0
        )
        product = jnp.dot(weight_ref[...], image, preferred_element_type=F32)
        for side, value in enumerate(joined_columns(product)):
            conv_ref[r, :, side * half : (side + 1) * half] = value
    sums_ref[...] = jnp.zeros_like(sums_ref)

    @pl.when(lax.axis_index("tm") == 0)
    def _():
        rows_here = rows // 2
        for n in range(rows_here + 2):
            upper = image_row(far, rows, odd, n - 1)
            lower = image_row(near, rows, odd, rows_here + n - 1)
            images_ref[n] = jnp.where(chan == 0, upper, lower)
        totals = [jnp.zeros((CHANNELS, half), F32)] * 2
        for r in range(rows_here):
            image = jnp.concatenate([images_ref[r + i] for i in range(3)], axis=0)
            product = jnp.dot(sum_ref[...], image, preferred_element_type=F32)
            for side, value in enumerate(joined_columns(product)):
                value = value.astype(BF16)
                extra_ref[r, :, side * half : (side + 1) * half] = value
                value = value.astype(F32)
                totals = [totals[0] + value, totals[1] + value * value]
        one, two = lane_totals(*totals)
        sums_ref[0:1, :] = one
        sums_ref[1:2, :] = two


def late_kernel(rows, halos, slabs, small_ref, weight_ref, part_ref, extra_ref, sums_ref, own_edge_ref, *refs):
    near, _ = local_sources(rows, *refs[:3], refs[3 : 3 + halos], refs[3 + halos : 3 + 2 * halos])
    refs = refs[3 + 2 * halos :]
    late_own_ref, late_other_ref, own_halo_ref, other_halo_ref = refs[:4]
    conv_ref, message_ref, keys_ref, images_ref = refs[4:]
    extent = CHANNELS // 2
    arrived = (
        (late_own_ref, 0, [(own_halo_ref, h * extent) for h in range(halos)]),
        (late_other_ref, 0, [(other_halo_ref, h * extent) for h in range(halos)]),
    )
    odd = lax.axis_index("space") % 2 == 1
    slab = lax.axis_index("tm")
    first = lax.axis_index("chan") == 0
    half = part_ref.shape[2] // 2
    kept = rows // 2
    tail = halos * extent
    absent = slab == jnp.where(first, slabs - 1, 0)
    late_tail = jnp.where(absent, 0.0, own_halo_ref[tail:, :CHANNELS].astype(F32))
    own_tail = own_edge_ref[tail:, :CHANNELS].astype(F32)
    number = jnp.max(late_tail[2 * kept : 2 * kept + 1, :]) - 1.0
    ids = [number_at(small_ref, n) for n in range(2)]
    same = number == jnp.where(first, ids[1], ids[0])
    keep = jnp.where(jnp.logical_or(same, jnp.logical_not(first)), 1.0, 0.0)
    use_late = jnp.logical_or(same, first)
    choice = jnp.where(same, 0, 1)
    for r in range(-1, rows + 1):
        late = image_row(arrived, rows, odd, r)
        here = image_row(near, rows, odd, r)
        images_ref[r + 1] = jnp.where(use_late, late, here)
    totals = [jnp.zeros((CHANNELS, half), F32)] * 2
    for r in range(rows):
        image = jnp.concatenate([images_ref[r + i] for i in range(3)], axis=0)
        product = jnp.dot(weight_ref[choice], image, preferred_element_type=F32)
        for side, value in enumerate(joined_columns(product)):
            lanes = slice(side * half, (side + 1) * half)
            value = (value + keep * part_ref[r, :, lanes]).astype(BF16)
            conv_ref[r, :, lanes] = value
            value = value.astype(F32)
            totals = [totals[0] + value, totals[1] + value * value]
    one, two = lane_totals(*totals)
    main_id = jnp.where(first, number, ids[1])
    extra_id = jnp.where(slab == 0, ids[0], -1.0)
    line = lax.broadcasted_iota(jnp.int32, (8, CHANNELS), 0)
    sums = jnp.where(line == 0, one, 0.0)
    sums = jnp.where(line == 1, two, sums)
    sums = jnp.where(line == 2, sums_ref[0:1, :], sums)
    sums = jnp.where(line == 3, sums_ref[1:2, :], sums)
    sums = group_totals(sums)
    place = group_place()
    message = jnp.concatenate(
        [
            jnp.sum(jnp.where(line == jnp.broadcast_to(place, line.shape), sums, 0.0), axis=0, keepdims=True),
            jnp.where(place < 2, main_id, extra_id),
        ],
        axis=0,
    )
    for p in range(message_ref.shape[0]):
        message_ref[p] = message
    keys = jnp.zeros((8, CHANNELS), F32)
    for n in range(kept):
        main_key = jnp.where(first, late_tail[n : n + 1, :], own_tail[kept + n : kept + n + 1, :])
        keys = jnp.where(line == n, main_key, keys)
    quarter = kept // 2
    for n in range(quarter):
        extra_key = jnp.where(first, own_tail[n : n + 1, :], own_tail[quarter + n : quarter + n + 1, :])
        keys = jnp.where(line == kept + n, jnp.where(slab == 0, extra_key, 0.0), keys)
    keys_ref[...] = keys
    conv_ref[rows + kept, :ID_ROWS, :CHANNELS] = jnp.concatenate([keys] * 2, axis=0).astype(BF16)

    @pl.when(slab == 0)
    def _():
        conv_ref[rows : rows + kept] = extra_ref[...]


def crossed(slabs):
    return slabs in (2, 4)


def norm_kernel(
    rows, slabs, spaces, capacity, message_ref, keys_ref, gathered_ref, small_ref, out_matrix_ref, conv_ref, other_ref,
    *send_refs
):
    columns = conv_ref.shape[2]
    half = columns // 2
    kept = rows // 2
    part = MOMENTS // 2
    slab, space, chan = [lax.axis_index(name) for name in PART]
    count = float(rows * columns)
    sums, ids = gathered_ref[:, 0, :], gathered_ref[:, 1, :]
    place = group_place()
    beside = (slab * spaces + space) * 2 + 1 - chan
    numbers = [message_ref[0, 1:2, 0:1], gathered_ref[beside, 1:2, 0:1], message_ref[0, 1:2, 2:3]]
    lines = []
    for number in numbers:
        mask = ids == number
        picked = jnp.sum(jnp.where(mask, sums, 0.0), axis=0, keepdims=True)
        pixels = jnp.where(place == 0, count, jnp.where(place == 2, 0.5 * count, 0.0))
        held = jnp.sum(jnp.where(mask, pixels, 0.0), axis=0, keepdims=True)
        lines += [jnp.where(place % 2 == n, picked, 0.0) for n in range(2)] + [held]
    totals = group_totals(jnp.concatenate(lines + [jnp.zeros((7, CHANNELS), F32)], axis=0))
    matrix = out_matrix_ref[pl.ds(pl.multiple_of(chan * part, part), part), :]

    def factors(first):
        size = float(CHANNELS // GROUPS)
        counts = totals[first + 2 : first + 3, :] * size
        mean = totals[first : first + 1, :] / counts
        var = totals[first + 1 : first + 2, :] / counts - mean * mean
        scale = lax.rsqrt(var + 1e-06) * small_ref[0:1, :]
        offset = small_ref[1:2, :] - mean * scale
        return [jnp.broadcast_to(0.5 * value, (CHANNELS, CHANNELS)).T for value in (scale, offset)]

    def project(source_ref, first, lines, scale, offset):
        images = []
        for r in range(first, first + lines, 2):
            pieces = []
            for i in range(2):
                for j in range(2):
                    value = source_ref[r + i, :, j * half : (j + 1) * half].astype(F32)
                    value = value * scale + offset
                    pieces.append((value + value * jnp.tanh(value)).astype(BF16))
            images.append(jnp.concatenate(pieces, axis=0))
        image = jnp.concatenate(images, axis=1)
        return jnp.dot(matrix, image, preferred_element_type=F32)

    own_keys = keys_ref[...]
    other_keys = other_ref[rows + kept, :ID_ROWS, :CHANNELS].astype(F32)

    def blocks(latent, keys, first):
        return [
            (keys[first + n : first + n + 1, :], latent[:, n * half : (n + 1) * half])
            for n in range(latent.shape[1] // half)
        ]

    def spread(groups, started):
        for d in range(slabs):
            owner = (slab ^ d if crossed(slabs) else jnp.int32(d)).astype(F32)
            for j in range(capacity):
                wanted = owner * float(capacity) + float(j + 1)
                for first, group in groups:
                    ref = send_refs[d].at[first + j] if crossed(slabs) else send_refs[0].at[d, first + j]
                    value = ref[...].astype(F32) if started else jnp.zeros((part, half), F32)
                    for key, block in group:
                        value = jnp.where(key == wanted, block, value)
                    ref[...] = value.astype(BF16)

    mine = project(conv_ref, 0, rows, *factors(0))
    others = project(other_ref, 0, rows, *factors(3))
    second = chan == 1
    now = blocks(jnp.where(second, mine, others), jnp.where(second, own_keys, other_keys[:8, :]), 0)
    following = blocks(jnp.where(second, others, mine), jnp.where(second, other_keys[:8, :], own_keys), 0)
    spread(((0, now), (capacity, following)), False)

    @pl.when(slab == 0)
    def _():
        scale, offset = factors(6)
        begin = []
        for ref, keys in ((conv_ref, own_keys), (other_ref, other_keys)):
            begin += blocks(project(ref, rows, kept, scale, offset), keys, kept)
        spread(((0, begin),), True)


def merge_kernel(slabs, capacity, *refs):
    sources, owned_ref = refs[:-1], refs[-1]
    slab = lax.axis_index("tm")

    def source(d):
        if crossed(slabs):
            return slab ^ d, sources[d]
        return d, sources[0].at[d]

    for d in range(slabs):
        block, ref = source(d)
        for j in range(capacity):
            owned_ref[block * capacity + j] = ref[j]
    for d in range(slabs):
        block, ref = source(d)

        @pl.when(block + 1 < slabs)
        def _():
            for j in range(capacity):
                n = (block + 1) * capacity + j
                owned_ref[n] = (owned_ref[n].astype(F32) + ref[capacity + j].astype(F32)).astype(BF16)


def shards(activations, frame_clip, conv_weight, norm_gain, norm_bias, out_weight, owner):
    half, frames, rows, columns = activations.shape
    sizes = tuple(lax.axis_size(name) for name in PART)
    slabs, spaces, chans = sizes
    assert (frames, chans, half * chans) == (2, 2, CHANNELS)
    parts = slabs * spaces * chans
    halos = 1 if spaces <= 2 else 2
    send_rows = frames * (rows // 2)
    capacity = max(2, 2 * send_rows // slabs)
    kept = rows // 2
    assert send_rows == SEND_ROWS
    payload = jax.ShapeDtypeStruct((rows * half, columns), BF16)
    pair = jax.ShapeDtypeStruct((2 * half, columns), BF16)
    cross, same, both, *edges = whole_call(
        lambda *refs: front_kernel(rows, *refs),
        (payload, payload, jax.ShapeDtypeStruct((2 * rows * half, columns), BF16)) + (pair,) * halos,
        (activations.reshape(half * frames * rows, columns),),
        flops=300000000,
    )
    own_halos = [space_swap(edge, sizes, start) for start, edge in enumerate(edges)]
    late_own = slab_swap(same, sizes, False)
    late_other = slab_swap(cross, sizes, True)
    turn = [(0, 1), (1, 0)]
    local_weight, late_weight, sum_weight, small, out_matrix = whole_call(
        weights_kernel,
        (
            jax.ShapeDtypeStruct((3 * CHANNELS, 6 * CHANNELS), BF16),
            jax.ShapeDtypeStruct((2, 3 * CHANNELS, 3 * CHANNELS), BF16),
            jax.ShapeDtypeStruct((3 * CHANNELS, 3 * CHANNELS), BF16),
            jax.ShapeDtypeStruct((8, CHANNELS), F32),
            jax.ShapeDtypeStruct((MOMENTS, 4 * CHANNELS), BF16),
        ),
        (
            frame_clip.reshape(1, frames), owner.reshape(1, send_rows), norm_gain.reshape(1, CHANNELS),
            norm_bias.reshape(1, CHANNELS), out_weight.transpose(0, 1, 3, 2), conv_weight, both,
        ),
        [
            pltpu.VMEM((1, frames), jnp.int32),
            pltpu.VMEM((1, send_rows), jnp.int32),
            pltpu.VMEM((1, CHANNELS), F32),
            pltpu.VMEM((1, CHANNELS), F32),
            pltpu.VMEM((2, 2, MOMENTS, CHANNELS), BF16),
            pltpu.VMEM((3, 3, 3, CHANNELS, CHANNELS), BF16),
            pltpu.SemaphoreType.DMA((5,)),
        ],
        [pl.BlockSpec(memory_space=pl.ANY)] * 5 + [VMEM] * 2,
        1200000000,
    )
    other = lax.ppermute(both, "chan", turn)
    message_halo = jax.ShapeDtypeStruct((halos * half + ID_ROWS, columns), BF16)
    *own_halos, cross_halo, same_halo = whole_call(
        lambda *refs: halo_kernel(halos, capacity, *refs),
        (pair,) * halos + (message_halo, message_halo),
        (small, *own_halos),
    )
    other_halos = [lax.ppermute(halo, "chan", turn) for halo in own_halos]
    late_own_halo = slab_swap(same_halo, sizes, False)
    late_other_halo = slab_swap(cross_halo, sizes, True)
    here = (cross, same, other, *own_halos, *other_halos)
    part, extra, extra_sums = whole_call(
        lambda *refs: local_kernel(rows, halos, *refs),
        (
            jax.ShapeDtypeStruct((rows, CHANNELS, columns), F32),
            jax.ShapeDtypeStruct((rows // 2, CHANNELS, columns), BF16),
            jax.ShapeDtypeStruct((8, CHANNELS), F32),
        ),
        (local_weight, sum_weight, *here),
        [pltpu.VMEM((rows // 2 + 2, CHANNELS, columns), BF16)],
        flops=1800000000,
    )
    conv, message, keys = whole_call(
        lambda *refs: late_kernel(rows, halos, slabs, *refs),
        (
            jax.ShapeDtypeStruct((rows + kept + 1, CHANNELS, columns), BF16),
            jax.ShapeDtypeStruct((parts, 2, CHANNELS), F32),
            jax.ShapeDtypeStruct((8, CHANNELS), F32),
        ),
        (
            small, late_weight, part, extra, extra_sums, cross_halo, *here, late_own, late_other, late_own_halo, late_other_halo,
        ),
        [pltpu.VMEM((rows + 2, CHANNELS, columns), BF16)],
        flops=1500000000,
    )
    conv_other = lax.ppermute(conv, "chan", turn)
    gathered = lax.all_to_all(message, PART, split_axis=0, concat_axis=0, tiled=True)
    part = MOMENTS // chans
    width = columns // 2
    blocks = (2 * capacity, part, width)
    if crossed(slabs):
        shapes = (jax.ShapeDtypeStruct(blocks, BF16),) * slabs
    else:
        shapes = (jax.ShapeDtypeStruct((slabs,) + blocks, BF16),)
    sends = whole_call(
        lambda *refs: norm_kernel(rows, slabs, spaces, capacity, *refs),
        shapes,
        (message, keys, gathered, small, out_matrix, conv, conv_other),
    )
    if crossed(slabs):
        received = [sends[0]]
        for d in range(1, slabs):
            received.append(lax.ppermute(sends[d], "tm", [(t, t ^ d) for t in range(slabs)]))
    else:
        received = [lax.all_to_all(sends[0], "tm", split_axis=0, concat_axis=0, tiled=True)]
    turns = list((0, 3, 1, 2)) if crossed(slabs) else [0]
    owned = pl.pallas_call(
        lambda *refs: merge_kernel(slabs, capacity, *[refs[turns.index(d)] for d in range(len(turns))], refs[-1]),
        out_shape=jax.ShapeDtypeStruct((slabs * capacity, part, width), BF16),
        in_specs=[VMEM] * len(received),
        out_specs=pl.BlockSpec((slabs * capacity, part, width), lambda: (0, 0, 0)),
        compiler_params=PARAMS,
    )(*[received[d] for d in turns])
    return owned[None]


def solution(mesh):
    placed = (
        P(("groups", "chan"), "tm", "space", None),
        P(("groups", "tm")),
        P(),
        P(),
        P(),
        P(),
        P(("groups", "space"), "tm", None),
    )
    return jax.shard_map(
        shards,
        mesh=mesh,
        in_specs=placed,
        out_specs=P(("groups", "space"), "tm", "chan", None),
        check_vma=False,
    )
```

```python
import jax
import jax.numpy as jnp
import numpy as np
from jax import lax
from jax.experimental import pallas as pl
from jax.experimental.pallas import tpu as pltpu
from jax.sharding import PartitionSpec as P

CHANNELS = 128
GROUPS = 32
MOMENTS = 32
SEND_ROWS = 8
ID_ROWS = 16
BLOCK = 16
BF16 = jnp.bfloat16
F32 = jnp.float32
VMEM = pl.BlockSpec(memory_space=pltpu.VMEM)
PARAMS = pltpu.CompilerParams(vmem_limit_bytes=40 * 1024 * 1024)
PART = ("tm", "space", "chan")


def flat_pairs(sizes, pairs):
    _, spaces, chans = sizes
    return [
        ((a[0] * spaces + a[1]) * chans + a[2], (b[0] * spaces + b[1]) * chans + b[2])
        for a, b in pairs
    ]


def space_swap(value, sizes, start):
    slabs, spaces, chans = sizes
    pairs = []
    for low in range(start, spaces - 1, 2):
        for t in range(slabs):
            for c in range(chans):
                pairs += [((t, low, c), (t, low + 1, c)), ((t, low + 1, c), (t, low, c))]
    return lax.ppermute(value, PART, flat_pairs(sizes, pairs))


def slab_swap(value, sizes, cross):
    slabs, spaces, _ = sizes
    last = slabs - 1
    pairs = []
    for s in range(spaces):
        for t in range(last):
            if cross:
                pairs += [((t, s, 0), (t + 1, s, 1)), ((t + 1, s, 1), (t, s, 0))]
            else:
                pairs += [((t, s, 1), (t + 1, s, 1)), ((t + 1, s, 0), (t, s, 0))]
        if spaces % 2 == 0 and cross:
            pairs += [((0, s, 1), (0, s ^ 1, 1)), ((last, s, 0), (last, s ^ 1, 0))]
        elif spaces % 2 == 0:
            pairs += [((last, s, 1), (last, s, 0)), ((0, s, 0), (0, s, 1))]
    return lax.ppermute(value, PART, flat_pairs(sizes, pairs))


def whole_call(kernel, out_shape, args, scratch=(), specs=None, flops=0, vmem=40, first=()):
    turns = list(first) + [n for n in range(len(args)) if n not in first]
    specs = specs or [VMEM] * len(args)

    def turned(*refs):
        kernel(*[refs[turns.index(n)] for n in range(len(args))], *refs[len(args) :])

    return pl.pallas_call(
        turned,
        out_shape=out_shape,
        in_specs=[specs[n] for n in turns],
        out_specs=jax.tree.map(lambda _: VMEM, out_shape),
        scratch_shapes=scratch,
        compiler_params=pltpu.CompilerParams(vmem_limit_bytes=vmem * 1024 * 1024),
        cost_estimate=pl.CostEstimate(flops=flops, bytes_accessed=flops // 400, transcendentals=0),
    )(*[args[n] for n in turns])


def number_at(small_ref, n):
    lane = lax.broadcasted_iota(jnp.int32, (1, CHANNELS), 1)
    return jnp.sum(jnp.where(lane == n, small_ref[2:3, :], 0.0))


def front_kernel(rows, pixels_ref, cross_ref, same_ref, both_ref, *edge_refs):
    chan = lax.axis_index("chan")
    odd = lax.axis_index("space") % 2 == 1
    half, columns = CHANNELS // 2, pixels_ref.shape[1]
    size = 2 * rows * BLOCK
    source = lax.broadcasted_iota(jnp.int32, (columns, columns), 0)
    target = lax.broadcasted_iota(jnp.int32, (1, columns), 1)
    wanted = jnp.where(target < columns // 2, 2 * target, 2 * target - columns + 1)
    split = jnp.where(source == wanted, 1.0, 0.0).astype(BF16)
    placed = lax.broadcasted_iota(jnp.int32, (size, size), 1)
    line = lax.broadcasted_iota(jnp.int32, (size, 1), 0)
    second = line // (rows * BLOCK)
    frame = jnp.where(second == 0, 1 - chan, chan)
    row = line // BLOCK % rows
    origin = line % BLOCK * (2 * rows) + frame * rows + row
    turn = jnp.where(placed == origin, 1.0, 0.0).astype(BF16)
    inside = rows * half
    for n in range(half // BLOCK):
        image = pixels_ref[n * size : (n + 1) * size, :]
        image = jnp.dot(turn, image, preferred_element_type=F32).astype(BF16)
        image = jnp.dot(image, split, preferred_element_type=F32).astype(BF16)
        for f, out_ref in enumerate((cross_ref, same_ref)):
            for r in range(rows):
                first = (f * rows + r) * BLOCK
                block = image[first : first + BLOCK, :]
                first = r * half + n * BLOCK
                out_ref[first : first + BLOCK, :] = block
                both_ref[f * inside + first : f * inside + first + BLOCK, :] = block
    for f, out_ref in enumerate((cross_ref, same_ref)):
        low, high = out_ref[:half, :], out_ref[(rows - 1) * half :, :]
        for h, edge_ref in enumerate(edge_refs):
            to_low = odd if h == 0 else jnp.logical_not(odd)
            edge_ref[f * half : (f + 1) * half, :] = jnp.where(to_low, low, high)


def halo_kernel(halos, capacity, small_ref, *refs):
    halo_refs, kept_refs, (cross_ref, same_ref) = refs[:halos], refs[halos : 2 * halos], refs[2 * halos :]
    for halo_ref, kept_ref in zip(halo_refs, kept_refs):
        kept_ref[...] = halo_ref[...]
    chan = lax.axis_index("chan")
    half, columns = CHANNELS // 2, cross_ref.shape[1]
    count = SEND_ROWS
    line = lax.broadcasted_iota(jnp.int32, (ID_ROWS, CHANNELS), 0)
    lane = lax.broadcasted_iota(jnp.int32, (ID_ROWS, CHANNELS), 1)
    owners = jnp.broadcast_to(small_ref[3:4, :], (ID_ROWS, CHANNELS))
    mine = jnp.sum(jnp.where(line == lane, owners, 0.0), axis=1, keepdims=True)
    rank = jnp.sum(jnp.where((owners == mine) & (lane < line), 1.0, 0.0), axis=1, keepdims=True)
    keys = mine * float(capacity) + rank + 1.0
    place = lax.broadcasted_iota(jnp.int32, (ID_ROWS, columns), 0)
    tail = jnp.where(place < count, keys, 0.0)
    ids = [number_at(small_ref, n) for n in range(2)]
    for n, (out_ref, frame) in enumerate(((cross_ref, 1 - chan), (same_ref, chan))):
        for h in range(halos):
            out_ref[h * half : (h + 1) * half, :] = halo_refs[h][n * half : (n + 1) * half, :]
        number = jnp.where(frame == 0, ids[0], ids[1])
        out_ref[halos * half :, :] = jnp.where(place == count, number + 1.0, tail).astype(BF16)


def weights_kernel(
    ids_any, owner_any, gain_any, bias_any, out_weight_any, weight_ref, _, local_ref, late_ref, sum_ref, small_ref,
    out_matrix_ref, ids_ref, owner_ref, gain_ref, bias_ref, out_weight_ref, taps_ref, copies
):
    chan = lax.axis_index("chan")
    fetched = [
        pltpu.make_async_copy(source, target, copies.at[n])
        for n, (source, target) in enumerate(
            (
                (ids_any, ids_ref),
                (owner_any, owner_ref),
                (gain_any, gain_ref),
                (bias_any, bias_ref),
                (out_weight_any, out_weight_ref),
            )
        )
    ]
    for copy in fetched:
        copy.start()
    half = CHANNELS // 2
    own = pl.multiple_of(chan * half, half)
    other = pl.multiple_of((1 - chan) * half, half)
    for j in range(3):
        for i in range(3):
            for k in range(3):
                block = jnp.concatenate(
                    [weight_ref[k, i, j, pl.ds(own, half), :], weight_ref[k, i, j, pl.ds(other, half), :]],
                    axis=0,
                )
                taps_ref[k, i, j] = block.T
    for copy in fetched:
        copy.wait()
    small_ref[...] = jnp.zeros_like(small_ref)
    small_ref[0:1, :] = gain_ref[...]
    small_ref[1:2, :] = bias_ref[...]
    small_ref[2:3, : ids_ref.shape[1]] = ids_ref[...].astype(F32)
    small_ref[3:4, :SEND_ROWS] = owner_ref[...].astype(F32)
    for i in range(2):
        for j in range(2):
            first = (2 * i + j) * CHANNELS
            out_matrix_ref[:, first : first + CHANNELS] = out_weight_ref[i, j]
    zero = jnp.float32(0.0)
    one = jnp.float32(1.0)
    first = chan == 0
    joined = number_at(small_ref, 0) == number_at(small_ref, 1)
    flag = jnp.where(joined, one, zero)
    on_first = jnp.where(first, one, zero)
    on_second = one - on_first
    near = (
        on_first * (one - flag),
        on_first + on_second * flag,
        zero,
    )
    far = (
        on_first * flag + on_second * (one - flag),
        on_second * (one - flag),
        on_second,
    )
    late_same = (on_second * flag, zero, on_first)
    late_apart = (on_first + on_second * flag, on_first, on_first)
    for j in range(3):
        for i in range(3):
            taps = [taps_ref[k, i, j].astype(F32) for k in range(3)]

            def mixed(scale):
                return (taps[0] * scale[0] + taps[1] * scale[1] + taps[2] * scale[2]).astype(BF16)

            rows = slice(j * CHANNELS, (j + 1) * CHANNELS)
            columns = slice(i * CHANNELS, (i + 1) * CHANNELS)
            shifted = slice((3 + i) * CHANNELS, (4 + i) * CHANNELS)
            local_ref[rows, columns] = mixed(near)
            local_ref[rows, shifted] = mixed(far)
            late_ref[0, rows, columns] = mixed(late_same)
            late_ref[1, rows, columns] = mixed(late_apart)
            sum_ref[rows, columns] = mixed((one, one, one))


def image_row(sources, rows, odd, r):
    half = CHANNELS // 2
    pieces = []
    for ref, start, halos in sources:
        if 0 <= r < rows:
            pieces.append(ref[start + r * half : start + (r + 1) * half, :])
            continue
        edges = [halo_ref[first : first + half, :] for halo_ref, first in halos]
        edges.append(jnp.zeros_like(edges[0]))
        on_first = odd if r < 0 else jnp.logical_not(odd)
        pieces.append(jnp.where(on_first, edges[0], edges[1]))
    return jnp.concatenate(pieces, axis=0)


def local_sources(rows, cross_ref, same_ref, other_ref, own_halos, other_halos):
    half = CHANNELS // 2
    inside = rows * half
    near = (
        (cross_ref, 0, [(ref, 0) for ref in own_halos]),
        (other_ref, inside, [(ref, half) for ref in other_halos]),
    )
    far = (
        (same_ref, 0, [(ref, half) for ref in own_halos]),
        (other_ref, 0, [(ref, 0) for ref in other_halos]),
    )
    return near, far


def joined_columns(product):
    half = product.shape[1] // 2
    left = product[:CHANNELS, :]
    middle = product[CHANNELS : 2 * CHANNELS, :]
    right = product[2 * CHANNELS :, :]
    lane = lax.broadcasted_iota(jnp.int32, (CHANNELS, half), 1)
    from_left = jnp.where(lane == 0, 0.0, pltpu.roll(left[:, half:], 1, 1))
    from_right = jnp.where(lane == half - 1, 0.0, pltpu.roll(right[:, :half], half - 1, 1))
    even = from_left + middle[:, :half] + right[:, half:]
    odd = left[:, :half] + middle[:, half:] + from_right
    return even, odd


def group_place():
    return lax.broadcasted_iota(jnp.int32, (1, CHANNELS), 1) % (CHANNELS // GROUPS)


def group_totals(lines):
    lane = lax.broadcasted_iota(jnp.int32, lines.shape, 1)
    step = 1
    while step < CHANNELS // GROUPS:
        ahead = pltpu.roll(lines, CHANNELS - step, 1)
        behind = pltpu.roll(lines, step, 1)
        lines = lines + jnp.where(lane // step % 2 == 0, ahead, behind)
        step *= 2
    return lines


def lane_totals(first, second):
    rows = [jnp.sum(value.T, axis=0, keepdims=True) for value in (first, second)]
    return rows


def local_kernel(rows, halos, weight_ref, sum_ref, *refs):
    conv_ref, extra_ref, sums_ref, images_ref = refs[3 + 2 * halos :]
    near, far = local_sources(rows, *refs[:3], refs[3 : 3 + halos], refs[3 + halos : 3 + 2 * halos])
    odd = lax.axis_index("space") % 2 == 1
    chan = lax.axis_index("chan")
    half = conv_ref.shape[2] // 2
    for r in range(rows):
        image = jnp.concatenate(
            [image_row(frame, rows, odd, r + i) for frame in (near, far) for i in (-1, 0, 1)], axis=0
        )
        product = jnp.dot(weight_ref[...], image, preferred_element_type=F32)
        for side, value in enumerate(joined_columns(product)):
            conv_ref[r, :, side * half : (side + 1) * half] = value
    sums_ref[...] = jnp.zeros_like(sums_ref)

    @pl.when(lax.axis_index("tm") == 0)
    def _():
        rows_here = rows // 2
        for n in range(rows_here + 2):
            upper = image_row(far, rows, odd, n - 1)
            lower = image_row(near, rows, odd, rows_here + n - 1)
            images_ref[n] = jnp.where(chan == 0, upper, lower)
        totals = [jnp.zeros((CHANNELS, half), F32)] * 2
        for r in range(rows_here):
            image = jnp.concatenate([images_ref[r + i] for i in range(3)], axis=0)
            product = jnp.dot(sum_ref[...], image, preferred_element_type=F32)
            for side, value in enumerate(joined_columns(product)):
                value = value.astype(BF16)
                extra_ref[r, :, side * half : (side + 1) * half] = value
                value = value.astype(F32)
                totals = [totals[0] + value, totals[1] + value * value]
        one, two = lane_totals(*totals)
        sums_ref[0:1, :] = one
        sums_ref[1:2, :] = two


def late_kernel(rows, halos, slabs, small_ref, weight_ref, part_ref, extra_ref, sums_ref, own_edge_ref, *refs):
    near, _ = local_sources(rows, *refs[:3], refs[3 : 3 + halos], refs[3 + halos : 3 + 2 * halos])
    refs = refs[3 + 2 * halos :]
    late_own_ref, late_other_ref, own_halo_ref, other_halo_ref = refs[:4]
    conv_ref, message_ref, keys_ref, images_ref = refs[4:]
    extent = CHANNELS // 2
    arrived = (
        (late_own_ref, 0, [(own_halo_ref, h * extent) for h in range(halos)]),
        (late_other_ref, 0, [(other_halo_ref, h * extent) for h in range(halos)]),
    )
    odd = lax.axis_index("space") % 2 == 1
    slab = lax.axis_index("tm")
    first = lax.axis_index("chan") == 0
    half = part_ref.shape[2] // 2
    kept = rows // 2
    tail = halos * extent
    absent = slab == jnp.where(first, slabs - 1, 0)
    late_tail = jnp.where(absent, 0.0, own_halo_ref[tail:, :CHANNELS].astype(F32))
    own_tail = own_edge_ref[tail:, :CHANNELS].astype(F32)
    number = jnp.max(late_tail[2 * kept : 2 * kept + 1, :]) - 1.0
    ids = [number_at(small_ref, n) for n in range(2)]
    same = number == jnp.where(first, ids[1], ids[0])
    keep = jnp.where(jnp.logical_or(same, jnp.logical_not(first)), 1.0, 0.0)
    use_late = jnp.logical_or(same, first)
    choice = jnp.where(same, 0, 1)
    for r in range(-1, rows + 1):
        late = image_row(arrived, rows, odd, r)
        here = image_row(near, rows, odd, r)
        images_ref[r + 1] = jnp.where(use_late, late, here)
    totals = [jnp.zeros((CHANNELS, half), F32)] * 2
    for r in range(rows):
        image = jnp.concatenate([images_ref[r + i] for i in range(3)], axis=0)
        product = jnp.dot(weight_ref[choice], image, preferred_element_type=F32)
        for side, value in enumerate(joined_columns(product)):
            lanes = slice(side * half, (side + 1) * half)
            value = (value + keep * part_ref[r, :, lanes]).astype(BF16)
            conv_ref[r, :, lanes] = value
            value = value.astype(F32)
            totals = [totals[0] + value, totals[1] + value * value]
    one, two = lane_totals(*totals)
    main_id = jnp.where(first, number, ids[1])
    extra_id = jnp.where(slab == 0, ids[0], -1.0)
    line = lax.broadcasted_iota(jnp.int32, (8, CHANNELS), 0)
    sums = jnp.where(line == 0, one, 0.0)
    sums = jnp.where(line == 1, two, sums)
    sums = jnp.where(line == 2, sums_ref[0:1, :], sums)
    sums = jnp.where(line == 3, sums_ref[1:2, :], sums)
    sums = group_totals(sums)
    place = group_place()
    message = jnp.concatenate(
        [
            jnp.sum(jnp.where(line == jnp.broadcast_to(place, line.shape), sums, 0.0), axis=0, keepdims=True),
            jnp.where(place < 2, main_id, extra_id),
        ],
        axis=0,
    )
    for p in range(message_ref.shape[0]):
        message_ref[p] = message
    keys = jnp.zeros((8, CHANNELS), F32)
    for n in range(kept):
        main_key = jnp.where(first, late_tail[n : n + 1, :], own_tail[kept + n : kept + n + 1, :])
        keys = jnp.where(line == n, main_key, keys)
    quarter = kept // 2
    for n in range(quarter):
        extra_key = jnp.where(first, own_tail[n : n + 1, :], own_tail[quarter + n : quarter + n + 1, :])
        keys = jnp.where(line == kept + n, jnp.where(slab == 0, extra_key, 0.0), keys)
    keys_ref[...] = keys
    conv_ref[rows + kept, :ID_ROWS, :CHANNELS] = jnp.concatenate([keys] * 2, axis=0).astype(BF16)

    @pl.when(slab == 0)
    def _():
        conv_ref[rows : rows + kept] = extra_ref[...]


def crossed(slabs):
    return slabs in (2, 4)


def norm_kernel(
    rows, slabs, spaces, capacity, message_ref, keys_ref, gathered_ref, small_ref, out_matrix_ref, conv_ref, other_ref,
    *send_refs
):
    columns = conv_ref.shape[2]
    half = columns // 2
    kept = rows // 2
    part = MOMENTS // 2
    slab, space, chan = [lax.axis_index(name) for name in PART]
    count = float(rows * columns)
    sums, ids = gathered_ref[:, 0, :], gathered_ref[:, 1, :]
    place = group_place()
    beside = (slab * spaces + space) * 2 + 1 - chan
    numbers = [message_ref[0, 1:2, 0:1], gathered_ref[beside, 1:2, 0:1], message_ref[0, 1:2, 2:3]]
    lines = []
    for number in numbers:
        mask = ids == number
        picked = jnp.sum(jnp.where(mask, sums, 0.0), axis=0, keepdims=True)
        pixels = jnp.where(place == 0, count, jnp.where(place == 2, 0.5 * count, 0.0))
        held = jnp.sum(jnp.where(mask, pixels, 0.0), axis=0, keepdims=True)
        lines += [jnp.where(place % 2 == n, picked, 0.0) for n in range(2)] + [held]
    totals = group_totals(jnp.concatenate(lines + [jnp.zeros((7, CHANNELS), F32)], axis=0))
    matrix = out_matrix_ref[pl.ds(pl.multiple_of(chan * part, part), part), :]

    def factors(first):
        size = float(CHANNELS // GROUPS)
        counts = totals[first + 2 : first + 3, :] * size
        mean = totals[first : first + 1, :] / counts
        var = totals[first + 1 : first + 2, :] / counts - mean * mean
        scale = lax.rsqrt(var + 1e-06) * small_ref[0:1, :]
        offset = small_ref[1:2, :] - mean * scale
        return [jnp.broadcast_to(0.5 * value, (CHANNELS, CHANNELS)).T for value in (scale, offset)]

    def project(source_ref, first, lines, scale, offset):
        images = []
        for r in range(first, first + lines, 2):
            pieces = []
            for i in range(2):
                for j in range(2):
                    value = source_ref[r + i, :, j * half : (j + 1) * half].astype(F32)
                    value = value * scale + offset
                    pieces.append((value + value * jnp.tanh(value)).astype(BF16))
            images.append(jnp.concatenate(pieces, axis=0))
        image = jnp.concatenate(images, axis=1)
        return jnp.dot(matrix, image, preferred_element_type=F32)

    own_keys = keys_ref[...]
    other_keys = other_ref[rows + kept, :ID_ROWS, :CHANNELS].astype(F32)

    def blocks(latent, keys, first):
        return [
            (keys[first + n : first + n + 1, :], latent[:, n * half : (n + 1) * half])
            for n in range(latent.shape[1] // half)
        ]

    def spread(groups, started):
        for d in range(slabs):
            owner = (slab ^ d if crossed(slabs) else jnp.int32(d)).astype(F32)
            for j in range(capacity):
                wanted = owner * float(capacity) + float(j + 1)
                for first, group in groups:
                    ref = send_refs[d].at[first + j] if crossed(slabs) else send_refs[0].at[d, first + j]
                    value = ref[...].astype(F32) if started else jnp.zeros((part, half), F32)
                    for key, block in group:
                        value = jnp.where(key == wanted, block, value)
                    ref[...] = value.astype(BF16)

    mine = project(conv_ref, 0, rows, *factors(0))
    others = project(other_ref, 0, rows, *factors(3))
    second = chan == 1
    now = blocks(jnp.where(second, mine, others), jnp.where(second, own_keys, other_keys[:8, :]), 0)
    following = blocks(jnp.where(second, others, mine), jnp.where(second, other_keys[:8, :], own_keys), 0)
    spread(((0, now), (capacity, following)), False)

    @pl.when(slab == 0)
    def _():
        scale, offset = factors(6)
        begin = []
        for ref, keys in ((conv_ref, own_keys), (other_ref, other_keys)):
            begin += blocks(project(ref, rows, kept, scale, offset), keys, kept)
        spread(((0, begin),), True)


def merge_kernel(slabs, capacity, *refs):
    sources, owned_ref = refs[:-1], refs[-1]
    slab = lax.axis_index("tm")

    def source(d):
        if crossed(slabs):
            return slab ^ d, sources[d]
        return d, sources[0].at[d]

    for d in range(slabs):
        block, ref = source(d)
        for j in range(capacity):
            owned_ref[block * capacity + j] = ref[j]
    for d in range(slabs):
        block, ref = source(d)

        @pl.when(block + 1 < slabs)
        def _():
            for j in range(capacity):
                n = (block + 1) * capacity + j
                owned_ref[n] = (owned_ref[n].astype(F32) + ref[capacity + j].astype(F32)).astype(BF16)


def shards(activations, frame_clip, conv_weight, norm_gain, norm_bias, out_weight, owner):
    half, frames, rows, columns = activations.shape
    sizes = tuple(lax.axis_size(name) for name in PART)
    slabs, spaces, chans = sizes
    assert (frames, chans, half * chans) == (2, 2, CHANNELS)
    parts = slabs * spaces * chans
    halos = 1 if spaces <= 2 else 2
    send_rows = frames * (rows // 2)
    capacity = max(2, 2 * send_rows // slabs)
    kept = rows // 2
    assert send_rows == SEND_ROWS
    payload = jax.ShapeDtypeStruct((rows * half, columns), BF16)
    pair = jax.ShapeDtypeStruct((2 * half, columns), BF16)
    cross, same, both, *edges = whole_call(
        lambda *refs: front_kernel(rows, *refs),
        (payload, payload, jax.ShapeDtypeStruct((2 * rows * half, columns), BF16)) + (pair,) * halos,
        (activations.reshape(half * frames * rows, columns),),
        flops=3000000000,
    )
    own_halos = [space_swap(edge, sizes, start) for start, edge in enumerate(edges)]
    late_own = slab_swap(same, sizes, False)
    late_other = slab_swap(cross, sizes, True)
    turn = [(0, 1), (1, 0)]
    local_weight, late_weight, sum_weight, small, out_matrix = whole_call(
        weights_kernel,
        (
            jax.ShapeDtypeStruct((3 * CHANNELS, 6 * CHANNELS), BF16),
            jax.ShapeDtypeStruct((2, 3 * CHANNELS, 3 * CHANNELS), BF16),
            jax.ShapeDtypeStruct((3 * CHANNELS, 3 * CHANNELS), BF16),
            jax.ShapeDtypeStruct((8, CHANNELS), F32),
            jax.ShapeDtypeStruct((MOMENTS, 4 * CHANNELS), BF16),
        ),
        (
            frame_clip.reshape(1, frames), owner.reshape(1, send_rows), norm_gain.reshape(1, CHANNELS),
            norm_bias.reshape(1, CHANNELS), out_weight.transpose(0, 1, 3, 2), conv_weight, both,
        ),
        [
            pltpu.VMEM((1, frames), jnp.int32),
            pltpu.VMEM((1, send_rows), jnp.int32),
            pltpu.VMEM((1, CHANNELS), F32),
            pltpu.VMEM((1, CHANNELS), F32),
            pltpu.VMEM((2, 2, MOMENTS, CHANNELS), BF16),
            pltpu.VMEM((3, 3, 3, CHANNELS, CHANNELS), BF16),
            pltpu.SemaphoreType.DMA((5,)),
        ],
        [pl.BlockSpec(memory_space=pl.ANY)] * 5 + [VMEM] * 2,
        1200000000,
    )
    other = lax.ppermute(both, "chan", turn)
    message_halo = jax.ShapeDtypeStruct((halos * half + ID_ROWS, columns), BF16)
    *own_halos, cross_halo, same_halo = whole_call(
        lambda *refs: halo_kernel(halos, capacity, *refs),
        (pair,) * halos + (message_halo, message_halo),
        (small, *own_halos),
    )
    other_halos = [lax.ppermute(halo, "chan", turn) for halo in own_halos]
    late_own_halo = slab_swap(same_halo, sizes, False)
    late_other_halo = slab_swap(cross_halo, sizes, True)
    here = (cross, same, other, *own_halos, *other_halos)
    part, extra, extra_sums = whole_call(
        lambda *refs: local_kernel(rows, halos, *refs),
        (
            jax.ShapeDtypeStruct((rows, CHANNELS, columns), F32),
            jax.ShapeDtypeStruct((rows // 2, CHANNELS, columns), BF16),
            jax.ShapeDtypeStruct((8, CHANNELS), F32),
        ),
        (local_weight, sum_weight, *here),
        [pltpu.VMEM((rows // 2 + 2, CHANNELS, columns), BF16)],
        flops=1800000000,
    )
    conv, message, keys = whole_call(
        lambda *refs: late_kernel(rows, halos, slabs, *refs),
        (
            jax.ShapeDtypeStruct((rows + kept + 1, CHANNELS, columns), BF16),
            jax.ShapeDtypeStruct((parts, 2, CHANNELS), F32),
            jax.ShapeDtypeStruct((8, CHANNELS), F32),
        ),
        (
            small, late_weight, part, extra, extra_sums, cross_halo, *here, late_own, late_other, late_own_halo, late_other_halo,
        ),
        [pltpu.VMEM((rows + 2, CHANNELS, columns), BF16)],
        flops=1500000000,
    )
    conv_other = lax.ppermute(conv, "chan", turn)
    gathered = lax.all_to_all(message, PART, split_axis=0, concat_axis=0, tiled=True)
    part = MOMENTS // chans
    width = columns // 2
    blocks = (2 * capacity, part, width)
    if crossed(slabs):
        shapes = (jax.ShapeDtypeStruct(blocks, BF16),) * slabs
    else:
        shapes = (jax.ShapeDtypeStruct((slabs,) + blocks, BF16),)
    sends = whole_call(
        lambda *refs: norm_kernel(rows, slabs, spaces, capacity, *refs),
        shapes,
        (message, keys, gathered, small, out_matrix, conv, conv_other),
    )
    if crossed(slabs):
        received = [sends[0]]
        for d in range(1, slabs):
            received.append(lax.ppermute(sends[d], "tm", [(t, t ^ d) for t in range(slabs)]))
    else:
        received = [lax.all_to_all(sends[0], "tm", split_axis=0, concat_axis=0, tiled=True)]
    turns = list((0, 3, 1, 2)) if crossed(slabs) else [0]
    owned = pl.pallas_call(
        lambda *refs: merge_kernel(slabs, capacity, *[refs[turns.index(d)] for d in range(len(turns))], refs[-1]),
        out_shape=jax.ShapeDtypeStruct((slabs * capacity, part, width), BF16),
        in_specs=[VMEM] * len(received),
        out_specs=pl.BlockSpec((slabs * capacity, part, width), lambda: (0, 0, 0)),
        compiler_params=PARAMS,
    )(*[received[d] for d in turns])
    return owned[None]


def solution(mesh):
    placed = (
        P(("groups", "chan"), "tm", "space", None),
        P(("groups", "tm")),
        P(),
        P(),
        P(),
        P(),
        P(("groups", "space"), "tm", None),
    )
    return jax.shard_map(
        shards,
        mesh=mesh,
        in_specs=placed,
        out_specs=P(("groups", "space"), "tm", "chan", None),
        check_vma=False,
    )
```

```python
import jax
import jax.numpy as jnp
import numpy as np
from jax import lax
from jax.experimental import pallas as pl
from jax.experimental.pallas import tpu as pltpu
from jax.sharding import PartitionSpec as P

CHANNELS = 128
GROUPS = 32
MOMENTS = 32
SEND_ROWS = 8
ID_ROWS = 16
BLOCK = 16
BF16 = jnp.bfloat16
F32 = jnp.float32
VMEM = pl.BlockSpec(memory_space=pltpu.VMEM)
PARAMS = pltpu.CompilerParams(vmem_limit_bytes=40 * 1024 * 1024)
PART = ("tm", "space", "chan")


def flat_pairs(sizes, pairs):
    _, spaces, chans = sizes
    return [
        ((a[0] * spaces + a[1]) * chans + a[2], (b[0] * spaces + b[1]) * chans + b[2])
        for a, b in pairs
    ]


def space_swap(value, sizes, start):
    slabs, spaces, chans = sizes
    pairs = []
    for low in range(start, spaces - 1, 2):
        for t in range(slabs):
            for c in range(chans):
                pairs += [((t, low, c), (t, low + 1, c)), ((t, low + 1, c), (t, low, c))]
    return lax.ppermute(value, PART, flat_pairs(sizes, pairs))


def slab_swap(value, sizes, cross):
    slabs, spaces, _ = sizes
    last = slabs - 1
    pairs = []
    for s in range(spaces):
        for t in range(last):
            if cross:
                pairs += [((t, s, 0), (t + 1, s, 1)), ((t + 1, s, 1), (t, s, 0))]
            else:
                pairs += [((t, s, 1), (t + 1, s, 1)), ((t + 1, s, 0), (t, s, 0))]
        if spaces % 2 == 0 and cross:
            pairs += [((0, s, 1), (0, s ^ 1, 1)), ((last, s, 0), (last, s ^ 1, 0))]
        elif spaces % 2 == 0:
            pairs += [((last, s, 1), (last, s, 0)), ((0, s, 0), (0, s, 1))]
    return lax.ppermute(value, PART, flat_pairs(sizes, pairs))


def whole_call(kernel, out_shape, args, scratch=(), specs=None, flops=0, vmem=40, first=()):
    turns = list(first) + [n for n in range(len(args)) if n not in first]
    specs = specs or [VMEM] * len(args)

    def turned(*refs):
        kernel(*[refs[turns.index(n)] for n in range(len(args))], *refs[len(args) :])

    return pl.pallas_call(
        turned,
        out_shape=out_shape,
        in_specs=[specs[n] for n in turns],
        out_specs=jax.tree.map(lambda _: VMEM, out_shape),
        scratch_shapes=scratch,
        compiler_params=pltpu.CompilerParams(vmem_limit_bytes=vmem * 1024 * 1024),
        cost_estimate=pl.CostEstimate(flops=flops, bytes_accessed=flops // 400, transcendentals=0),
    )(*[args[n] for n in turns])


def number_at(small_ref, n):
    lane = lax.broadcasted_iota(jnp.int32, (1, CHANNELS), 1)
    return jnp.sum(jnp.where(lane == n, small_ref[2:3, :], 0.0))


def front_kernel(rows, pixels_ref, cross_ref, same_ref, both_ref, *edge_refs):
    chan = lax.axis_index("chan")
    odd = lax.axis_index("space") % 2 == 1
    half, columns = CHANNELS // 2, pixels_ref.shape[1]
    size = 2 * rows * BLOCK
    source = lax.broadcasted_iota(jnp.int32, (columns, columns), 0)
    target = lax.broadcasted_iota(jnp.int32, (1, columns), 1)
    wanted = jnp.where(target < columns // 2, 2 * target, 2 * target - columns + 1)
    split = jnp.where(source == wanted, 1.0, 0.0).astype(BF16)
    placed = lax.broadcasted_iota(jnp.int32, (size, size), 1)
    line = lax.broadcasted_iota(jnp.int32, (size, 1), 0)
    second = line // (rows * BLOCK)
    frame = jnp.where(second == 0, 1 - chan, chan)
    row = line // BLOCK % rows
    origin = line % BLOCK * (2 * rows) + frame * rows + row
    turn = jnp.where(placed == origin, 1.0, 0.0).astype(BF16)
    inside = rows * half
    for n in range(half // BLOCK):
        image = pixels_ref[n * size : (n + 1) * size, :]
        image = jnp.dot(turn, image, preferred_element_type=F32).astype(BF16)
        image = jnp.dot(image, split, preferred_element_type=F32).astype(BF16)
        for f, out_ref in enumerate((cross_ref, same_ref)):
            for r in range(rows):
                first = (f * rows + r) * BLOCK
                block = image[first : first + BLOCK, :]
                first = r * half + n * BLOCK
                out_ref[first : first + BLOCK, :] = block
                both_ref[f * inside + first : f * inside + first + BLOCK, :] = block
    for f, out_ref in enumerate((cross_ref, same_ref)):
        low, high = out_ref[:half, :], out_ref[(rows - 1) * half :, :]
        for h, edge_ref in enumerate(edge_refs):
            to_low = odd if h == 0 else jnp.logical_not(odd)
            edge_ref[f * half : (f + 1) * half, :] = jnp.where(to_low, low, high)


def halo_kernel(halos, capacity, small_ref, *refs):
    halo_refs, kept_refs, (cross_ref, same_ref) = refs[:halos], refs[halos : 2 * halos], refs[2 * halos :]
    for halo_ref, kept_ref in zip(halo_refs, kept_refs):
        kept_ref[...] = halo_ref[...]
    chan = lax.axis_index("chan")
    half, columns = CHANNELS // 2, cross_ref.shape[1]
    count = SEND_ROWS
    line = lax.broadcasted_iota(jnp.int32, (ID_ROWS, CHANNELS), 0)
    lane = lax.broadcasted_iota(jnp.int32, (ID_ROWS, CHANNELS), 1)
    owners = jnp.broadcast_to(small_ref[3:4, :], (ID_ROWS, CHANNELS))
    mine = jnp.sum(jnp.where(line == lane, owners, 0.0), axis=1, keepdims=True)
    rank = jnp.sum(jnp.where((owners == mine) & (lane < line), 1.0, 0.0), axis=1, keepdims=True)
    keys = mine * float(capacity) + rank + 1.0
    place = lax.broadcasted_iota(jnp.int32, (ID_ROWS, columns), 0)
    tail = jnp.where(place < count, keys, 0.0)
    ids = [number_at(small_ref, n) for n in range(2)]
    for n, (out_ref, frame) in enumerate(((cross_ref, 1 - chan), (same_ref, chan))):
        for h in range(halos):
            out_ref[h * half : (h + 1) * half, :] = halo_refs[h][n * half : (n + 1) * half, :]
        number = jnp.where(frame == 0, ids[0], ids[1])
        out_ref[halos * half :, :] = jnp.where(place == count, number + 1.0, tail).astype(BF16)


def weights_kernel(
    ids_any, owner_any, gain_any, bias_any, out_weight_any, weight_ref, _, local_ref, late_ref, sum_ref, small_ref,
    out_matrix_ref, ids_ref, owner_ref, gain_ref, bias_ref, out_weight_ref, taps_ref, copies
):
    chan = lax.axis_index("chan")
    fetched = [
        pltpu.make_async_copy(source, target, copies.at[n])
        for n, (source, target) in enumerate(
            (
                (ids_any, ids_ref),
                (owner_any, owner_ref),
                (gain_any, gain_ref),
                (bias_any, bias_ref),
                (out_weight_any, out_weight_ref),
            )
        )
    ]
    for copy in fetched:
        copy.start()
    half = CHANNELS // 2
    own = pl.multiple_of(chan * half, half)
    other = pl.multiple_of((1 - chan) * half, half)
    for j in range(3):
        for i in range(3):
            for k in range(3):
                block = jnp.concatenate(
                    [weight_ref[k, i, j, pl.ds(own, half), :], weight_ref[k, i, j, pl.ds(other, half), :]],
                    axis=0,
                )
                taps_ref[k, i, j] = block.T
    for copy in fetched:
        copy.wait()
    small_ref[...] = jnp.zeros_like(small_ref)
    small_ref[0:1, :] = gain_ref[...]
    small_ref[1:2, :] = bias_ref[...]
    small_ref[2:3, : ids_ref.shape[1]] = ids_ref[...].astype(F32)
    small_ref[3:4, :SEND_ROWS] = owner_ref[...].astype(F32)
    for i in range(2):
        for j in range(2):
            first = (2 * i + j) * CHANNELS
            out_matrix_ref[:, first : first + CHANNELS] = out_weight_ref[i, j]
    zero = jnp.float32(0.0)
    one = jnp.float32(1.0)
    first = chan == 0
    joined = number_at(small_ref, 0) == number_at(small_ref, 1)
    flag = jnp.where(joined, one, zero)
    on_first = jnp.where(first, one, zero)
    on_second = one - on_first
    near = (
        on_first * (one - flag),
        on_first + on_second * flag,
        zero,
    )
    far = (
        on_first * flag + on_second * (one - flag),
        on_second * (one - flag),
        on_second,
    )
    late_same = (on_second * flag, zero, on_first)
    late_apart = (on_first + on_second * flag, on_first, on_first)
    for j in range(3):
        for i in range(3):
            taps = [taps_ref[k, i, j].astype(F32) for k in range(3)]

            def mixed(scale):
                return (taps[0] * scale[0] + taps[1] * scale[1] + taps[2] * scale[2]).astype(BF16)

            rows = slice(j * CHANNELS, (j + 1) * CHANNELS)
            columns = slice(i * CHANNELS, (i + 1) * CHANNELS)
            shifted = slice((3 + i) * CHANNELS, (4 + i) * CHANNELS)
            local_ref[rows, columns] = mixed(near)
            local_ref[rows, shifted] = mixed(far)
            late_ref[0, rows, columns] = mixed(late_same)
            late_ref[1, rows, columns] = mixed(late_apart)
            sum_ref[rows, columns] = mixed((one, one, one))


def image_row(sources, rows, odd, r):
    half = CHANNELS // 2
    pieces = []
    for ref, start, halos in sources:
        if 0 <= r < rows:
            pieces.append(ref[start + r * half : start + (r + 1) * half, :])
            continue
        edges = [halo_ref[first : first + half, :] for halo_ref, first in halos]
        edges.append(jnp.zeros_like(edges[0]))
        on_first = odd if r < 0 else jnp.logical_not(odd)
        pieces.append(jnp.where(on_first, edges[0], edges[1]))
    return jnp.concatenate(pieces, axis=0)


def local_sources(rows, cross_ref, same_ref, other_ref, own_halos, other_halos):
    half = CHANNELS // 2
    inside = rows * half
    near = (
        (cross_ref, 0, [(ref, 0) for ref in own_halos]),
        (other_ref, inside, [(ref, half) for ref in other_halos]),
    )
    far = (
        (same_ref, 0, [(ref, half) for ref in own_halos]),
        (other_ref, 0, [(ref, 0) for ref in other_halos]),
    )
    return near, far


def joined_columns(product):
    half = product.shape[1] // 2
    left = product[:CHANNELS, :]
    middle = product[CHANNELS : 2 * CHANNELS, :]
    right = product[2 * CHANNELS :, :]
    lane = lax.broadcasted_iota(jnp.int32, (CHANNELS, half), 1)
    from_left = jnp.where(lane == 0, 0.0, pltpu.roll(left[:, half:], 1, 1))
    from_right = jnp.where(lane == half - 1, 0.0, pltpu.roll(right[:, :half], half - 1, 1))
    even = from_left + middle[:, :half] + right[:, half:]
    odd = left[:, :half] + middle[:, half:] + from_right
    return even, odd


def group_place():
    return lax.broadcasted_iota(jnp.int32, (1, CHANNELS), 1) % (CHANNELS // GROUPS)


def group_totals(lines):
    lane = lax.broadcasted_iota(jnp.int32, lines.shape, 1)
    step = 1
    while step < CHANNELS // GROUPS:
        ahead = pltpu.roll(lines, CHANNELS - step, 1)
        behind = pltpu.roll(lines, step, 1)
        lines = lines + jnp.where(lane // step % 2 == 0, ahead, behind)
        step *= 2
    return lines


def lane_totals(first, second):
    rows = [jnp.sum(value.T, axis=0, keepdims=True) for value in (first, second)]
    return rows


def local_kernel(rows, halos, weight_ref, sum_ref, *refs):
    conv_ref, extra_ref, sums_ref, images_ref = refs[3 + 2 * halos :]
    near, far = local_sources(rows, *refs[:3], refs[3 : 3 + halos], refs[3 + halos : 3 + 2 * halos])
    odd = lax.axis_index("space") % 2 == 1
    chan = lax.axis_index("chan")
    half = conv_ref.shape[2] // 2
    for r in range(rows):
        image = jnp.concatenate(
            [image_row(frame, rows, odd, r + i) for frame in (near, far) for i in (-1, 0, 1)], axis=0
        )
        product = jnp.dot(weight_ref[...], image, preferred_element_type=F32)
        for side, value in enumerate(joined_columns(product)):
            conv_ref[r, :, side * half : (side + 1) * half] = value
    sums_ref[...] = jnp.zeros_like(sums_ref)

    @pl.when(lax.axis_index("tm") == 0)
    def _():
        rows_here = rows // 2
        for n in range(rows_here + 2):
            upper = image_row(far, rows, odd, n - 1)
            lower = image_row(near, rows, odd, rows_here + n - 1)
            images_ref[n] = jnp.where(chan == 0, upper, lower)
        totals = [jnp.zeros((CHANNELS, half), F32)] * 2
        for r in range(rows_here):
            image = jnp.concatenate([images_ref[r + i] for i in range(3)], axis=0)
            product = jnp.dot(sum_ref[...], image, preferred_element_type=F32)
            for side, value in enumerate(joined_columns(product)):
                value = value.astype(BF16)
                extra_ref[r, :, side * half : (side + 1) * half] = value
                value = value.astype(F32)
                totals = [totals[0] + value, totals[1] + value * value]
        one, two = lane_totals(*totals)
        sums_ref[0:1, :] = one
        sums_ref[1:2, :] = two


def late_kernel(rows, halos, slabs, small_ref, weight_ref, part_ref, extra_ref, sums_ref, own_edge_ref, *refs):
    near, _ = local_sources(rows, *refs[:3], refs[3 : 3 + halos], refs[3 + halos : 3 + 2 * halos])
    refs = refs[3 + 2 * halos :]
    late_own_ref, late_other_ref, own_halo_ref, other_halo_ref = refs[:4]
    conv_ref, message_ref, keys_ref, images_ref = refs[4:]
    extent = CHANNELS // 2
    arrived = (
        (late_own_ref, 0, [(own_halo_ref, h * extent) for h in range(halos)]),
        (late_other_ref, 0, [(other_halo_ref, h * extent) for h in range(halos)]),
    )
    odd = lax.axis_index("space") % 2 == 1
    slab = lax.axis_index("tm")
    first = lax.axis_index("chan") == 0
    half = part_ref.shape[2] // 2
    kept = rows // 2
    tail = halos * extent
    absent = slab == jnp.where(first, slabs - 1, 0)
    late_tail = jnp.where(absent, 0.0, own_halo_ref[tail:, :CHANNELS].astype(F32))
    own_tail = own_edge_ref[tail:, :CHANNELS].astype(F32)
    number = jnp.max(late_tail[2 * kept : 2 * kept + 1, :]) - 1.0
    ids = [number_at(small_ref, n) for n in range(2)]
    same = number == jnp.where(first, ids[1], ids[0])
    keep = jnp.where(jnp.logical_or(same, jnp.logical_not(first)), 1.0, 0.0)
    use_late = jnp.logical_or(same, first)
    choice = jnp.where(same, 0, 1)
    for r in range(-1, rows + 1):
        late = image_row(arrived, rows, odd, r)
        here = image_row(near, rows, odd, r)
        images_ref[r + 1] = jnp.where(use_late, late, here)
    totals = [jnp.zeros((CHANNELS, half), F32)] * 2
    for r in range(rows):
        image = jnp.concatenate([images_ref[r + i] for i in range(3)], axis=0)
        product = jnp.dot(weight_ref[choice], image, preferred_element_type=F32)
        for side, value in enumerate(joined_columns(product)):
            lanes = slice(side * half, (side + 1) * half)
            value = (value + keep * part_ref[r, :, lanes]).astype(BF16)
            conv_ref[r, :, lanes] = value
            value = value.astype(F32)
            totals = [totals[0] + value, totals[1] + value * value]
    one, two = lane_totals(*totals)
    main_id = jnp.where(first, number, ids[1])
    extra_id = jnp.where(slab == 0, ids[0], -1.0)
    line = lax.broadcasted_iota(jnp.int32, (8, CHANNELS), 0)
    sums = jnp.where(line == 0, one, 0.0)
    sums = jnp.where(line == 1, two, sums)
    sums = jnp.where(line == 2, sums_ref[0:1, :], sums)
    sums = jnp.where(line == 3, sums_ref[1:2, :], sums)
    sums = group_totals(sums)
    place = group_place()
    message = jnp.concatenate(
        [
            jnp.sum(jnp.where(line == jnp.broadcast_to(place, line.shape), sums, 0.0), axis=0, keepdims=True),
            jnp.where(place < 2, main_id, extra_id),
        ],
        axis=1,
    )
    message_ref[...] = jnp.broadcast_to(message, message_ref.shape)
    keys = jnp.zeros((8, CHANNELS), F32)
    for n in range(kept):
        main_key = jnp.where(first, late_tail[n : n + 1, :], own_tail[kept + n : kept + n + 1, :])
        keys = jnp.where(line == n, main_key, keys)
    quarter = kept // 2
    for n in range(quarter):
        extra_key = jnp.where(first, own_tail[n : n + 1, :], own_tail[quarter + n : quarter + n + 1, :])
        keys = jnp.where(line == kept + n, jnp.where(slab == 0, extra_key, 0.0), keys)
    keys_ref[...] = keys
    conv_ref[rows + kept, :ID_ROWS, :CHANNELS] = jnp.concatenate([keys] * 2, axis=0).astype(BF16)

    @pl.when(slab == 0)
    def _():
        conv_ref[rows : rows + kept] = extra_ref[...]


def crossed(slabs):
    return slabs in (2, 4)


def norm_kernel(
    rows, slabs, spaces, capacity, message_ref, keys_ref, gathered_ref, small_ref, out_matrix_ref, conv_ref, other_ref,
    *send_refs
):
    columns = conv_ref.shape[2]
    half = columns // 2
    kept = rows // 2
    part = MOMENTS // 2
    slab, space, chan = [lax.axis_index(name) for name in PART]
    count = float(rows * columns)
    sums, ids = gathered_ref[:, :CHANNELS], gathered_ref[:, CHANNELS:]
    place = group_place()
    beside = (slab * spaces + space) * 2 + 1 - chan
    line = lax.broadcasted_iota(jnp.int32, (gathered_ref.shape[0], 1), 0)
    numbers = [
        message_ref[0:1, CHANNELS : CHANNELS + 1],
        jnp.sum(jnp.where(line == beside, gathered_ref[:, CHANNELS : CHANNELS + 1], 0.0), axis=0, keepdims=True),
        message_ref[0:1, CHANNELS + 2 : CHANNELS + 3],
    ]
    lines = []
    for number in numbers:
        mask = ids == number
        picked = jnp.sum(jnp.where(mask, sums, 0.0), axis=0, keepdims=True)
        pixels = jnp.where(place == 0, count, jnp.where(place == 2, 0.5 * count, 0.0))
        held = jnp.sum(jnp.where(mask, pixels, 0.0), axis=0, keepdims=True)
        lines += [jnp.where(place % 2 == n, picked, 0.0) for n in range(2)] + [held]
    totals = group_totals(jnp.concatenate(lines + [jnp.zeros((7, CHANNELS), F32)], axis=0))
    matrix = out_matrix_ref[pl.ds(pl.multiple_of(chan * part, part), part), :]

    def factors(first):
        size = float(CHANNELS // GROUPS)
        counts = totals[first + 2 : first + 3, :] * size
        mean = totals[first : first + 1, :] / counts
        var = totals[first + 1 : first + 2, :] / counts - mean * mean
        scale = lax.rsqrt(var + 1e-06) * small_ref[0:1, :]
        offset = small_ref[1:2, :] - mean * scale
        return [jnp.broadcast_to(0.5 * value, (CHANNELS, CHANNELS)).T for value in (scale, offset)]

    def project(source_ref, first, lines, scale, offset):
        images = []
        for r in range(first, first + lines, 2):
            pieces = []
            for i in range(2):
                for j in range(2):
                    value = source_ref[r + i, :, j * half : (j + 1) * half].astype(F32)
                    value = value * scale + offset
                    pieces.append((value + value * jnp.tanh(value)).astype(BF16))
            images.append(jnp.concatenate(pieces, axis=0))
        image = jnp.concatenate(images, axis=1)
        return jnp.dot(matrix, image, preferred_element_type=F32)

    own_keys = keys_ref[...]
    other_keys = other_ref[rows + kept, :ID_ROWS, :CHANNELS].astype(F32)

    def blocks(latent, keys, first):
        return [
            (keys[first + n : first + n + 1, :], latent[:, n * half : (n + 1) * half])
            for n in range(latent.shape[1] // half)
        ]

    def spread(groups, started):
        for d in range(slabs):
            owner = (slab ^ d if crossed(slabs) else jnp.int32(d)).astype(F32)
            for j in range(capacity):
                wanted = owner * float(capacity) + float(j + 1)
                for first, group in groups:
                    ref = send_refs[d].at[first + j] if crossed(slabs) else send_refs[0].at[d, first + j]
                    value = ref[...].astype(F32) if started else jnp.zeros((part, half), F32)
                    for key, block in group:
                        value = jnp.where(key == wanted, block, value)
                    ref[...] = value.astype(BF16)

    mine = project(conv_ref, 0, rows, *factors(0))
    others = project(other_ref, 0, rows, *factors(3))
    second = chan == 1
    now = blocks(jnp.where(second, mine, others), jnp.where(second, own_keys, other_keys[:8, :]), 0)
    following = blocks(jnp.where(second, others, mine), jnp.where(second, other_keys[:8, :], own_keys), 0)
    spread(((0, now), (capacity, following)), False)

    @pl.when(slab == 0)
    def _():
        scale, offset = factors(6)
        begin = []
        for ref, keys in ((conv_ref, own_keys), (other_ref, other_keys)):
            begin += blocks(project(ref, rows, kept, scale, offset), keys, kept)
        spread(((0, begin),), True)


def merge_kernel(slabs, capacity, *refs):
    sources, owned_ref = refs[:-1], refs[-1]
    slab = lax.axis_index("tm")

    def source(d):
        if crossed(slabs):
            return slab ^ d, sources[d]
        return d, sources[0].at[d]

    for d in range(slabs):
        block, ref = source(d)
        for j in range(capacity):
            owned_ref[block * capacity + j] = ref[j]
    for d in range(slabs):
        block, ref = source(d)

        @pl.when(block + 1 < slabs)
        def _():
            for j in range(capacity):
                n = (block + 1) * capacity + j
                owned_ref[n] = (owned_ref[n].astype(F32) + ref[capacity + j].astype(F32)).astype(BF16)


def shards(activations, frame_clip, conv_weight, norm_gain, norm_bias, out_weight, owner):
    half, frames, rows, columns = activations.shape
    sizes = tuple(lax.axis_size(name) for name in PART)
    slabs, spaces, chans = sizes
    assert (frames, chans, half * chans) == (2, 2, CHANNELS)
    parts = slabs * spaces * chans
    halos = 1 if spaces <= 2 else 2
    send_rows = frames * (rows // 2)
    capacity = max(2, 2 * send_rows // slabs)
    kept = rows // 2
    assert send_rows == SEND_ROWS
    payload = jax.ShapeDtypeStruct((rows * half, columns), BF16)
    pair = jax.ShapeDtypeStruct((2 * half, columns), BF16)
    cross, same, both, *edges = whole_call(
        lambda *refs: front_kernel(rows, *refs),
        (payload, payload, jax.ShapeDtypeStruct((2 * rows * half, columns), BF16)) + (pair,) * halos,
        (activations.reshape(half * frames * rows, columns),),
        flops=3000000000,
    )
    own_halos = [space_swap(edge, sizes, start) for start, edge in enumerate(edges)]
    late_own = slab_swap(same, sizes, False)
    late_other = slab_swap(cross, sizes, True)
    turn = [(0, 1), (1, 0)]
    local_weight, late_weight, sum_weight, small, out_matrix = whole_call(
        weights_kernel,
        (
            jax.ShapeDtypeStruct((3 * CHANNELS, 6 * CHANNELS), BF16),
            jax.ShapeDtypeStruct((2, 3 * CHANNELS, 3 * CHANNELS), BF16),
            jax.ShapeDtypeStruct((3 * CHANNELS, 3 * CHANNELS), BF16),
            jax.ShapeDtypeStruct((8, CHANNELS), F32),
            jax.ShapeDtypeStruct((MOMENTS, 4 * CHANNELS), BF16),
        ),
        (
            frame_clip.reshape(1, frames), owner.reshape(1, send_rows), norm_gain.reshape(1, CHANNELS),
            norm_bias.reshape(1, CHANNELS), out_weight.transpose(0, 1, 3, 2), conv_weight, both,
        ),
        [
            pltpu.VMEM((1, frames), jnp.int32),
            pltpu.VMEM((1, send_rows), jnp.int32),
            pltpu.VMEM((1, CHANNELS), F32),
            pltpu.VMEM((1, CHANNELS), F32),
            pltpu.VMEM((2, 2, MOMENTS, CHANNELS), BF16),
            pltpu.VMEM((3, 3, 3, CHANNELS, CHANNELS), BF16),
            pltpu.SemaphoreType.DMA((5,)),
        ],
        [pl.BlockSpec(memory_space=pl.ANY)] * 5 + [VMEM] * 2,
        1200000000,
    )
    other = lax.ppermute(both, "chan", turn)
    message_halo = jax.ShapeDtypeStruct((halos * half + ID_ROWS, columns), BF16)
    *own_halos, cross_halo, same_halo = whole_call(
        lambda *refs: halo_kernel(halos, capacity, *refs[: 1 + halos], *refs[2 + halos :]),
        (pair,) * halos + (message_halo, message_halo),
        (small, *own_halos, other),
    )
    other_halos = [lax.ppermute(halo, "chan", turn) for halo in own_halos]
    late_own_halo = slab_swap(same_halo, sizes, False)
    late_other_halo = slab_swap(cross_halo, sizes, True)
    here = (cross, same, other, *own_halos, *other_halos)
    part, extra, extra_sums = whole_call(
        lambda *refs: local_kernel(rows, halos, *refs),
        (
            jax.ShapeDtypeStruct((rows, CHANNELS, columns), F32),
            jax.ShapeDtypeStruct((rows // 2, CHANNELS, columns), BF16),
            jax.ShapeDtypeStruct((8, CHANNELS), F32),
        ),
        (local_weight, sum_weight, *here),
        [pltpu.VMEM((rows // 2 + 2, CHANNELS, columns), BF16)],
        flops=1800000000,
    )
    conv, message, keys = whole_call(
        lambda *refs: late_kernel(rows, halos, slabs, *refs),
        (
            jax.ShapeDtypeStruct((rows + kept + 1, CHANNELS, columns), BF16),
            jax.ShapeDtypeStruct((parts, 2 * CHANNELS), F32),
            jax.ShapeDtypeStruct((8, CHANNELS), F32),
        ),
        (
            small, late_weight, part, extra, extra_sums, cross_halo, *here, late_own, late_other, late_own_halo, late_other_halo,
        ),
        [pltpu.VMEM((rows + 2, CHANNELS, columns), BF16)],
        flops=1500000000,
    )
    conv_other = lax.ppermute(conv, "chan", turn)
    gathered = lax.all_to_all(message, PART, split_axis=0, concat_axis=0, tiled=True)
    part = MOMENTS // chans
    width = columns // 2
    blocks = (2 * capacity, part, width)
    if crossed(slabs):
        shapes = (jax.ShapeDtypeStruct(blocks, BF16),) * slabs
    else:
        shapes = (jax.ShapeDtypeStruct((slabs,) + blocks, BF16),)
    sends = whole_call(
        lambda *refs: norm_kernel(rows, slabs, spaces, capacity, *refs),
        shapes,
        (message, keys, gathered, small, out_matrix, conv, conv_other),
    )
    if crossed(slabs):
        received = [sends[0]]
        for d in range(1, slabs):
            received.append(lax.ppermute(sends[d], "tm", [(t, t ^ d) for t in range(slabs)]))
    else:
        received = [lax.all_to_all(sends[0], "tm", split_axis=0, concat_axis=0, tiled=True)]
    turns = list((0, 3, 1, 2)) if crossed(slabs) else [0]
    owned = pl.pallas_call(
        lambda *refs: merge_kernel(slabs, capacity, *[refs[turns.index(d)] for d in range(len(turns))], refs[-1]),
        out_shape=jax.ShapeDtypeStruct((slabs * capacity, part, width), BF16),
        in_specs=[VMEM] * len(received),
        out_specs=pl.BlockSpec((slabs * capacity, part, width), lambda: (0, 0, 0)),
        compiler_params=PARAMS,
    )(*[received[d] for d in turns])
    return owned[None]


def solution(mesh):
    placed = (
        P(("groups", "chan"), "tm", "space", None),
        P(("groups", "tm")),
        P(),
        P(),
        P(),
        P(),
        P(("groups", "space"), "tm", None),
    )
    return jax.shard_map(
        shards,
        mesh=mesh,
        in_specs=placed,
        out_specs=P(("groups", "space"), "tm", "chan", None),
        check_vma=False,
    )
```

```python
import jax
import jax.numpy as jnp
import numpy as np
from jax import lax
from jax.experimental import pallas as pl
from jax.experimental.pallas import tpu as pltpu
from jax.sharding import PartitionSpec as P

CHANNELS = 128
GROUPS = 32
MOMENTS = 32
SEND_ROWS = 8
ID_ROWS = 16
BLOCK = 16
BF16 = jnp.bfloat16
F32 = jnp.float32
VMEM = pl.BlockSpec(memory_space=pltpu.VMEM)
PARAMS = pltpu.CompilerParams(vmem_limit_bytes=40 * 1024 * 1024)
PART = ("tm", "space", "chan")


def flat_pairs(sizes, pairs):
    _, spaces, chans = sizes
    return [
        ((a[0] * spaces + a[1]) * chans + a[2], (b[0] * spaces + b[1]) * chans + b[2])
        for a, b in pairs
    ]


def space_swap(value, sizes, start):
    slabs, spaces, chans = sizes
    pairs = []
    for low in range(start, spaces - 1, 2):
        for t in range(slabs):
            for c in range(chans):
                pairs += [((t, low, c), (t, low + 1, c)), ((t, low + 1, c), (t, low, c))]
    return lax.ppermute(value, PART, flat_pairs(sizes, pairs))


def slab_swap(value, sizes, cross):
    slabs, spaces, _ = sizes
    last = slabs - 1
    pairs = []
    for s in range(spaces):
        for t in range(last):
            if cross:
                pairs += [((t, s, 0), (t + 1, s, 1)), ((t + 1, s, 1), (t, s, 0))]
            else:
                pairs += [((t, s, 1), (t + 1, s, 1)), ((t + 1, s, 0), (t, s, 0))]
        if spaces % 2 == 0 and cross:
            pairs += [((0, s, 1), (0, s ^ 1, 1)), ((last, s, 0), (last, s ^ 1, 0))]
        elif spaces % 2 == 0:
            pairs += [((last, s, 1), (last, s, 0)), ((0, s, 0), (0, s, 1))]
    return lax.ppermute(value, PART, flat_pairs(sizes, pairs))


def whole_call(kernel, out_shape, args, scratch=(), specs=None, flops=0, vmem=40, first=()):
    turns = list(first) + [n for n in range(len(args)) if n not in first]
    specs = specs or [VMEM] * len(args)

    def turned(*refs):
        kernel(*[refs[turns.index(n)] for n in range(len(args))], *refs[len(args) :])

    return pl.pallas_call(
        turned,
        out_shape=out_shape,
        in_specs=[specs[n] for n in turns],
        out_specs=jax.tree.map(lambda _: VMEM, out_shape),
        scratch_shapes=scratch,
        compiler_params=pltpu.CompilerParams(vmem_limit_bytes=vmem * 1024 * 1024),
        cost_estimate=pl.CostEstimate(flops=flops, bytes_accessed=flops // 400, transcendentals=0),
    )(*[args[n] for n in turns])


def number_at(small_ref, n):
    lane = lax.broadcasted_iota(jnp.int32, (1, CHANNELS), 1)
    return jnp.sum(jnp.where(lane == n, small_ref[2:3, :], 0.0))


def front_kernel(rows, pixels_ref, cross_ref, same_ref, both_ref, *edge_refs):
    chan = lax.axis_index("chan")
    odd = lax.axis_index("space") % 2 == 1
    half, columns = CHANNELS // 2, pixels_ref.shape[1]
    size = 2 * rows * BLOCK
    source = lax.broadcasted_iota(jnp.int32, (columns, columns), 0)
    target = lax.broadcasted_iota(jnp.int32, (1, columns), 1)
    wanted = jnp.where(target < columns // 2, 2 * target, 2 * target - columns + 1)
    split = jnp.where(source == wanted, 1.0, 0.0).astype(BF16)
    placed = lax.broadcasted_iota(jnp.int32, (size, size), 1)
    line = lax.broadcasted_iota(jnp.int32, (size, 1), 0)
    second = line // (rows * BLOCK)
    frame = jnp.where(second == 0, 1 - chan, chan)
    row = line // BLOCK % rows
    origin = line % BLOCK * (2 * rows) + frame * rows + row
    turn = jnp.where(placed == origin, 1.0, 0.0).astype(BF16)
    inside = rows * half
    for n in range(half // BLOCK):
        image = pixels_ref[n * size : (n + 1) * size, :]
        image = jnp.dot(turn, image, preferred_element_type=F32).astype(BF16)
        image = jnp.dot(image, split, preferred_element_type=F32).astype(BF16)
        for f, out_ref in enumerate((cross_ref, same_ref)):
            for r in range(rows):
                first = (f * rows + r) * BLOCK
                block = image[first : first + BLOCK, :]
                first = r * half + n * BLOCK
                out_ref[first : first + BLOCK, :] = block
                both_ref[f * inside + first : f * inside + first + BLOCK, :] = block
    for f, out_ref in enumerate((cross_ref, same_ref)):
        low, high = out_ref[:half, :], out_ref[(rows - 1) * half :, :]
        for h, edge_ref in enumerate(edge_refs):
            to_low = odd if h == 0 else jnp.logical_not(odd)
            edge_ref[f * half : (f + 1) * half, :] = jnp.where(to_low, low, high)


def halo_kernel(halos, capacity, small_ref, *refs):
    halo_refs, kept_refs, (cross_ref, same_ref) = refs[:halos], refs[halos : 2 * halos], refs[2 * halos :]
    for halo_ref, kept_ref in zip(halo_refs, kept_refs):
        kept_ref[...] = halo_ref[...]
    chan = lax.axis_index("chan")
    half, columns = CHANNELS // 2, cross_ref.shape[1]
    count = SEND_ROWS
    line = lax.broadcasted_iota(jnp.int32, (ID_ROWS, CHANNELS), 0)
    lane = lax.broadcasted_iota(jnp.int32, (ID_ROWS, CHANNELS), 1)
    owners = jnp.broadcast_to(small_ref[3:4, :], (ID_ROWS, CHANNELS))
    mine = jnp.sum(jnp.where(line == lane, owners, 0.0), axis=1, keepdims=True)
    rank = jnp.sum(jnp.where((owners == mine) & (lane < line), 1.0, 0.0), axis=1, keepdims=True)
    keys = mine * float(capacity) + rank + 1.0
    place = lax.broadcasted_iota(jnp.int32, (ID_ROWS, columns), 0)
    tail = jnp.where(place < count, keys, 0.0)
    ids = [number_at(small_ref, n) for n in range(2)]
    for n, (out_ref, frame) in enumerate(((cross_ref, 1 - chan), (same_ref, chan))):
        for h in range(halos):
            out_ref[h * half : (h + 1) * half, :] = halo_refs[h][n * half : (n + 1) * half, :]
        number = jnp.where(frame == 0, ids[0], ids[1])
        if n == 1:
            out_ref[halos * half :, :] = jnp.where(place == count, number + 1.0, tail).astype(BF16)


def weights_kernel(
    ids_any, owner_any, gain_any, bias_any, out_weight_any, weight_ref, _, local_ref, late_ref, sum_ref, small_ref,
    out_matrix_ref, ids_ref, owner_ref, gain_ref, bias_ref, out_weight_ref, taps_ref, copies
):
    chan = lax.axis_index("chan")
    fetched = [
        pltpu.make_async_copy(source, target, copies.at[n])
        for n, (source, target) in enumerate(
            (
                (ids_any, ids_ref),
                (owner_any, owner_ref),
                (gain_any, gain_ref),
                (bias_any, bias_ref),
                (out_weight_any, out_weight_ref),
            )
        )
    ]
    for copy in fetched:
        copy.start()
    half = CHANNELS // 2
    own = pl.multiple_of(chan * half, half)
    other = pl.multiple_of((1 - chan) * half, half)
    for j in range(3):
        for i in range(3):
            for k in range(3):
                block = jnp.concatenate(
                    [weight_ref[k, i, j, pl.ds(own, half), :], weight_ref[k, i, j, pl.ds(other, half), :]],
                    axis=0,
                )
                taps_ref[k, i, j] = block.T
    for copy in fetched:
        copy.wait()
    small_ref[...] = jnp.zeros_like(small_ref)
    small_ref[0:1, :] = gain_ref[...]
    small_ref[1:2, :] = bias_ref[...]
    small_ref[2:3, : ids_ref.shape[1]] = ids_ref[...].astype(F32)
    small_ref[3:4, :SEND_ROWS] = owner_ref[...].astype(F32)
    for i in range(2):
        for j in range(2):
            first = (2 * i + j) * CHANNELS
            out_matrix_ref[:, first : first + CHANNELS] = out_weight_ref[i, j]
    zero = jnp.float32(0.0)
    one = jnp.float32(1.0)
    first = chan == 0
    joined = number_at(small_ref, 0) == number_at(small_ref, 1)
    flag = jnp.where(joined, one, zero)
    on_first = jnp.where(first, one, zero)
    on_second = one - on_first
    near = (
        on_first * (one - flag),
        on_first + on_second * flag,
        zero,
    )
    far = (
        on_first * flag + on_second * (one - flag),
        on_second * (one - flag),
        on_second,
    )
    late_same = (on_second * flag, zero, on_first)
    late_apart = (on_first + on_second * flag, on_first, on_first)
    for j in range(3):
        for i in range(3):
            taps = [taps_ref[k, i, j].astype(F32) for k in range(3)]

            def mixed(scale):
                return (taps[0] * scale[0] + taps[1] * scale[1] + taps[2] * scale[2]).astype(BF16)

            rows = slice(j * CHANNELS, (j + 1) * CHANNELS)
            columns = slice(i * CHANNELS, (i + 1) * CHANNELS)
            shifted = slice((3 + i) * CHANNELS, (4 + i) * CHANNELS)
            local_ref[rows, columns] = mixed(near)
            local_ref[rows, shifted] = mixed(far)
            late_ref[0, rows, columns] = mixed(late_same)
            late_ref[1, rows, columns] = mixed(late_apart)
            sum_ref[rows, columns] = mixed((one, one, one))


def image_row(sources, rows, odd, r):
    half = CHANNELS // 2
    pieces = []
    for ref, start, halos in sources:
        if 0 <= r < rows:
            pieces.append(ref[start + r * half : start + (r + 1) * half, :])
            continue
        edges = [halo_ref[first : first + half, :] for halo_ref, first in halos]
        edges.append(jnp.zeros_like(edges[0]))
        on_first = odd if r < 0 else jnp.logical_not(odd)
        pieces.append(jnp.where(on_first, edges[0], edges[1]))
    return jnp.concatenate(pieces, axis=0)


def local_sources(rows, cross_ref, same_ref, other_ref, own_halos, other_halos):
    half = CHANNELS // 2
    inside = rows * half
    near = (
        (cross_ref, 0, [(ref, 0) for ref in own_halos]),
        (other_ref, inside, [(ref, half) for ref in other_halos]),
    )
    far = (
        (same_ref, 0, [(ref, half) for ref in own_halos]),
        (other_ref, 0, [(ref, 0) for ref in other_halos]),
    )
    return near, far


def joined_columns(product):
    half = product.shape[1] // 2
    left = product[:CHANNELS, :]
    middle = product[CHANNELS : 2 * CHANNELS, :]
    right = product[2 * CHANNELS :, :]
    lane = lax.broadcasted_iota(jnp.int32, (CHANNELS, half), 1)
    from_left = jnp.where(lane == 0, 0.0, pltpu.roll(left[:, half:], 1, 1))
    from_right = jnp.where(lane == half - 1, 0.0, pltpu.roll(right[:, :half], half - 1, 1))
    even = from_left + middle[:, :half] + right[:, half:]
    odd = left[:, :half] + middle[:, half:] + from_right
    return even, odd


def group_place():
    return lax.broadcasted_iota(jnp.int32, (1, CHANNELS), 1) % (CHANNELS // GROUPS)


def group_totals(lines):
    lane = lax.broadcasted_iota(jnp.int32, lines.shape, 1)
    step = 1
    while step < CHANNELS // GROUPS:
        ahead = pltpu.roll(lines, CHANNELS - step, 1)
        behind = pltpu.roll(lines, step, 1)
        lines = lines + jnp.where(lane // step % 2 == 0, ahead, behind)
        step *= 2
    return lines


def lane_totals(first, second):
    rows = [jnp.sum(value.T, axis=0, keepdims=True) for value in (first, second)]
    return rows


def local_kernel(rows, halos, weight_ref, sum_ref, *refs):
    conv_ref, extra_ref, sums_ref, images_ref = refs[3 + 2 * halos :]
    near, far = local_sources(rows, *refs[:3], refs[3 : 3 + halos], refs[3 + halos : 3 + 2 * halos])
    odd = lax.axis_index("space") % 2 == 1
    chan = lax.axis_index("chan")
    half = conv_ref.shape[2] // 2
    for r in range(rows):
        image = jnp.concatenate(
            [image_row(frame, rows, odd, r + i) for frame in (near, far) for i in (-1, 0, 1)], axis=0
        )
        product = jnp.dot(weight_ref[...], image, preferred_element_type=F32)
        for side, value in enumerate(joined_columns(product)):
            conv_ref[r, :, side * half : (side + 1) * half] = value
    sums_ref[...] = jnp.zeros_like(sums_ref)

    @pl.when(lax.axis_index("tm") == 0)
    def _():
        rows_here = rows // 2
        for n in range(rows_here + 2):
            upper = image_row(far, rows, odd, n - 1)
            lower = image_row(near, rows, odd, rows_here + n - 1)
            images_ref[n] = jnp.where(chan == 0, upper, lower)
        totals = [jnp.zeros((CHANNELS, half), F32)] * 2
        for r in range(rows_here):
            image = jnp.concatenate([images_ref[r + i] for i in range(3)], axis=0)
            product = jnp.dot(sum_ref[...], image, preferred_element_type=F32)
            for side, value in enumerate(joined_columns(product)):
                value = value.astype(BF16)
                extra_ref[r, :, side * half : (side + 1) * half] = value
                value = value.astype(F32)
                totals = [totals[0] + value, totals[1] + value * value]
        one, two = lane_totals(*totals)
        sums_ref[0:1, :] = one
        sums_ref[1:2, :] = two


def late_kernel(rows, halos, slabs, small_ref, weight_ref, part_ref, extra_ref, sums_ref, own_edge_ref, *refs):
    near, _ = local_sources(rows, *refs[:3], refs[3 : 3 + halos], refs[3 + halos : 3 + 2 * halos])
    refs = refs[3 + 2 * halos :]
    late_own_ref, late_other_ref, own_halo_ref, other_halo_ref = refs[:4]
    conv_ref, message_ref, keys_ref, images_ref = refs[4:]
    extent = CHANNELS // 2
    arrived = (
        (late_own_ref, 0, [(own_halo_ref, h * extent) for h in range(halos)]),
        (late_other_ref, 0, [(other_halo_ref, h * extent) for h in range(halos)]),
    )
    odd = lax.axis_index("space") % 2 == 1
    slab = lax.axis_index("tm")
    first = lax.axis_index("chan") == 0
    half = part_ref.shape[2] // 2
    kept = rows // 2
    tail = halos * extent
    absent = slab == jnp.where(first, slabs - 1, 0)
    late_tail = jnp.where(absent, 0.0, own_halo_ref[tail:, :CHANNELS].astype(F32))
    own_tail = own_edge_ref[tail:, :CHANNELS].astype(F32)
    number = jnp.max(late_tail[2 * kept : 2 * kept + 1, :]) - 1.0
    ids = [number_at(small_ref, n) for n in range(2)]
    same = number == jnp.where(first, ids[1], ids[0])
    keep = jnp.where(jnp.logical_or(same, jnp.logical_not(first)), 1.0, 0.0)
    use_late = jnp.logical_or(same, first)
    choice = jnp.where(same, 0, 1)
    for r in range(-1, rows + 1):
        late = image_row(arrived, rows, odd, r)
        here = image_row(near, rows, odd, r)
        images_ref[r + 1] = jnp.where(use_late, late, here)
    totals = [jnp.zeros((CHANNELS, half), F32)] * 2
    for r in range(rows):
        image = jnp.concatenate([images_ref[r + i] for i in range(3)], axis=0)
        product = jnp.dot(weight_ref[choice], image, preferred_element_type=F32)
        for side, value in enumerate(joined_columns(product)):
            lanes = slice(side * half, (side + 1) * half)
            value = (value + keep * part_ref[r, :, lanes]).astype(BF16)
            conv_ref[r, :, lanes] = value
            value = value.astype(F32)
            totals = [totals[0] + value, totals[1] + value * value]
    one, two = lane_totals(*totals)
    main_id = jnp.where(first, number, ids[1])
    extra_id = jnp.where(slab == 0, ids[0], -1.0)
    line = lax.broadcasted_iota(jnp.int32, (8, CHANNELS), 0)
    sums = jnp.where(line == 0, one, 0.0)
    sums = jnp.where(line == 1, two, sums)
    sums = jnp.where(line == 2, sums_ref[0:1, :], sums)
    sums = jnp.where(line == 3, sums_ref[1:2, :], sums)
    sums = group_totals(sums)
    place = group_place()
    message = jnp.concatenate(
        [
            jnp.sum(jnp.where(line == jnp.broadcast_to(place, line.shape), sums, 0.0), axis=0, keepdims=True),
            jnp.where(place < 2, main_id, extra_id),
        ],
        axis=1,
    )
    message_ref[...] = jnp.broadcast_to(message, message_ref.shape)
    keys = jnp.zeros((8, CHANNELS), F32)
    for n in range(kept):
        main_key = jnp.where(first, late_tail[n : n + 1, :], own_tail[kept + n : kept + n + 1, :])
        keys = jnp.where(line == n, main_key, keys)
    quarter = kept // 2
    for n in range(quarter):
        extra_key = jnp.where(first, own_tail[n : n + 1, :], own_tail[quarter + n : quarter + n + 1, :])
        keys = jnp.where(line == kept + n, jnp.where(slab == 0, extra_key, 0.0), keys)
    keys_ref[...] = keys
    conv_ref[rows + kept, :ID_ROWS, :CHANNELS] = jnp.concatenate([keys] * 2, axis=0).astype(BF16)

    @pl.when(slab == 0)
    def _():
        conv_ref[rows : rows + kept] = extra_ref[...]


def crossed(slabs):
    return slabs in (2, 4)


def norm_kernel(
    rows, slabs, spaces, capacity, message_ref, keys_ref, gathered_ref, small_ref, out_matrix_ref, conv_ref, other_ref,
    *send_refs
):
    columns = conv_ref.shape[2]
    half = columns // 2
    kept = rows // 2
    part = MOMENTS // 2
    slab, space, chan = [lax.axis_index(name) for name in PART]
    count = float(rows * columns)
    sums, ids = gathered_ref[:, :CHANNELS], gathered_ref[:, CHANNELS:]
    place = group_place()
    beside = (slab * spaces + space) * 2 + 1 - chan
    line = lax.broadcasted_iota(jnp.int32, (gathered_ref.shape[0], 1), 0)
    numbers = [
        message_ref[0:1, CHANNELS : CHANNELS + 1],
        jnp.sum(jnp.where(line == beside, gathered_ref[:, CHANNELS : CHANNELS + 1], 0.0), axis=0, keepdims=True),
        message_ref[0:1, CHANNELS + 2 : CHANNELS + 3],
    ]
    lines = []
    for number in numbers:
        mask = ids == number
        picked = jnp.sum(jnp.where(mask, sums, 0.0), axis=0, keepdims=True)
        pixels = jnp.where(place == 0, count, jnp.where(place == 2, 0.5 * count, 0.0))
        held = jnp.sum(jnp.where(mask, pixels, 0.0), axis=0, keepdims=True)
        lines += [jnp.where(place % 2 == n, picked, 0.0) for n in range(2)] + [held]
    totals = group_totals(jnp.concatenate(lines + [jnp.zeros((7, CHANNELS), F32)], axis=0))
    matrix = out_matrix_ref[pl.ds(pl.multiple_of(chan * part, part), part), :]

    def factors(first):
        size = float(CHANNELS // GROUPS)
        counts = totals[first + 2 : first + 3, :] * size
        mean = totals[first : first + 1, :] / counts
        var = totals[first + 1 : first + 2, :] / counts - mean * mean
        scale = lax.rsqrt(var + 1e-06) * small_ref[0:1, :]
        offset = small_ref[1:2, :] - mean * scale
        return [jnp.broadcast_to(0.5 * value, (CHANNELS, CHANNELS)).T for value in (scale, offset)]

    def project(source_ref, first, lines, scale, offset):
        images = []
        for r in range(first, first + lines, 2):
            pieces = []
            for i in range(2):
                for j in range(2):
                    value = source_ref[r + i, :, j * half : (j + 1) * half].astype(F32)
                    value = value * scale + offset
                    pieces.append((value + value * jnp.tanh(value)).astype(BF16))
            images.append(jnp.concatenate(pieces, axis=0))
        image = jnp.concatenate(images, axis=1)
        return jnp.dot(matrix, image, preferred_element_type=F32)

    own_keys = keys_ref[...]
    other_keys = other_ref[rows + kept, :ID_ROWS, :CHANNELS].astype(F32)

    def blocks(latent, keys, first):
        return [
            (keys[first + n : first + n + 1, :], latent[:, n * half : (n + 1) * half])
            for n in range(latent.shape[1] // half)
        ]

    def spread(groups, started):
        for d in range(slabs):
            owner = (slab ^ d if crossed(slabs) else jnp.int32(d)).astype(F32)
            for j in range(capacity):
                wanted = owner * float(capacity) + float(j + 1)
                for first, group in groups:
                    ref = send_refs[d].at[first + j] if crossed(slabs) else send_refs[0].at[d, first + j]
                    value = ref[...].astype(F32) if started else jnp.zeros((part, half), F32)
                    for key, block in group:
                        value = jnp.where(key == wanted, block, value)
                    ref[...] = value.astype(BF16)

    mine = project(conv_ref, 0, rows, *factors(0))
    others = project(other_ref, 0, rows, *factors(3))
    second = chan == 1
    now = blocks(jnp.where(second, mine, others), jnp.where(second, own_keys, other_keys[:8, :]), 0)
    following = blocks(jnp.where(second, others, mine), jnp.where(second, other_keys[:8, :], own_keys), 0)
    spread(((0, now), (capacity, following)), False)

    @pl.when(slab == 0)
    def _():
        scale, offset = factors(6)
        begin = []
        for ref, keys in ((conv_ref, own_keys), (other_ref, other_keys)):
            begin += blocks(project(ref, rows, kept, scale, offset), keys, kept)
        spread(((0, begin),), True)


def merge_kernel(slabs, capacity, *refs):
    sources, owned_ref = refs[:-1], refs[-1]
    slab = lax.axis_index("tm")

    def source(d):
        if crossed(slabs):
            return slab ^ d, sources[d]
        return d, sources[0].at[d]

    for d in range(slabs):
        block, ref = source(d)
        for j in range(capacity):
            owned_ref[block * capacity + j] = ref[j]
    for d in range(slabs):
        block, ref = source(d)

        @pl.when(block + 1 < slabs)
        def _():
            for j in range(capacity):
                n = (block + 1) * capacity + j
                owned_ref[n] = (owned_ref[n].astype(F32) + ref[capacity + j].astype(F32)).astype(BF16)


def shards(activations, frame_clip, conv_weight, norm_gain, norm_bias, out_weight, owner):
    half, frames, rows, columns = activations.shape
    sizes = tuple(lax.axis_size(name) for name in PART)
    slabs, spaces, chans = sizes
    assert (frames, chans, half * chans) == (2, 2, CHANNELS)
    parts = slabs * spaces * chans
    halos = 1 if spaces <= 2 else 2
    send_rows = frames * (rows // 2)
    capacity = max(2, 2 * send_rows // slabs)
    kept = rows // 2
    assert send_rows == SEND_ROWS
    payload = jax.ShapeDtypeStruct((rows * half, columns), BF16)
    pair = jax.ShapeDtypeStruct((2 * half, columns), BF16)
    cross, same, both, *edges = whole_call(
        lambda *refs: front_kernel(rows, *refs),
        (payload, payload, jax.ShapeDtypeStruct((2 * rows * half, columns), BF16)) + (pair,) * halos,
        (activations.reshape(half * frames * rows, columns),),
        flops=3000000000,
    )
    own_halos = [space_swap(edge, sizes, start) for start, edge in enumerate(edges)]
    late_own = slab_swap(same, sizes, False)
    late_other = slab_swap(cross, sizes, True)
    turn = [(0, 1), (1, 0)]
    local_weight, late_weight, sum_weight, small, out_matrix = whole_call(
        weights_kernel,
        (
            jax.ShapeDtypeStruct((3 * CHANNELS, 6 * CHANNELS), BF16),
            jax.ShapeDtypeStruct((2, 3 * CHANNELS, 3 * CHANNELS), BF16),
            jax.ShapeDtypeStruct((3 * CHANNELS, 3 * CHANNELS), BF16),
            jax.ShapeDtypeStruct((8, CHANNELS), F32),
            jax.ShapeDtypeStruct((MOMENTS, 4 * CHANNELS), BF16),
        ),
        (
            frame_clip.reshape(1, frames), owner.reshape(1, send_rows), norm_gain.reshape(1, CHANNELS),
            norm_bias.reshape(1, CHANNELS), out_weight.transpose(0, 1, 3, 2), conv_weight, both,
        ),
        [
            pltpu.VMEM((1, frames), jnp.int32),
            pltpu.VMEM((1, send_rows), jnp.int32),
            pltpu.VMEM((1, CHANNELS), F32),
            pltpu.VMEM((1, CHANNELS), F32),
            pltpu.VMEM((2, 2, MOMENTS, CHANNELS), BF16),
            pltpu.VMEM((3, 3, 3, CHANNELS, CHANNELS), BF16),
            pltpu.SemaphoreType.DMA((5,)),
        ],
        [pl.BlockSpec(memory_space=pl.ANY)] * 5 + [VMEM] * 2,
        1200000000,
    )
    other = lax.ppermute(both, "chan", turn)
    message_halo = jax.ShapeDtypeStruct((halos * half + ID_ROWS, columns), BF16)
    *own_halos, cross_halo, same_halo = whole_call(
        lambda *refs: halo_kernel(halos, capacity, *refs[: 1 + halos], *refs[2 + halos :]),
        (pair,) * halos + (jax.ShapeDtypeStruct((halos * half, columns), BF16), message_halo),
        (small, *own_halos, other),
    )
    other_halos = [lax.ppermute(halo, "chan", turn) for halo in own_halos]
    late_own_halo = slab_swap(same_halo, sizes, False)
    late_other_halo = slab_swap(cross_halo, sizes, True)
    here = (cross, same, other, *own_halos, *other_halos)
    part, extra, extra_sums = whole_call(
        lambda *refs: local_kernel(rows, halos, *refs),
        (
            jax.ShapeDtypeStruct((rows, CHANNELS, columns), F32),
            jax.ShapeDtypeStruct((rows // 2, CHANNELS, columns), BF16),
            jax.ShapeDtypeStruct((8, CHANNELS), F32),
        ),
        (local_weight, sum_weight, *here),
        [pltpu.VMEM((rows // 2 + 2, CHANNELS, columns), BF16)],
        flops=1800000000,
    )
    conv, message, keys = whole_call(
        lambda *refs: late_kernel(rows, halos, slabs, *refs),
        (
            jax.ShapeDtypeStruct((rows + kept + 1, CHANNELS, columns), BF16),
            jax.ShapeDtypeStruct((parts, 2 * CHANNELS), F32),
            jax.ShapeDtypeStruct((8, CHANNELS), F32),
        ),
        (
            small, late_weight, part, extra, extra_sums, same_halo, *here, late_own, late_other, late_own_halo, late_other_halo,
        ),
        [pltpu.VMEM((rows + 2, CHANNELS, columns), BF16)],
        flops=1500000000,
    )
    conv_other = lax.ppermute(conv, "chan", turn)
    gathered = lax.all_to_all(message, PART, split_axis=0, concat_axis=0, tiled=True)
    part = MOMENTS // chans
    width = columns // 2
    blocks = (2 * capacity, part, width)
    if crossed(slabs):
        shapes = (jax.ShapeDtypeStruct(blocks, BF16),) * slabs
    else:
        shapes = (jax.ShapeDtypeStruct((slabs,) + blocks, BF16),)
    sends = whole_call(
        lambda *refs: norm_kernel(rows, slabs, spaces, capacity, *refs),
        shapes,
        (message, keys, gathered, small, out_matrix, conv, conv_other),
    )
    if crossed(slabs):
        received = [sends[0]]
        for d in range(1, slabs):
            received.append(lax.ppermute(sends[d], "tm", [(t, t ^ d) for t in range(slabs)]))
    else:
        received = [lax.all_to_all(sends[0], "tm", split_axis=0, concat_axis=0, tiled=True)]
    turns = list((0, 3, 1, 2)) if crossed(slabs) else [0]
    owned = pl.pallas_call(
        lambda *refs: merge_kernel(slabs, capacity, *[refs[turns.index(d)] for d in range(len(turns))], refs[-1]),
        out_shape=jax.ShapeDtypeStruct((slabs * capacity, part, width), BF16),
        in_specs=[VMEM] * len(received),
        out_specs=pl.BlockSpec((slabs * capacity, part, width), lambda: (0, 0, 0)),
        compiler_params=PARAMS,
    )(*[received[d] for d in turns])
    return owned[None]


def solution(mesh):
    placed = (
        P(("groups", "chan"), "tm", "space", None),
        P(("groups", "tm")),
        P(),
        P(),
        P(),
        P(),
        P(("groups", "space"), "tm", None),
    )
    return jax.shard_map(
        shards,
        mesh=mesh,
        in_specs=placed,
        out_specs=P(("groups", "space"), "tm", "chan", None),
        check_vma=False,
    )
```

```python
import jax
import jax.numpy as jnp
import numpy as np
from jax import lax
from jax.experimental import pallas as pl
from jax.experimental.pallas import tpu as pltpu
from jax.sharding import PartitionSpec as P

CHANNELS = 128
GROUPS = 32
MOMENTS = 32
SEND_ROWS = 8
ID_ROWS = 16
BLOCK = 16
BF16 = jnp.bfloat16
F32 = jnp.float32
VMEM = pl.BlockSpec(memory_space=pltpu.VMEM)
PARAMS = pltpu.CompilerParams(vmem_limit_bytes=40 * 1024 * 1024)
PART = ("tm", "space", "chan")


def flat_pairs(sizes, pairs):
    _, spaces, chans = sizes
    return [
        ((a[0] * spaces + a[1]) * chans + a[2], (b[0] * spaces + b[1]) * chans + b[2])
        for a, b in pairs
    ]


def space_swap(value, sizes, start):
    slabs, spaces, chans = sizes
    pairs = []
    for low in range(start, spaces - 1, 2):
        for t in range(slabs):
            for c in range(chans):
                pairs += [((t, low, c), (t, low + 1, c)), ((t, low + 1, c), (t, low, c))]
    return lax.ppermute(value, PART, flat_pairs(sizes, pairs))


def slab_swap(value, sizes, cross):
    slabs, spaces, _ = sizes
    last = slabs - 1
    pairs = []
    for s in range(spaces):
        for t in range(last):
            if cross:
                pairs += [((t, s, 0), (t + 1, s, 1)), ((t + 1, s, 1), (t, s, 0))]
            else:
                pairs += [((t, s, 1), (t + 1, s, 1)), ((t + 1, s, 0), (t, s, 0))]
        if spaces % 2 == 0 and cross:
            pairs += [((0, s, 1), (0, s ^ 1, 1)), ((last, s, 0), (last, s ^ 1, 0))]
        elif spaces % 2 == 0:
            pairs += [((last, s, 1), (last, s, 0)), ((0, s, 0), (0, s, 1))]
    return lax.ppermute(value, PART, flat_pairs(sizes, pairs))


def whole_call(kernel, out_shape, args, scratch=(), specs=None, flops=0, vmem=40, first=()):
    turns = list(first) + [n for n in range(len(args)) if n not in first]
    specs = specs or [VMEM] * len(args)

    def turned(*refs):
        kernel(*[refs[turns.index(n)] for n in range(len(args))], *refs[len(args) :])

    return pl.pallas_call(
        turned,
        out_shape=out_shape,
        in_specs=[specs[n] for n in turns],
        out_specs=jax.tree.map(lambda _: VMEM, out_shape),
        scratch_shapes=scratch,
        compiler_params=pltpu.CompilerParams(vmem_limit_bytes=vmem * 1024 * 1024),
        cost_estimate=pl.CostEstimate(flops=flops, bytes_accessed=flops // 400, transcendentals=0),
    )(*[args[n] for n in turns])


def number_at(small_ref, n):
    lane = lax.broadcasted_iota(jnp.int32, (1, CHANNELS), 1)
    return jnp.sum(jnp.where(lane == n, small_ref[2:3, :], 0.0))


def front_kernel(rows, pixels_ref, cross_ref, same_ref, both_ref, *edge_refs):
    chan = lax.axis_index("chan")
    odd = lax.axis_index("space") % 2 == 1
    half, columns = CHANNELS // 2, pixels_ref.shape[1]
    size = 2 * rows * BLOCK
    source = lax.broadcasted_iota(jnp.int32, (columns, columns), 0)
    target = lax.broadcasted_iota(jnp.int32, (1, columns), 1)
    wanted = jnp.where(target < columns // 2, 2 * target, 2 * target - columns + 1)
    split = jnp.where(source == wanted, 1.0, 0.0).astype(BF16)
    placed = lax.broadcasted_iota(jnp.int32, (size, size), 1)
    line = lax.broadcasted_iota(jnp.int32, (size, 1), 0)
    second = line // (rows * BLOCK)
    frame = jnp.where(second == 0, 1 - chan, chan)
    row = line // BLOCK % rows
    origin = line % BLOCK * (2 * rows) + frame * rows + row
    turn = jnp.where(placed == origin, 1.0, 0.0).astype(BF16)
    inside = rows * half
    for n in range(half // BLOCK):
        image = pixels_ref[n * size : (n + 1) * size, :]
        image = jnp.dot(turn, image, preferred_element_type=F32).astype(BF16)
        image = jnp.dot(image, split, preferred_element_type=F32).astype(BF16)
        for f, out_ref in enumerate((cross_ref, same_ref)):
            for r in range(rows):
                first = (f * rows + r) * BLOCK
                block = image[first : first + BLOCK, :]
                first = r * half + n * BLOCK
                out_ref[first : first + BLOCK, :] = block
                both_ref[f * inside + first : f * inside + first + BLOCK, :] = block
    for f, out_ref in enumerate((cross_ref, same_ref)):
        low, high = out_ref[:half, :], out_ref[(rows - 1) * half :, :]
        for h, edge_ref in enumerate(edge_refs):
            to_low = odd if h == 0 else jnp.logical_not(odd)
            edge_ref[f * half : (f + 1) * half, :] = jnp.where(to_low, low, high)


def halo_kernel(halos, capacity, small_ref, *refs):
    halo_refs, kept_refs, (cross_ref, same_ref) = refs[:halos], refs[halos : 2 * halos], refs[2 * halos :]
    for halo_ref, kept_ref in zip(halo_refs, kept_refs):
        kept_ref[...] = halo_ref[...]
    chan = lax.axis_index("chan")
    half, columns = CHANNELS // 2, cross_ref.shape[1]
    count = SEND_ROWS
    line = lax.broadcasted_iota(jnp.int32, (ID_ROWS, CHANNELS), 0)
    lane = lax.broadcasted_iota(jnp.int32, (ID_ROWS, CHANNELS), 1)
    owners = jnp.broadcast_to(small_ref[3:4, :], (ID_ROWS, CHANNELS))
    mine = jnp.sum(jnp.where(line == lane, owners, 0.0), axis=1, keepdims=True)
    rank = jnp.sum(jnp.where((owners == mine) & (lane < line), 1.0, 0.0), axis=1, keepdims=True)
    keys = mine * float(capacity) + rank + 1.0
    place = lax.broadcasted_iota(jnp.int32, (ID_ROWS, columns), 0)
    tail = jnp.where(place < count, keys, 0.0)
    ids = [number_at(small_ref, n) for n in range(2)]
    for n, (out_ref, frame) in enumerate(((cross_ref, 1 - chan), (same_ref, chan))):
        for h in range(halos):
            out_ref[h * half : (h + 1) * half, :] = halo_refs[h][n * half : (n + 1) * half, :]
        number = jnp.where(frame == 0, ids[0], ids[1])
        if n == 1:
            out_ref[halos * half :, :] = jnp.where(place == count, number + 1.0, tail).astype(BF16)


def weights_kernel(
    ids_any, owner_any, gain_any, bias_any, out_weight_any, weight_ref, _, local_ref, late_ref, sum_ref, small_ref,
    out_matrix_ref, ids_ref, owner_ref, gain_ref, bias_ref, out_weight_ref, taps_ref, copies
):
    chan = lax.axis_index("chan")
    fetched = [
        pltpu.make_async_copy(source, target, copies.at[n])
        for n, (source, target) in enumerate(
            (
                (ids_any, ids_ref),
                (owner_any, owner_ref),
                (gain_any, gain_ref),
                (bias_any, bias_ref),
                (out_weight_any, out_weight_ref),
            )
        )
    ]
    for copy in fetched:
        copy.start()
    half = CHANNELS // 2
    own = pl.multiple_of(chan * half, half)
    other = pl.multiple_of((1 - chan) * half, half)
    for j in range(3):
        for i in range(3):
            for k in range(3):
                block = jnp.concatenate(
                    [weight_ref[k, i, j, pl.ds(own, half), :], weight_ref[k, i, j, pl.ds(other, half), :]],
                    axis=0,
                )
                taps_ref[k, i, j] = block.T
    for copy in fetched:
        copy.wait()
    small_ref[...] = jnp.zeros_like(small_ref)
    small_ref[0:1, :] = gain_ref[...]
    small_ref[1:2, :] = bias_ref[...]
    small_ref[2:3, : ids_ref.shape[1]] = ids_ref[...].astype(F32)
    small_ref[3:4, :SEND_ROWS] = owner_ref[...].astype(F32)
    for i in range(2):
        for j in range(2):
            first = (2 * i + j) * CHANNELS
            out_matrix_ref[:, first : first + CHANNELS] = out_weight_ref[i, j]
    zero = jnp.float32(0.0)
    one = jnp.float32(1.0)
    first = chan == 0
    joined = number_at(small_ref, 0) == number_at(small_ref, 1)
    flag = jnp.where(joined, one, zero)
    on_first = jnp.where(first, one, zero)
    on_second = one - on_first
    near = (
        on_first * (one - flag),
        on_first + on_second * flag,
        zero,
    )
    far = (
        on_first * flag + on_second * (one - flag),
        on_second * (one - flag),
        on_second,
    )
    late_same = (on_second * flag, zero, on_first)
    late_apart = (on_first + on_second * flag, on_first, on_first)
    for j in range(3):
        for i in range(3):
            taps = [taps_ref[k, i, j].astype(F32) for k in range(3)]

            def mixed(scale):
                return (taps[0] * scale[0] + taps[1] * scale[1] + taps[2] * scale[2]).astype(BF16)

            rows = slice(j * CHANNELS, (j + 1) * CHANNELS)
            columns = slice(i * CHANNELS, (i + 1) * CHANNELS)
            shifted = slice((3 + i) * CHANNELS, (4 + i) * CHANNELS)
            local_ref[rows, columns] = mixed(near)
            local_ref[rows, shifted] = mixed(far)
            late_ref[0, rows, columns] = mixed(late_same)
            late_ref[1, rows, columns] = mixed(late_apart)
            sum_ref[rows, columns] = mixed((one, one, one))


def image_row(sources, rows, odd, r):
    half = CHANNELS // 2
    pieces = []
    for ref, start, halos in sources:
        if 0 <= r < rows:
            pieces.append(ref[start + r * half : start + (r + 1) * half, :])
            continue
        edges = [halo_ref[first : first + half, :] for halo_ref, first in halos]
        edges.append(jnp.zeros_like(edges[0]))
        on_first = odd if r < 0 else jnp.logical_not(odd)
        pieces.append(jnp.where(on_first, edges[0], edges[1]))
    return jnp.concatenate(pieces, axis=0)


def local_sources(rows, cross_ref, same_ref, other_ref, own_halos, other_halos):
    half = CHANNELS // 2
    inside = rows * half
    near = (
        (cross_ref, 0, [(ref, 0) for ref in own_halos]),
        (other_ref, inside, [(ref, half) for ref in other_halos]),
    )
    far = (
        (same_ref, 0, [(ref, half) for ref in own_halos]),
        (other_ref, 0, [(ref, 0) for ref in other_halos]),
    )
    return near, far


def joined_columns(product):
    half = product.shape[1] // 2
    left = product[:CHANNELS, :]
    middle = product[CHANNELS : 2 * CHANNELS, :]
    right = product[2 * CHANNELS :, :]
    lane = lax.broadcasted_iota(jnp.int32, (CHANNELS, half), 1)
    from_left = jnp.where(lane == 0, 0.0, pltpu.roll(left[:, half:], 1, 1))
    from_right = jnp.where(lane == half - 1, 0.0, pltpu.roll(right[:, :half], half - 1, 1))
    even = from_left + middle[:, :half] + right[:, half:]
    odd = left[:, :half] + middle[:, half:] + from_right
    return even, odd


def group_place():
    return lax.broadcasted_iota(jnp.int32, (1, CHANNELS), 1) % (CHANNELS // GROUPS)


def group_totals(lines):
    lane = lax.broadcasted_iota(jnp.int32, lines.shape, 1)
    step = 1
    while step < CHANNELS // GROUPS:
        ahead = pltpu.roll(lines, CHANNELS - step, 1)
        behind = pltpu.roll(lines, step, 1)
        lines = lines + jnp.where(lane // step % 2 == 0, ahead, behind)
        step *= 2
    return lines


def lane_totals(first, second):
    rows = [jnp.sum(value.T, axis=0, keepdims=True) for value in (first, second)]
    return rows


def local_kernel(rows, halos, weight_ref, sum_ref, *refs):
    conv_ref, extra_ref, sums_ref, images_ref = refs[3 + 2 * halos :]
    near, far = local_sources(rows, *refs[:3], refs[3 : 3 + halos], refs[3 + halos : 3 + 2 * halos])
    odd = lax.axis_index("space") % 2 == 1
    chan = lax.axis_index("chan")
    half = conv_ref.shape[2] // 2
    for r in range(rows):
        image = jnp.concatenate(
            [image_row(frame, rows, odd, r + i) for frame in (near, far) for i in (-1, 0, 1)], axis=0
        )
        product = jnp.dot(weight_ref[...], image, preferred_element_type=F32)
        for side, value in enumerate(joined_columns(product)):
            conv_ref[r, :, side * half : (side + 1) * half] = value
    sums_ref[...] = jnp.zeros_like(sums_ref)

    @pl.when(lax.axis_index("tm") == 0)
    def _():
        rows_here = rows // 2
        for n in range(rows_here + 2):
            upper = image_row(far, rows, odd, n - 1)
            lower = image_row(near, rows, odd, rows_here + n - 1)
            images_ref[n] = jnp.where(chan == 0, upper, lower)
        totals = [jnp.zeros((CHANNELS, half), F32)] * 2
        for r in range(rows_here):
            image = jnp.concatenate([images_ref[r + i] for i in range(3)], axis=0)
            product = jnp.dot(sum_ref[...], image, preferred_element_type=F32)
            for side, value in enumerate(joined_columns(product)):
                value = value.astype(BF16)
                extra_ref[r, :, side * half : (side + 1) * half] = value
                value = value.astype(F32)
                totals = [totals[0] + value, totals[1] + value * value]
        one, two = lane_totals(*totals)
        sums_ref[0:1, :] = one
        sums_ref[1:2, :] = two


def late_kernel(rows, halos, slabs, small_ref, weight_ref, part_ref, extra_ref, sums_ref, own_edge_ref, *refs):
    near, _ = local_sources(rows, *refs[:3], refs[3 : 3 + halos], refs[3 + halos : 3 + 2 * halos])
    refs = refs[3 + 2 * halos :]
    late_own_ref, late_other_ref, own_halo_ref, other_halo_ref = refs[:4]
    conv_ref, message_ref, keys_ref, images_ref = refs[4:]
    extent = CHANNELS // 2
    arrived = (
        (late_own_ref, 0, [(own_halo_ref, h * extent) for h in range(halos)]),
        (late_other_ref, 0, [(other_halo_ref, h * extent) for h in range(halos)]),
    )
    odd = lax.axis_index("space") % 2 == 1
    slab = lax.axis_index("tm")
    first = lax.axis_index("chan") == 0
    half = part_ref.shape[2] // 2
    kept = rows // 2
    tail = halos * extent
    absent = slab == jnp.where(first, slabs - 1, 0)
    late_tail = jnp.where(absent, 0.0, own_halo_ref[tail:, :CHANNELS].astype(F32))
    own_tail = own_edge_ref[tail:, :CHANNELS].astype(F32)
    number = jnp.max(late_tail[2 * kept : 2 * kept + 1, :]) - 1.0
    ids = [number_at(small_ref, n) for n in range(2)]
    same = number == jnp.where(first, ids[1], ids[0])
    keep = jnp.where(jnp.logical_or(same, jnp.logical_not(first)), 1.0, 0.0)
    use_late = jnp.logical_or(same, first)
    choice = jnp.where(same, 0, 1)
    for r in range(-1, rows + 1):
        late = image_row(arrived, rows, odd, r)
        here = image_row(near, rows, odd, r)
        images_ref[r + 1] = jnp.where(use_late, late, here)
    totals = [jnp.zeros((CHANNELS, half), F32)] * 2
    for r in range(rows):
        image = jnp.concatenate([images_ref[r + i] for i in range(3)], axis=0)
        product = jnp.dot(weight_ref[choice], image, preferred_element_type=F32)
        for side, value in enumerate(joined_columns(product)):
            lanes = slice(side * half, (side + 1) * half)
            value = (value + keep * part_ref[r, :, lanes]).astype(BF16)
            conv_ref[r, :, lanes] = value
            value = value.astype(F32)
            totals = [totals[0] + value, totals[1] + value * value]
    one, two = lane_totals(*totals)
    main_id = jnp.where(first, number, ids[1])
    extra_id = jnp.where(slab == 0, ids[0], -1.0)
    line = lax.broadcasted_iota(jnp.int32, (8, CHANNELS), 0)
    sums = jnp.where(line == 0, one, 0.0)
    sums = jnp.where(line == 1, two, sums)
    sums = jnp.where(line == 2, sums_ref[0:1, :], sums)
    sums = jnp.where(line == 3, sums_ref[1:2, :], sums)
    sums = group_totals(sums)
    place = group_place()
    message = jnp.concatenate(
        [
            jnp.sum(jnp.where(line == jnp.broadcast_to(place, line.shape), sums, 0.0), axis=0, keepdims=True),
            jnp.where(place < 2, main_id, extra_id),
        ],
        axis=1,
    )
    message_ref[...] = jnp.broadcast_to(message, message_ref.shape)
    keys = jnp.zeros((8, CHANNELS), F32)
    for n in range(kept):
        main_key = jnp.where(first, late_tail[n : n + 1, :], own_tail[kept + n : kept + n + 1, :])
        keys = jnp.where(line == n, main_key, keys)
    quarter = kept // 2
    for n in range(quarter):
        extra_key = jnp.where(first, own_tail[n : n + 1, :], own_tail[quarter + n : quarter + n + 1, :])
        keys = jnp.where(line == kept + n, jnp.where(slab == 0, extra_key, 0.0), keys)
    keys_ref[...] = keys
    conv_ref[rows + kept, :ID_ROWS, :CHANNELS] = jnp.concatenate([keys] * 2, axis=0).astype(BF16)

    @pl.when(slab == 0)
    def _():
        conv_ref[rows : rows + kept] = extra_ref[...]


def crossed(slabs):
    return slabs in (2, 4)


def norm_kernel(
    rows, slabs, spaces, capacity, message_ref, keys_ref, gathered_ref, small_ref, out_matrix_ref, conv_ref, other_ref,
    *send_refs
):
    columns = conv_ref.shape[2]
    half = columns // 2
    kept = rows // 2
    part = MOMENTS // 2
    slab, space, chan = [lax.axis_index(name) for name in PART]
    count = float(rows * columns)
    sums, ids = gathered_ref[:, :CHANNELS], gathered_ref[:, CHANNELS:]
    place = group_place()
    beside = (slab * spaces + space) * 2 + 1 - chan
    line = lax.broadcasted_iota(jnp.int32, (gathered_ref.shape[0], 1), 0)
    numbers = [
        message_ref[0:1, CHANNELS : CHANNELS + 1],
        jnp.sum(jnp.where(line == beside, gathered_ref[:, CHANNELS : CHANNELS + 1], 0.0), axis=0, keepdims=True),
        message_ref[0:1, CHANNELS + 2 : CHANNELS + 3],
    ]
    lines = []
    for number in numbers:
        mask = ids == number
        picked = jnp.sum(jnp.where(mask, sums, 0.0), axis=0, keepdims=True)
        pixels = jnp.where(place == 0, count, jnp.where(place == 2, 0.5 * count, 0.0))
        held = jnp.sum(jnp.where(mask, pixels, 0.0), axis=0, keepdims=True)
        lines += [jnp.where(place % 2 == n, picked, 0.0) for n in range(2)] + [held]
    totals = group_totals(jnp.concatenate(lines + [jnp.zeros((7, CHANNELS), F32)], axis=0))
    matrix = out_matrix_ref[pl.ds(pl.multiple_of(chan * part, part), part), :]

    def factors(first):
        size = float(CHANNELS // GROUPS)
        counts = totals[first + 2 : first + 3, :] * size
        mean = totals[first : first + 1, :] / counts
        var = totals[first + 1 : first + 2, :] / counts - mean * mean
        scale = lax.rsqrt(var + 1e-06) * small_ref[0:1, :]
        offset = small_ref[1:2, :] - mean * scale
        return [jnp.broadcast_to(0.5 * value, (CHANNELS, CHANNELS)).T for value in (scale, offset)]

    def project(source_ref, first, lines, scale, offset):
        images = []
        for r in range(first, first + lines, 2):
            pieces = []
            for i in range(2):
                for j in range(2):
                    value = source_ref[r + i, :, j * half : (j + 1) * half].astype(F32)
                    value = value * scale + offset
                    pieces.append((value + value * jnp.tanh(value)).astype(BF16))
            images.append(jnp.concatenate(pieces, axis=0))
        image = jnp.concatenate(images, axis=1)
        return jnp.dot(matrix, image, preferred_element_type=F32)

    own_keys = keys_ref[...]
    other_keys = other_ref[rows + kept, :ID_ROWS, :CHANNELS].astype(F32)

    def blocks(latent, keys, first):
        return [
            (keys[first + n : first + n + 1, :], latent[:, n * half : (n + 1) * half])
            for n in range(latent.shape[1] // half)
        ]

    def spread(groups, started):
        for d in range(slabs):
            owner = (slab ^ d if crossed(slabs) else jnp.int32(d)).astype(F32)
            for j in range(capacity):
                wanted = owner * float(capacity) + float(j + 1)
                for first, group in groups:
                    ref = send_refs[d].at[first + j] if crossed(slabs) else send_refs[0].at[d, first + j]
                    value = ref[...].astype(F32) if started else jnp.zeros((part, half), F32)
                    for key, block in group:
                        value = jnp.where(key == wanted, block, value)
                    ref[...] = value.astype(BF16)

    mine = project(conv_ref, 0, rows, *factors(0))
    others = project(other_ref, 0, rows, *factors(3))
    second = chan == 1
    now = blocks(jnp.where(second, mine, others), jnp.where(second, own_keys, other_keys[:8, :]), 0)
    following = blocks(jnp.where(second, others, mine), jnp.where(second, other_keys[:8, :], own_keys), 0)
    spread(((0, now), (capacity, following)), False)

    @pl.when(slab == 0)
    def _():
        scale, offset = factors(6)
        begin = []
        for ref, keys in ((conv_ref, own_keys), (other_ref, other_keys)):
            begin += blocks(project(ref, rows, kept, scale, offset), keys, kept)
        spread(((0, begin),), True)


def merge_kernel(slabs, capacity, *refs):
    sources, owned_ref = refs[:-1], refs[-1]
    slab = lax.axis_index("tm")

    def source(d):
        if crossed(slabs):
            return slab ^ d, sources[d]
        return d, sources[0].at[d]

    for d in range(slabs):
        block, ref = source(d)
        for j in range(capacity):
            owned_ref[block * capacity + j] = ref[j]
    for d in range(slabs):
        block, ref = source(d)

        @pl.when(block + 1 < slabs)
        def _():
            for j in range(capacity):
                n = (block + 1) * capacity + j
                owned_ref[n] = (owned_ref[n].astype(F32) + ref[capacity + j].astype(F32)).astype(BF16)


def shards(activations, frame_clip, conv_weight, norm_gain, norm_bias, out_weight, owner):
    half, frames, rows, columns = activations.shape
    sizes = tuple(lax.axis_size(name) for name in PART)
    slabs, spaces, chans = sizes
    assert (frames, chans, half * chans) == (2, 2, CHANNELS)
    parts = slabs * spaces * chans
    halos = 1 if spaces <= 2 else 2
    send_rows = frames * (rows // 2)
    capacity = max(2, 2 * send_rows // slabs)
    kept = rows // 2
    assert send_rows == SEND_ROWS
    payload = jax.ShapeDtypeStruct((rows * half, columns), BF16)
    pair = jax.ShapeDtypeStruct((2 * half, columns), BF16)
    cross, same, both, *edges = whole_call(
        lambda *refs: front_kernel(rows, *refs),
        (payload, payload, jax.ShapeDtypeStruct((2 * rows * half, columns), BF16)) + (pair,) * halos,
        (activations.reshape(half * frames * rows, columns),),
        flops=3000000000,
    )
    own_halos = [space_swap(edge, sizes, start) for start, edge in enumerate(edges)]
    late_own = slab_swap(same, sizes, False)
    late_other = slab_swap(cross, sizes, True)
    turn = [(0, 1), (1, 0)]
    local_weight, late_weight, sum_weight, small, out_matrix = whole_call(
        weights_kernel,
        (
            jax.ShapeDtypeStruct((3 * CHANNELS, 6 * CHANNELS), BF16),
            jax.ShapeDtypeStruct((2, 3 * CHANNELS, 3 * CHANNELS), BF16),
            jax.ShapeDtypeStruct((3 * CHANNELS, 3 * CHANNELS), BF16),
            jax.ShapeDtypeStruct((8, CHANNELS), F32),
            jax.ShapeDtypeStruct((MOMENTS, 4 * CHANNELS), BF16),
        ),
        (
            frame_clip.reshape(1, frames), owner.reshape(1, send_rows), norm_gain.reshape(1, CHANNELS),
            norm_bias.reshape(1, CHANNELS), out_weight.transpose(0, 1, 3, 2), conv_weight, both,
        ),
        [
            pltpu.VMEM((1, frames), jnp.int32),
            pltpu.VMEM((1, send_rows), jnp.int32),
            pltpu.VMEM((1, CHANNELS), F32),
            pltpu.VMEM((1, CHANNELS), F32),
            pltpu.VMEM((2, 2, MOMENTS, CHANNELS), BF16),
            pltpu.VMEM((3, 3, 3, CHANNELS, CHANNELS), BF16),
            pltpu.SemaphoreType.DMA((5,)),
        ],
        [pl.BlockSpec(memory_space=pl.ANY)] * 5 + [VMEM] * 2,
        4800000000,
    )
    other = lax.ppermute(both, "chan", turn)
    message_halo = jax.ShapeDtypeStruct((halos * half + ID_ROWS, columns), BF16)
    *own_halos, cross_halo, same_halo = whole_call(
        lambda *refs: halo_kernel(halos, capacity, *refs[: 1 + halos], *refs[2 + halos :]),
        (pair,) * halos + (jax.ShapeDtypeStruct((halos * half, columns), BF16), message_halo),
        (small, *own_halos, other),
    )
    other_halos = [lax.ppermute(halo, "chan", turn) for halo in own_halos]
    late_own_halo = slab_swap(same_halo, sizes, False)
    late_other_halo = slab_swap(cross_halo, sizes, True)
    here = (cross, same, other, *own_halos, *other_halos)
    part, extra, extra_sums = whole_call(
        lambda *refs: local_kernel(rows, halos, *refs),
        (
            jax.ShapeDtypeStruct((rows, CHANNELS, columns), F32),
            jax.ShapeDtypeStruct((rows // 2, CHANNELS, columns), BF16),
            jax.ShapeDtypeStruct((8, CHANNELS), F32),
        ),
        (local_weight, sum_weight, *here),
        [pltpu.VMEM((rows // 2 + 2, CHANNELS, columns), BF16)],
        flops=1000000,
    )
    conv, message, keys = whole_call(
        lambda *refs: late_kernel(rows, halos, slabs, *refs),
        (
            jax.ShapeDtypeStruct((rows + kept + 1, CHANNELS, columns), BF16),
            jax.ShapeDtypeStruct((parts, 2 * CHANNELS), F32),
            jax.ShapeDtypeStruct((8, CHANNELS), F32),
        ),
        (
            small, late_weight, part, extra, extra_sums, same_halo, *here, late_own, late_other, late_own_halo, late_other_halo,
        ),
        [pltpu.VMEM((rows + 2, CHANNELS, columns), BF16)],
        flops=1500000000,
    )
    conv_other = lax.ppermute(conv, "chan", turn)
    gathered = lax.all_to_all(message, PART, split_axis=0, concat_axis=0, tiled=True)
    part = MOMENTS // chans
    width = columns // 2
    blocks = (2 * capacity, part, width)
    if crossed(slabs):
        shapes = (jax.ShapeDtypeStruct(blocks, BF16),) * slabs
    else:
        shapes = (jax.ShapeDtypeStruct((slabs,) + blocks, BF16),)
    sends = whole_call(
        lambda *refs: norm_kernel(rows, slabs, spaces, capacity, *refs),
        shapes,
        (message, keys, gathered, small, out_matrix, conv, conv_other),
    )
    if crossed(slabs):
        received = [sends[0]]
        for d in range(1, slabs):
            received.append(lax.ppermute(sends[d], "tm", [(t, t ^ d) for t in range(slabs)]))
    else:
        received = [lax.all_to_all(sends[0], "tm", split_axis=0, concat_axis=0, tiled=True)]
    turns = list((0, 3, 1, 2)) if crossed(slabs) else [0]
    owned = pl.pallas_call(
        lambda *refs: merge_kernel(slabs, capacity, *[refs[turns.index(d)] for d in range(len(turns))], refs[-1]),
        out_shape=jax.ShapeDtypeStruct((slabs * capacity, part, width), BF16),
        in_specs=[VMEM] * len(received),
        out_specs=pl.BlockSpec((slabs * capacity, part, width), lambda: (0, 0, 0)),
        compiler_params=PARAMS,
    )(*[received[d] for d in turns])
    return owned[None]


def solution(mesh):
    placed = (
        P(("groups", "chan"), "tm", "space", None),
        P(("groups", "tm")),
        P(),
        P(),
        P(),
        P(),
        P(("groups", "space"), "tm", None),
    )
    return jax.shard_map(
        shards,
        mesh=mesh,
        in_specs=placed,
        out_specs=P(("groups", "space"), "tm", "chan", None),
        check_vma=False,
    )
```

```python
import jax
import jax.numpy as jnp
import numpy as np
from jax import lax
from jax.experimental import pallas as pl
from jax.experimental.pallas import tpu as pltpu
from jax.sharding import PartitionSpec as P

CHANNELS = 128
GROUPS = 32
MOMENTS = 32
SEND_ROWS = 8
ID_ROWS = 16
BLOCK = 16
BF16 = jnp.bfloat16
F32 = jnp.float32
VMEM = pl.BlockSpec(memory_space=pltpu.VMEM)
PARAMS = pltpu.CompilerParams(vmem_limit_bytes=40 * 1024 * 1024)
PART = ("tm", "space", "chan")


def flat_pairs(sizes, pairs):
    _, spaces, chans = sizes
    return [
        ((a[0] * spaces + a[1]) * chans + a[2], (b[0] * spaces + b[1]) * chans + b[2])
        for a, b in pairs
    ]


def space_swap(value, sizes, start):
    slabs, spaces, chans = sizes
    pairs = []
    for low in range(start, spaces - 1, 2):
        for t in range(slabs):
            for c in range(chans):
                pairs += [((t, low, c), (t, low + 1, c)), ((t, low + 1, c), (t, low, c))]
    return lax.ppermute(value, PART, flat_pairs(sizes, pairs))


def slab_swap(value, sizes, cross):
    slabs, spaces, _ = sizes
    last = slabs - 1
    pairs = []
    for s in range(spaces):
        for t in range(last):
            if cross:
                pairs += [((t, s, 0), (t + 1, s, 1)), ((t + 1, s, 1), (t, s, 0))]
            else:
                pairs += [((t, s, 1), (t + 1, s, 1)), ((t + 1, s, 0), (t, s, 0))]
        if spaces % 2 == 0 and cross:
            pairs += [((0, s, 1), (0, s ^ 1, 1)), ((last, s, 0), (last, s ^ 1, 0))]
        elif spaces % 2 == 0:
            pairs += [((last, s, 1), (last, s, 0)), ((0, s, 0), (0, s, 1))]
    return lax.ppermute(value, PART, flat_pairs(sizes, pairs))


def whole_call(kernel, out_shape, args, scratch=(), specs=None, flops=0, vmem=40, first=()):
    turns = list(first) + [n for n in range(len(args)) if n not in first]
    specs = specs or [VMEM] * len(args)

    def turned(*refs):
        kernel(*[refs[turns.index(n)] for n in range(len(args))], *refs[len(args) :])

    return pl.pallas_call(
        turned,
        out_shape=out_shape,
        in_specs=[specs[n] for n in turns],
        out_specs=jax.tree.map(lambda _: VMEM, out_shape),
        scratch_shapes=scratch,
        compiler_params=pltpu.CompilerParams(vmem_limit_bytes=vmem * 1024 * 1024),
        cost_estimate=pl.CostEstimate(flops=flops, bytes_accessed=flops // 400, transcendentals=0),
    )(*[args[n] for n in turns])


def number_at(small_ref, n):
    lane = lax.broadcasted_iota(jnp.int32, (1, CHANNELS), 1)
    return jnp.sum(jnp.where(lane == n, small_ref[2:3, :], 0.0))


def front_kernel(rows, pixels_ref, cross_ref, same_ref, both_ref, *edge_refs):
    chan = lax.axis_index("chan")
    odd = lax.axis_index("space") % 2 == 1
    half, columns = CHANNELS // 2, pixels_ref.shape[1]
    size = 2 * rows * BLOCK
    source = lax.broadcasted_iota(jnp.int32, (columns, columns), 0)
    target = lax.broadcasted_iota(jnp.int32, (1, columns), 1)
    wanted = jnp.where(target < columns // 2, 2 * target, 2 * target - columns + 1)
    split = jnp.where(source == wanted, 1.0, 0.0).astype(BF16)
    placed = lax.broadcasted_iota(jnp.int32, (size, size), 1)
    line = lax.broadcasted_iota(jnp.int32, (size, 1), 0)
    second = line // (rows * BLOCK)
    frame = jnp.where(second == 0, 1 - chan, chan)
    row = line // BLOCK % rows
    origin = line % BLOCK * (2 * rows) + frame * rows + row
    turn = jnp.where(placed == origin, 1.0, 0.0).astype(BF16)
    inside = rows * half
    for n in range(half // BLOCK):
        image = pixels_ref[n * size : (n + 1) * size, :]
        image = jnp.dot(turn, image, preferred_element_type=F32).astype(BF16)
        image = jnp.dot(image, split, preferred_element_type=F32).astype(BF16)
        for f, out_ref in enumerate((cross_ref, same_ref)):
            for r in range(rows):
                first = (f * rows + r) * BLOCK
                block = image[first : first + BLOCK, :]
                first = r * half + n * BLOCK
                out_ref[first : first + BLOCK, :] = block
                both_ref[f * inside + first : f * inside + first + BLOCK, :] = block
    for f, out_ref in enumerate((cross_ref, same_ref)):
        low, high = out_ref[:half, :], out_ref[(rows - 1) * half :, :]
        for h, edge_ref in enumerate(edge_refs):
            to_low = odd if h == 0 else jnp.logical_not(odd)
            edge_ref[f * half : (f + 1) * half, :] = jnp.where(to_low, low, high)


def halo_kernel(halos, capacity, small_ref, *refs):
    halo_refs, kept_refs, (cross_ref, same_ref) = refs[:halos], refs[halos : 2 * halos], refs[2 * halos :]
    for halo_ref, kept_ref in zip(halo_refs, kept_refs):
        kept_ref[...] = halo_ref[...]
    chan = lax.axis_index("chan")
    half, columns = CHANNELS // 2, cross_ref.shape[1]
    count = SEND_ROWS
    line = lax.broadcasted_iota(jnp.int32, (ID_ROWS, CHANNELS), 0)
    lane = lax.broadcasted_iota(jnp.int32, (ID_ROWS, CHANNELS), 1)
    owners = jnp.broadcast_to(small_ref[3:4, :], (ID_ROWS, CHANNELS))
    mine = jnp.sum(jnp.where(line == lane, owners, 0.0), axis=1, keepdims=True)
    rank = jnp.sum(jnp.where((owners == mine) & (lane < line), 1.0, 0.0), axis=1, keepdims=True)
    keys = mine * float(capacity) + rank + 1.0
    place = lax.broadcasted_iota(jnp.int32, (ID_ROWS, columns), 0)
    tail = jnp.where(place < count, keys, 0.0)
    ids = [number_at(small_ref, n) for n in range(2)]
    for n, (out_ref, frame) in enumerate(((cross_ref, 1 - chan), (same_ref, chan))):
        for h in range(halos):
            out_ref[h * half : (h + 1) * half, :] = halo_refs[h][n * half : (n + 1) * half, :]
        number = jnp.where(frame == 0, ids[0], ids[1])
        if n == 1:
            out_ref[halos * half :, :] = jnp.where(place == count, number + 1.0, tail).astype(BF16)


def weights_kernel(
    ids_any, owner_any, gain_any, bias_any, out_weight_any, weight_ref, _, local_ref, late_ref, sum_ref, small_ref,
    out_matrix_ref, ids_ref, owner_ref, gain_ref, bias_ref, out_weight_ref, taps_ref, copies
):
    chan = lax.axis_index("chan")
    fetched = [
        pltpu.make_async_copy(source, target, copies.at[n])
        for n, (source, target) in enumerate(
            (
                (ids_any, ids_ref),
                (owner_any, owner_ref),
                (gain_any, gain_ref),
                (bias_any, bias_ref),
                (out_weight_any, out_weight_ref),
            )
        )
    ]
    for copy in fetched:
        copy.start()
    half = CHANNELS // 2
    own = pl.multiple_of(chan * half, half)
    other = pl.multiple_of((1 - chan) * half, half)
    for j in range(3):
        for i in range(3):
            for k in range(3):
                block = jnp.concatenate(
                    [weight_ref[k, i, j, pl.ds(own, half), :], weight_ref[k, i, j, pl.ds(other, half), :]],
                    axis=0,
                )
                taps_ref[k, i, j] = block.T
    for copy in fetched:
        copy.wait()
    small_ref[...] = jnp.zeros_like(small_ref)
    small_ref[0:1, :] = gain_ref[...]
    small_ref[1:2, :] = bias_ref[...]
    small_ref[2:3, : ids_ref.shape[1]] = ids_ref[...].astype(F32)
    small_ref[3:4, :SEND_ROWS] = owner_ref[...].astype(F32)
    for i in range(2):
        for j in range(2):
            first = (2 * i + j) * CHANNELS
            out_matrix_ref[:, first : first + CHANNELS] = out_weight_ref[i, j]
    zero = jnp.float32(0.0)
    one = jnp.float32(1.0)
    first = chan == 0
    joined = number_at(small_ref, 0) == number_at(small_ref, 1)
    flag = jnp.where(joined, one, zero)
    on_first = jnp.where(first, one, zero)
    on_second = one - on_first
    near = (
        on_first * (one - flag),
        on_first + on_second * flag,
        zero,
    )
    far = (
        on_first * flag + on_second * (one - flag),
        on_second * (one - flag),
        on_second,
    )
    late_same = (on_second * flag, zero, on_first)
    late_apart = (on_first + on_second * flag, on_first, on_first)
    for j in range(3):
        for i in range(3):
            taps = [taps_ref[k, i, j].astype(F32) for k in range(3)]

            def mixed(scale):
                return (taps[0] * scale[0] + taps[1] * scale[1] + taps[2] * scale[2]).astype(BF16)

            rows = slice(j * CHANNELS, (j + 1) * CHANNELS)
            columns = slice(i * CHANNELS, (i + 1) * CHANNELS)
            shifted = slice((3 + i) * CHANNELS, (4 + i) * CHANNELS)
            local_ref[rows, columns] = mixed(near)
            local_ref[rows, shifted] = mixed(far)
            late_ref[0, rows, columns] = mixed(late_same)
            late_ref[1, rows, columns] = mixed(late_apart)
            sum_ref[rows, columns] = mixed((one, one, one))


def image_row(sources, rows, odd, r):
    half = CHANNELS // 2
    pieces = []
    for ref, start, halos in sources:
        if 0 <= r < rows:
            pieces.append(ref[start + r * half : start + (r + 1) * half, :])
            continue
        edges = [halo_ref[first : first + half, :] for halo_ref, first in halos]
        edges.append(jnp.zeros_like(edges[0]))
        on_first = odd if r < 0 else jnp.logical_not(odd)
        pieces.append(jnp.where(on_first, edges[0], edges[1]))
    return jnp.concatenate(pieces, axis=0)


def local_sources(rows, cross_ref, same_ref, other_ref, own_halos, other_halos):
    half = CHANNELS // 2
    inside = rows * half
    near = (
        (cross_ref, 0, [(ref, 0) for ref in own_halos]),
        (other_ref, inside, [(ref, half) for ref in other_halos]),
    )
    far = (
        (same_ref, 0, [(ref, half) for ref in own_halos]),
        (other_ref, 0, [(ref, 0) for ref in other_halos]),
    )
    return near, far


def joined_columns(product):
    half = product.shape[1] // 2
    left = product[:CHANNELS, :]
    middle = product[CHANNELS : 2 * CHANNELS, :]
    right = product[2 * CHANNELS :, :]
    lane = lax.broadcasted_iota(jnp.int32, (CHANNELS, half), 1)
    from_left = jnp.where(lane == 0, 0.0, pltpu.roll(left[:, half:], 1, 1))
    from_right = jnp.where(lane == half - 1, 0.0, pltpu.roll(right[:, :half], half - 1, 1))
    even = from_left + middle[:, :half] + right[:, half:]
    odd = left[:, :half] + middle[:, half:] + from_right
    return even, odd


def group_place():
    return lax.broadcasted_iota(jnp.int32, (1, CHANNELS), 1) % (CHANNELS // GROUPS)


def group_totals(lines):
    lane = lax.broadcasted_iota(jnp.int32, lines.shape, 1)
    step = 1
    while step < CHANNELS // GROUPS:
        ahead = pltpu.roll(lines, CHANNELS - step, 1)
        behind = pltpu.roll(lines, step, 1)
        lines = lines + jnp.where(lane // step % 2 == 0, ahead, behind)
        step *= 2
    return lines


def lane_totals(first, second):
    rows = [jnp.sum(value.T, axis=0, keepdims=True) for value in (first, second)]
    return rows


def local_kernel(rows, halos, weight_ref, sum_ref, *refs):
    conv_ref, extra_ref, sums_ref, images_ref = refs[3 + 2 * halos :]
    near, far = local_sources(rows, *refs[:3], refs[3 : 3 + halos], refs[3 + halos : 3 + 2 * halos])
    odd = lax.axis_index("space") % 2 == 1
    chan = lax.axis_index("chan")
    half = conv_ref.shape[2] // 2
    for r in range(rows):
        image = jnp.concatenate(
            [image_row(frame, rows, odd, r + i) for frame in (near, far) for i in (-1, 0, 1)], axis=0
        )
        product = jnp.dot(weight_ref[...], image, preferred_element_type=F32)
        for side, value in enumerate(joined_columns(product)):
            conv_ref[r, :, side * half : (side + 1) * half] = value
    sums_ref[...] = jnp.zeros_like(sums_ref)

    @pl.when(lax.axis_index("tm") == 0)
    def _():
        rows_here = rows // 2
        for n in range(rows_here + 2):
            upper = image_row(far, rows, odd, n - 1)
            lower = image_row(near, rows, odd, rows_here + n - 1)
            images_ref[n] = jnp.where(chan == 0, upper, lower)
        totals = [jnp.zeros((CHANNELS, half), F32)] * 2
        for r in range(rows_here):
            image = jnp.concatenate([images_ref[r + i] for i in range(3)], axis=0)
            product = jnp.dot(sum_ref[...], image, preferred_element_type=F32)
            for side, value in enumerate(joined_columns(product)):
                value = value.astype(BF16)
                extra_ref[r, :, side * half : (side + 1) * half] = value
                value = value.astype(F32)
                totals = [totals[0] + value, totals[1] + value * value]
        one, two = lane_totals(*totals)
        sums_ref[0:1, :] = one
        sums_ref[1:2, :] = two


def late_kernel(rows, halos, slabs, small_ref, weight_ref, part_ref, extra_ref, sums_ref, own_edge_ref, *refs):
    near, _ = local_sources(rows, *refs[:3], refs[3 : 3 + halos], refs[3 + halos : 3 + 2 * halos])
    refs = refs[3 + 2 * halos :]
    late_own_ref, late_other_ref, own_halo_ref, other_halo_ref = refs[:4]
    conv_ref, message_ref, keys_ref, images_ref = refs[4:]
    extent = CHANNELS // 2
    arrived = (
        (late_own_ref, 0, [(own_halo_ref, h * extent) for h in range(halos)]),
        (late_other_ref, 0, [(other_halo_ref, h * extent) for h in range(halos)]),
    )
    odd = lax.axis_index("space") % 2 == 1
    slab = lax.axis_index("tm")
    first = lax.axis_index("chan") == 0
    half = part_ref.shape[2] // 2
    kept = rows // 2
    tail = halos * extent
    absent = slab == jnp.where(first, slabs - 1, 0)
    late_tail = jnp.where(absent, 0.0, own_halo_ref[tail:, :CHANNELS].astype(F32))
    own_tail = own_edge_ref[tail:, :CHANNELS].astype(F32)
    number = jnp.max(late_tail[2 * kept : 2 * kept + 1, :]) - 1.0
    ids = [number_at(small_ref, n) for n in range(2)]
    same = number == jnp.where(first, ids[1], ids[0])
    keep = jnp.where(jnp.logical_or(same, jnp.logical_not(first)), 1.0, 0.0)
    use_late = jnp.logical_or(same, first)
    choice = jnp.where(same, 0, 1)
    for r in range(-1, rows + 1):
        late = image_row(arrived, rows, odd, r)
        here = image_row(near, rows, odd, r)
        images_ref[r + 1] = jnp.where(use_late, late, here)
    totals = [jnp.zeros((CHANNELS, half), F32)] * 2
    for r in range(rows):
        image = jnp.concatenate([images_ref[r + i] for i in range(3)], axis=0)
        product = jnp.dot(weight_ref[choice], image, preferred_element_type=F32)
        for side, value in enumerate(joined_columns(product)):
            lanes = slice(side * half, (side + 1) * half)
            value = (value + keep * part_ref[r, :, lanes]).astype(BF16)
            conv_ref[r, :, lanes] = value
            value = value.astype(F32)
            totals = [totals[0] + value, totals[1] + value * value]
    one, two = lane_totals(*totals)
    main_id = jnp.where(first, number, ids[1])
    extra_id = jnp.where(slab == 0, ids[0], -1.0)
    line = lax.broadcasted_iota(jnp.int32, (8, CHANNELS), 0)
    sums = jnp.where(line == 0, one, 0.0)
    sums = jnp.where(line == 1, two, sums)
    sums = jnp.where(line == 2, sums_ref[0:1, :], sums)
    sums = jnp.where(line == 3, sums_ref[1:2, :], sums)
    sums = group_totals(sums)
    place = group_place()
    message = jnp.concatenate(
        [
            jnp.sum(jnp.where(line == jnp.broadcast_to(place, line.shape), sums, 0.0), axis=0, keepdims=True),
            jnp.where(place < 2, main_id, extra_id),
        ],
        axis=1,
    )
    message_ref[...] = jnp.broadcast_to(message, message_ref.shape)
    keys = jnp.zeros((8, CHANNELS), F32)
    for n in range(kept):
        main_key = jnp.where(first, late_tail[n : n + 1, :], own_tail[kept + n : kept + n + 1, :])
        keys = jnp.where(line == n, main_key, keys)
    quarter = kept // 2
    for n in range(quarter):
        extra_key = jnp.where(first, own_tail[n : n + 1, :], own_tail[quarter + n : quarter + n + 1, :])
        keys = jnp.where(line == kept + n, jnp.where(slab == 0, extra_key, 0.0), keys)
    keys_ref[...] = keys
    conv_ref[rows + kept, :ID_ROWS, :CHANNELS] = jnp.concatenate([keys] * 2, axis=0).astype(BF16)

    @pl.when(slab == 0)
    def _():
        conv_ref[rows : rows + kept] = extra_ref[...]


def crossed(slabs):
    return slabs in (2, 4)


def norm_kernel(
    rows, slabs, spaces, capacity, message_ref, keys_ref, gathered_ref, small_ref, out_matrix_ref, conv_ref, other_ref,
    *send_refs
):
    columns = conv_ref.shape[2]
    half = columns // 2
    kept = rows // 2
    part = MOMENTS // 2
    slab, space, chan = [lax.axis_index(name) for name in PART]
    count = float(rows * columns)
    sums, ids = gathered_ref[:, :CHANNELS], gathered_ref[:, CHANNELS:]
    place = group_place()
    beside = (slab * spaces + space) * 2 + 1 - chan
    line = lax.broadcasted_iota(jnp.int32, (gathered_ref.shape[0], 1), 0)
    numbers = [
        message_ref[0:1, CHANNELS : CHANNELS + 1],
        jnp.sum(jnp.where(line == beside, gathered_ref[:, CHANNELS : CHANNELS + 1], 0.0), axis=0, keepdims=True),
        message_ref[0:1, CHANNELS + 2 : CHANNELS + 3],
    ]
    lines = []
    for number in numbers:
        mask = ids == number
        picked = jnp.sum(jnp.where(mask, sums, 0.0), axis=0, keepdims=True)
        pixels = jnp.where(place == 0, count, jnp.where(place == 2, 0.5 * count, 0.0))
        held = jnp.sum(jnp.where(mask, pixels, 0.0), axis=0, keepdims=True)
        lines += [jnp.where(place % 2 == n, picked, 0.0) for n in range(2)] + [held]
    totals = group_totals(jnp.concatenate(lines + [jnp.zeros((7, CHANNELS), F32)], axis=0))
    matrix = out_matrix_ref[pl.ds(pl.multiple_of(chan * part, part), part), :]

    def factors(first):
        size = float(CHANNELS // GROUPS)
        counts = totals[first + 2 : first + 3, :] * size
        mean = totals[first : first + 1, :] / counts
        var = totals[first + 1 : first + 2, :] / counts - mean * mean
        scale = lax.rsqrt(var + 1e-06) * small_ref[0:1, :]
        offset = small_ref[1:2, :] - mean * scale
        return [jnp.broadcast_to(0.5 * value, (CHANNELS, CHANNELS)).T for value in (scale, offset)]

    def project(source_ref, first, lines, scale, offset):
        images = []
        for r in range(first, first + lines, 2):
            pieces = []
            for i in range(2):
                for j in range(2):
                    value = source_ref[r + i, :, j * half : (j + 1) * half].astype(F32)
                    value = value * scale + offset
                    pieces.append((value + value * jnp.tanh(value)).astype(BF16))
            images.append(jnp.concatenate(pieces, axis=0))
        image = jnp.concatenate(images, axis=1)
        return jnp.dot(matrix, image, preferred_element_type=F32)

    own_keys = keys_ref[...]
    other_keys = other_ref[rows + kept, :ID_ROWS, :CHANNELS].astype(F32)

    def blocks(latent, keys, first):
        return [
            (keys[first + n : first + n + 1, :], latent[:, n * half : (n + 1) * half])
            for n in range(latent.shape[1] // half)
        ]

    def spread(groups, started):
        for d in range(slabs):
            owner = (slab ^ d if crossed(slabs) else jnp.int32(d)).astype(F32)
            for j in range(capacity):
                wanted = owner * float(capacity) + float(j + 1)
                for first, group in groups:
                    ref = send_refs[d].at[first + j] if crossed(slabs) else send_refs[0].at[d, first + j]
                    value = ref[...].astype(F32) if started else jnp.zeros((part, half), F32)
                    for key, block in group:
                        value = jnp.where(key == wanted, block, value)
                    ref[...] = value.astype(BF16)

    mine = project(conv_ref, 0, rows, *factors(0))
    others = project(other_ref, 0, rows, *factors(3))
    second = chan == 1
    now = blocks(jnp.where(second, mine, others), jnp.where(second, own_keys, other_keys[:8, :]), 0)
    following = blocks(jnp.where(second, others, mine), jnp.where(second, other_keys[:8, :], own_keys), 0)
    spread(((0, now), (capacity, following)), False)

    @pl.when(slab == 0)
    def _():
        scale, offset = factors(6)
        begin = []
        for ref, keys in ((conv_ref, own_keys), (other_ref, other_keys)):
            begin += blocks(project(ref, rows, kept, scale, offset), keys, kept)
        spread(((0, begin),), True)


def merge_kernel(slabs, capacity, *refs):
    sources, owned_ref = refs[:-1], refs[-1]
    slab = lax.axis_index("tm")

    def source(d):
        if crossed(slabs):
            return slab ^ d, sources[d]
        return d, sources[0].at[d]

    for d in range(slabs):
        block, ref = source(d)
        for j in range(capacity):
            owned_ref[block * capacity + j] = ref[j]
    for d in range(slabs):
        block, ref = source(d)

        inside = block + 1 < slabs
        first = jnp.minimum(block + 1, slabs - 1) * capacity
        for j in range(capacity):
            value = jnp.where(inside, ref[capacity + j].astype(F32), 0.0)
            owned_ref[first + j] = (owned_ref[first + j].astype(F32) + value).astype(BF16)


def shards(activations, frame_clip, conv_weight, norm_gain, norm_bias, out_weight, owner):
    half, frames, rows, columns = activations.shape
    sizes = tuple(lax.axis_size(name) for name in PART)
    slabs, spaces, chans = sizes
    assert (frames, chans, half * chans) == (2, 2, CHANNELS)
    parts = slabs * spaces * chans
    halos = 1 if spaces <= 2 else 2
    send_rows = frames * (rows // 2)
    capacity = max(2, 2 * send_rows // slabs)
    kept = rows // 2
    assert send_rows == SEND_ROWS
    payload = jax.ShapeDtypeStruct((rows * half, columns), BF16)
    pair = jax.ShapeDtypeStruct((2 * half, columns), BF16)
    cross, same, both, *edges = whole_call(
        lambda *refs: front_kernel(rows, *refs),
        (payload, payload, jax.ShapeDtypeStruct((2 * rows * half, columns), BF16)) + (pair,) * halos,
        (activations.reshape(half * frames * rows, columns),),
        flops=3000000000,
    )
    own_halos = [space_swap(edge, sizes, start) for start, edge in enumerate(edges)]
    late_own = slab_swap(same, sizes, False)
    late_other = slab_swap(cross, sizes, True)
    turn = [(0, 1), (1, 0)]
    local_weight, late_weight, sum_weight, small, out_matrix = whole_call(
        weights_kernel,
        (
            jax.ShapeDtypeStruct((3 * CHANNELS, 6 * CHANNELS), BF16),
            jax.ShapeDtypeStruct((2, 3 * CHANNELS, 3 * CHANNELS), BF16),
            jax.ShapeDtypeStruct((3 * CHANNELS, 3 * CHANNELS), BF16),
            jax.ShapeDtypeStruct((8, CHANNELS), F32),
            jax.ShapeDtypeStruct((MOMENTS, 4 * CHANNELS), BF16),
        ),
        (
            frame_clip.reshape(1, frames), owner.reshape(1, send_rows), norm_gain.reshape(1, CHANNELS),
            norm_bias.reshape(1, CHANNELS), out_weight.transpose(0, 1, 3, 2), conv_weight, both,
        ),
        [
            pltpu.VMEM((1, frames), jnp.int32),
            pltpu.VMEM((1, send_rows), jnp.int32),
            pltpu.VMEM((1, CHANNELS), F32),
            pltpu.VMEM((1, CHANNELS), F32),
            pltpu.VMEM((2, 2, MOMENTS, CHANNELS), BF16),
            pltpu.VMEM((3, 3, 3, CHANNELS, CHANNELS), BF16),
            pltpu.SemaphoreType.DMA((5,)),
        ],
        [pl.BlockSpec(memory_space=pl.ANY)] * 5 + [VMEM] * 2,
        4800000000,
    )
    other = lax.ppermute(both, "chan", turn)
    message_halo = jax.ShapeDtypeStruct((halos * half + ID_ROWS, columns), BF16)
    *own_halos, cross_halo, same_halo = whole_call(
        lambda *refs: halo_kernel(halos, capacity, *refs[: 1 + halos], *refs[2 + halos :]),
        (pair,) * halos + (jax.ShapeDtypeStruct((halos * half, columns), BF16), message_halo),
        (small, *own_halos, other),
    )
    other_halos = [lax.ppermute(halo, "chan", turn) for halo in own_halos]
    late_own_halo = slab_swap(same_halo, sizes, False)
    late_other_halo = slab_swap(cross_halo, sizes, True)
    here = (cross, same, other, *own_halos, *other_halos)
    part, extra, extra_sums = whole_call(
        lambda *refs: local_kernel(rows, halos, *refs),
        (
            jax.ShapeDtypeStruct((rows, CHANNELS, columns), F32),
            jax.ShapeDtypeStruct((rows // 2, CHANNELS, columns), BF16),
            jax.ShapeDtypeStruct((8, CHANNELS), F32),
        ),
        (local_weight, sum_weight, *here),
        [pltpu.VMEM((rows // 2 + 2, CHANNELS, columns), BF16)],
        flops=1000000,
    )
    conv, message, keys = whole_call(
        lambda *refs: late_kernel(rows, halos, slabs, *refs),
        (
            jax.ShapeDtypeStruct((rows + kept + 1, CHANNELS, columns), BF16),
            jax.ShapeDtypeStruct((parts, 2 * CHANNELS), F32),
            jax.ShapeDtypeStruct((8, CHANNELS), F32),
        ),
        (
            small, late_weight, part, extra, extra_sums, same_halo, *here, late_own, late_other, late_own_halo, late_other_halo,
        ),
        [pltpu.VMEM((rows + 2, CHANNELS, columns), BF16)],
        flops=1500000000,
    )
    conv_other = lax.ppermute(conv, "chan", turn)
    gathered = lax.all_to_all(message, PART, split_axis=0, concat_axis=0, tiled=True)
    part = MOMENTS // chans
    width = columns // 2
    blocks = (2 * capacity, part, width)
    if crossed(slabs):
        shapes = (jax.ShapeDtypeStruct(blocks, BF16),) * slabs
    else:
        shapes = (jax.ShapeDtypeStruct((slabs,) + blocks, BF16),)
    sends = whole_call(
        lambda *refs: norm_kernel(rows, slabs, spaces, capacity, *refs),
        shapes,
        (message, keys, gathered, small, out_matrix, conv, conv_other),
    )
    if crossed(slabs):
        received = [sends[0]]
        for d in range(1, slabs):
            received.append(lax.ppermute(sends[d], "tm", [(t, t ^ d) for t in range(slabs)]))
    else:
        received = [lax.all_to_all(sends[0], "tm", split_axis=0, concat_axis=0, tiled=True)]
    turns = list((0, 3, 1, 2)) if crossed(slabs) else [0]
    owned = pl.pallas_call(
        lambda *refs: merge_kernel(slabs, capacity, *[refs[turns.index(d)] for d in range(len(turns))], refs[-1]),
        out_shape=jax.ShapeDtypeStruct((slabs * capacity, part, width), BF16),
        in_specs=[VMEM] * len(received),
        out_specs=pl.BlockSpec((slabs * capacity, part, width), lambda: (0, 0, 0)),
        compiler_params=PARAMS,
    )(*[received[d] for d in turns])
    return owned[None]


def solution(mesh):
    placed = (
        P(("groups", "chan"), "tm", "space", None),
        P(("groups", "tm")),
        P(),
        P(),
        P(),
        P(),
        P(("groups", "space"), "tm", None),
    )
    return jax.shard_map(
        shards,
        mesh=mesh,
        in_specs=placed,
        out_specs=P(("groups", "space"), "tm", "chan", None),
        check_vma=False,
    )
```

```python
import jax
import jax.numpy as jnp
import numpy as np
from jax import lax
from jax.experimental import pallas as pl
from jax.experimental.pallas import tpu as pltpu
from jax.sharding import PartitionSpec as P

CHANNELS = 128
GROUPS = 32
MOMENTS = 32
SEND_ROWS = 8
ID_ROWS = 16
BLOCK = 16
BF16 = jnp.bfloat16
F32 = jnp.float32
VMEM = pl.BlockSpec(memory_space=pltpu.VMEM)
PARAMS = pltpu.CompilerParams(vmem_limit_bytes=40 * 1024 * 1024)
PART = ("tm", "space", "chan")


def flat_pairs(sizes, pairs):
    _, spaces, chans = sizes
    return [
        ((a[0] * spaces + a[1]) * chans + a[2], (b[0] * spaces + b[1]) * chans + b[2])
        for a, b in pairs
    ]


def space_swap(value, sizes, start):
    slabs, spaces, chans = sizes
    pairs = []
    for low in range(start, spaces - 1, 2):
        for t in range(slabs):
            for c in range(chans):
                pairs += [((t, low, c), (t, low + 1, c)), ((t, low + 1, c), (t, low, c))]
    return lax.ppermute(value, PART, flat_pairs(sizes, pairs))


def slab_swap(value, sizes, cross):
    slabs, spaces, _ = sizes
    last = slabs - 1
    pairs = []
    for s in range(spaces):
        for t in range(last):
            if cross:
                pairs += [((t, s, 0), (t + 1, s, 1)), ((t + 1, s, 1), (t, s, 0))]
            else:
                pairs += [((t, s, 1), (t + 1, s, 1)), ((t + 1, s, 0), (t, s, 0))]
        if spaces % 2 == 0 and cross:
            pairs += [((0, s, 1), (0, s ^ 1, 1)), ((last, s, 0), (last, s ^ 1, 0))]
        elif spaces % 2 == 0:
            pairs += [((last, s, 1), (last, s, 0)), ((0, s, 0), (0, s, 1))]
    return lax.ppermute(value, PART, flat_pairs(sizes, pairs))


def whole_call(kernel, out_shape, args, scratch=(), specs=None, flops=0, vmem=40, first=()):
    turns = list(first) + [n for n in range(len(args)) if n not in first]
    specs = specs or [VMEM] * len(args)

    def turned(*refs):
        kernel(*[refs[turns.index(n)] for n in range(len(args))], *refs[len(args) :])

    return pl.pallas_call(
        turned,
        out_shape=out_shape,
        in_specs=[specs[n] for n in turns],
        out_specs=jax.tree.map(lambda _: VMEM, out_shape),
        scratch_shapes=scratch,
        compiler_params=pltpu.CompilerParams(vmem_limit_bytes=vmem * 1024 * 1024),
        cost_estimate=pl.CostEstimate(flops=flops, bytes_accessed=flops // 400, transcendentals=0),
    )(*[args[n] for n in turns])


def number_at(small_ref, n):
    lane = lax.broadcasted_iota(jnp.int32, (1, CHANNELS), 1)
    return jnp.sum(jnp.where(lane == n, small_ref[2:3, :], 0.0))


def front_kernel(rows, pixels_ref, cross_ref, same_ref, both_ref, *edge_refs):
    chan = lax.axis_index("chan")
    odd = lax.axis_index("space") % 2 == 1
    half, columns = CHANNELS // 2, pixels_ref.shape[1]
    size = 2 * rows * BLOCK
    source = lax.broadcasted_iota(jnp.int32, (columns, columns), 0)
    target = lax.broadcasted_iota(jnp.int32, (1, columns), 1)
    wanted = jnp.where(target < columns // 2, 2 * target, 2 * target - columns + 1)
    split = jnp.where(source == wanted, 1.0, 0.0).astype(BF16)
    placed = lax.broadcasted_iota(jnp.int32, (size, size), 1)
    line = lax.broadcasted_iota(jnp.int32, (size, 1), 0)
    second = line // (rows * BLOCK)
    frame = jnp.where(second == 0, 1 - chan, chan)
    row = line // BLOCK % rows
    origin = line % BLOCK * (2 * rows) + frame * rows + row
    turn = jnp.where(placed == origin, 1.0, 0.0).astype(BF16)
    inside = rows * half
    for n in range(half // BLOCK):
        image = pixels_ref[n * size : (n + 1) * size, :]
        image = jnp.dot(turn, image, preferred_element_type=F32).astype(BF16)
        image = jnp.dot(image, split, preferred_element_type=F32).astype(BF16)
        for f, out_ref in enumerate((cross_ref, same_ref)):
            for r in range(rows):
                first = (f * rows + r) * BLOCK
                block = image[first : first + BLOCK, :]
                first = r * half + n * BLOCK
                out_ref[first : first + BLOCK, :] = block
                both_ref[f * inside + first : f * inside + first + BLOCK, :] = block
    for f, out_ref in enumerate((cross_ref, same_ref)):
        low, high = out_ref[:half, :], out_ref[(rows - 1) * half :, :]
        for h, edge_ref in enumerate(edge_refs):
            to_low = odd if h == 0 else jnp.logical_not(odd)
            edge_ref[f * half : (f + 1) * half, :] = jnp.where(to_low, low, high)


def halo_kernel(halos, capacity, small_ref, *refs):
    halo_refs, kept_refs, (cross_ref, same_ref) = refs[:halos], refs[halos : 2 * halos], refs[2 * halos :]
    for halo_ref, kept_ref in zip(halo_refs, kept_refs):
        kept_ref[...] = halo_ref[...]
    chan = lax.axis_index("chan")
    half, columns = CHANNELS // 2, cross_ref.shape[1]
    count = SEND_ROWS
    line = lax.broadcasted_iota(jnp.int32, (ID_ROWS, CHANNELS), 0)
    lane = lax.broadcasted_iota(jnp.int32, (ID_ROWS, CHANNELS), 1)
    owners = jnp.broadcast_to(small_ref[3:4, :], (ID_ROWS, CHANNELS))
    mine = jnp.sum(jnp.where(line == lane, owners, 0.0), axis=1, keepdims=True)
    rank = jnp.sum(jnp.where((owners == mine) & (lane < line), 1.0, 0.0), axis=1, keepdims=True)
    keys = mine * float(capacity) + rank + 1.0
    place = lax.broadcasted_iota(jnp.int32, (ID_ROWS, columns), 0)
    tail = jnp.where(place < count, keys, 0.0)
    ids = [number_at(small_ref, n) for n in range(2)]
    for n, (out_ref, frame) in enumerate(((cross_ref, 1 - chan), (same_ref, chan))):
        for h in range(halos):
            out_ref[h * half : (h + 1) * half, :] = halo_refs[h][n * half : (n + 1) * half, :]
        number = jnp.where(frame == 0, ids[0], ids[1])
        if n == 1:
            out_ref[halos * half :, :] = jnp.where(place == count, number + 1.0, tail).astype(BF16)


def weights_kernel(
    ids_any, owner_any, gain_any, bias_any, out_weight_any, weight_ref, _, local_ref, late_ref, sum_ref, small_ref,
    out_matrix_ref, ids_ref, owner_ref, gain_ref, bias_ref, out_weight_ref, taps_ref, copies
):
    chan = lax.axis_index("chan")
    fetched = [
        pltpu.make_async_copy(source, target, copies.at[n])
        for n, (source, target) in enumerate(
            (
                (ids_any, ids_ref),
                (owner_any, owner_ref),
                (gain_any, gain_ref),
                (bias_any, bias_ref),
                (out_weight_any, out_weight_ref),
            )
        )
    ]
    for copy in fetched:
        copy.start()
    half = CHANNELS // 2
    own = pl.multiple_of(chan * half, half)
    other = pl.multiple_of((1 - chan) * half, half)
    for j in range(3):
        for i in range(3):
            for k in range(3):
                block = jnp.concatenate(
                    [weight_ref[k, i, j, pl.ds(own, half), :], weight_ref[k, i, j, pl.ds(other, half), :]],
                    axis=0,
                )
                taps_ref[k, i, j] = block.T
    for copy in fetched:
        copy.wait()
    small_ref[...] = jnp.zeros_like(small_ref)
    small_ref[0:1, :] = gain_ref[...]
    small_ref[1:2, :] = bias_ref[...]
    small_ref[2:3, : ids_ref.shape[1]] = ids_ref[...].astype(F32)
    small_ref[3:4, :SEND_ROWS] = owner_ref[...].astype(F32)
    for i in range(2):
        for j in range(2):
            first = (2 * i + j) * CHANNELS
            out_matrix_ref[:, first : first + CHANNELS] = out_weight_ref[i, j]
    zero = jnp.float32(0.0)
    one = jnp.float32(1.0)
    first = chan == 0
    joined = number_at(small_ref, 0) == number_at(small_ref, 1)
    flag = jnp.where(joined, one, zero)
    on_first = jnp.where(first, one, zero)
    on_second = one - on_first
    near = (
        on_first * (one - flag),
        on_first + on_second * flag,
        zero,
    )
    far = (
        on_first * flag + on_second * (one - flag),
        on_second * (one - flag),
        on_second,
    )
    late_same = (on_second * flag, zero, on_first)
    late_apart = (on_first + on_second * flag, on_first, on_first)
    for j in range(3):
        for i in range(3):
            taps = [taps_ref[k, i, j].astype(F32) for k in range(3)]

            def mixed(scale):
                return (taps[0] * scale[0] + taps[1] * scale[1] + taps[2] * scale[2]).astype(BF16)

            rows = slice(j * CHANNELS, (j + 1) * CHANNELS)
            columns = slice(i * CHANNELS, (i + 1) * CHANNELS)
            shifted = slice((3 + i) * CHANNELS, (4 + i) * CHANNELS)
            local_ref[rows, columns] = mixed(near)
            local_ref[rows, shifted] = mixed(far)
            late_ref[0, rows, columns] = mixed(late_same)
            late_ref[1, rows, columns] = mixed(late_apart)
            sum_ref[rows, columns] = mixed((one, one, one))


def image_row(sources, rows, odd, r):
    half = CHANNELS // 2
    pieces = []
    for ref, start, halos in sources:
        if 0 <= r < rows:
            pieces.append(ref[start + r * half : start + (r + 1) * half, :])
            continue
        edges = [halo_ref[first : first + half, :] for halo_ref, first in halos]
        edges.append(jnp.zeros_like(edges[0]))
        on_first = odd if r < 0 else jnp.logical_not(odd)
        pieces.append(jnp.where(on_first, edges[0], edges[1]))
    return jnp.concatenate(pieces, axis=0)


def local_sources(rows, cross_ref, same_ref, other_ref, own_halos, other_halos):
    half = CHANNELS // 2
    inside = rows * half
    near = (
        (cross_ref, 0, [(ref, 0) for ref in own_halos]),
        (other_ref, inside, [(ref, half) for ref in other_halos]),
    )
    far = (
        (same_ref, 0, [(ref, half) for ref in own_halos]),
        (other_ref, 0, [(ref, 0) for ref in other_halos]),
    )
    return near, far


def joined_columns(product):
    half = product.shape[1] // 2
    left = product[:CHANNELS, :]
    middle = product[CHANNELS : 2 * CHANNELS, :]
    right = product[2 * CHANNELS :, :]
    lane = lax.broadcasted_iota(jnp.int32, (CHANNELS, half), 1)
    from_left = jnp.where(lane == 0, 0.0, pltpu.roll(left[:, half:], 1, 1))
    from_right = jnp.where(lane == half - 1, 0.0, pltpu.roll(right[:, :half], half - 1, 1))
    even = from_left + middle[:, :half] + right[:, half:]
    odd = left[:, :half] + middle[:, half:] + from_right
    return even, odd


def group_place():
    return lax.broadcasted_iota(jnp.int32, (1, CHANNELS), 1) % (CHANNELS // GROUPS)


def group_totals(lines):
    lane = lax.broadcasted_iota(jnp.int32, lines.shape, 1)
    step = 1
    while step < CHANNELS // GROUPS:
        ahead = pltpu.roll(lines, CHANNELS - step, 1)
        behind = pltpu.roll(lines, step, 1)
        lines = lines + jnp.where(lane // step % 2 == 0, ahead, behind)
        step *= 2
    return lines


def lane_totals(first, second):
    rows = [jnp.sum(value.T, axis=0, keepdims=True) for value in (first, second)]
    return rows


def local_kernel(rows, halos, weight_ref, sum_ref, *refs):
    conv_ref, extra_ref, sums_ref, images_ref = refs[3 + 2 * halos :]
    near, far = local_sources(rows, *refs[:3], refs[3 : 3 + halos], refs[3 + halos : 3 + 2 * halos])
    odd = lax.axis_index("space") % 2 == 1
    chan = lax.axis_index("chan")
    half = conv_ref.shape[2] // 2
    for r in range(rows):
        image = jnp.concatenate(
            [image_row(frame, rows, odd, r + i) for frame in (near, far) for i in (-1, 0, 1)], axis=0
        )
        product = jnp.dot(weight_ref[...], image, preferred_element_type=F32)
        for side, value in enumerate(joined_columns(product)):
            conv_ref[r, :, side * half : (side + 1) * half] = value
    sums_ref[...] = jnp.zeros_like(sums_ref)

    @pl.when(lax.axis_index("tm") == 0)
    def _():
        rows_here = rows // 2
        for n in range(rows_here + 2):
            upper = image_row(far, rows, odd, n - 1)
            lower = image_row(near, rows, odd, rows_here + n - 1)
            images_ref[n] = jnp.where(chan == 0, upper, lower)
        totals = [jnp.zeros((CHANNELS, half), F32)] * 2
        for r in range(rows_here):
            image = jnp.concatenate([images_ref[r + i] for i in range(3)], axis=0)
            product = jnp.dot(sum_ref[...], image, preferred_element_type=F32)
            for side, value in enumerate(joined_columns(product)):
                value = value.astype(BF16)
                extra_ref[r, :, side * half : (side + 1) * half] = value
                value = value.astype(F32)
                totals = [totals[0] + value, totals[1] + value * value]
        one, two = lane_totals(*totals)
        sums_ref[0:1, :] = one
        sums_ref[1:2, :] = two


def late_kernel(rows, halos, slabs, small_ref, weight_ref, part_ref, extra_ref, sums_ref, own_edge_ref, *refs):
    near, _ = local_sources(rows, *refs[:3], refs[3 : 3 + halos], refs[3 + halos : 3 + 2 * halos])
    refs = refs[3 + 2 * halos :]
    late_own_ref, late_other_ref, own_halo_ref, other_halo_ref = refs[:4]
    conv_ref, message_ref, keys_ref, images_ref = refs[4:]
    extent = CHANNELS // 2
    arrived = (
        (late_own_ref, 0, [(own_halo_ref, h * extent) for h in range(halos)]),
        (late_other_ref, 0, [(other_halo_ref, h * extent) for h in range(halos)]),
    )
    odd = lax.axis_index("space") % 2 == 1
    slab = lax.axis_index("tm")
    first = lax.axis_index("chan") == 0
    half = part_ref.shape[2] // 2
    kept = rows // 2
    tail = halos * extent
    absent = slab == jnp.where(first, slabs - 1, 0)
    late_tail = jnp.where(absent, 0.0, own_halo_ref[tail:, :CHANNELS].astype(F32))
    own_tail = own_edge_ref[tail:, :CHANNELS].astype(F32)
    number = jnp.max(late_tail[2 * kept : 2 * kept + 1, :]) - 1.0
    ids = [number_at(small_ref, n) for n in range(2)]
    same = number == jnp.where(first, ids[1], ids[0])
    keep = jnp.where(jnp.logical_or(same, jnp.logical_not(first)), 1.0, 0.0)
    use_late = jnp.logical_or(same, first)
    choice = jnp.where(same, 0, 1)
    for r in range(-1, rows + 1):
        late = image_row(arrived, rows, odd, r)
        here = image_row(near, rows, odd, r)
        images_ref[r + 1] = jnp.where(use_late, late, here)
    totals = [jnp.zeros((CHANNELS, half), F32)] * 2
    for r in range(rows):
        image = jnp.concatenate([images_ref[r + i] for i in range(3)], axis=0)
        product = jnp.dot(weight_ref[choice], image, preferred_element_type=F32)
        for side, value in enumerate(joined_columns(product)):
            lanes = slice(side * half, (side + 1) * half)
            value = (value + keep * part_ref[r, :, lanes]).astype(BF16)
            conv_ref[r, :, lanes] = value
            value = value.astype(F32)
            totals = [totals[0] + value, totals[1] + value * value]
    one, two = lane_totals(*totals)
    main_id = jnp.where(first, number, ids[1])
    extra_id = jnp.where(slab == 0, ids[0], -1.0)
    line = lax.broadcasted_iota(jnp.int32, (8, CHANNELS), 0)
    sums = jnp.where(line == 0, one, 0.0)
    sums = jnp.where(line == 1, two, sums)
    sums = jnp.where(line == 2, sums_ref[0:1, :], sums)
    sums = jnp.where(line == 3, sums_ref[1:2, :], sums)
    sums = group_totals(sums)
    place = group_place()
    message = jnp.concatenate(
        [
            jnp.sum(jnp.where(line == jnp.broadcast_to(place, line.shape), sums, 0.0), axis=0, keepdims=True),
            jnp.where(place < 2, main_id, extra_id),
        ],
        axis=1,
    )
    message_ref[...] = jnp.broadcast_to(message, message_ref.shape)
    keys = jnp.zeros((8, CHANNELS), F32)
    for n in range(kept):
        main_key = jnp.where(first, late_tail[n : n + 1, :], own_tail[kept + n : kept + n + 1, :])
        keys = jnp.where(line == n, main_key, keys)
    quarter = kept // 2
    for n in range(quarter):
        extra_key = jnp.where(first, own_tail[n : n + 1, :], own_tail[quarter + n : quarter + n + 1, :])
        keys = jnp.where(line == kept + n, jnp.where(slab == 0, extra_key, 0.0), keys)
    keys_ref[...] = keys
    conv_ref[rows + kept, :ID_ROWS, :CHANNELS] = jnp.concatenate([keys] * 2, axis=0).astype(BF16)

    @pl.when(slab == 0)
    def _():
        conv_ref[rows : rows + kept] = extra_ref[...]


def crossed(slabs):
    return slabs in (2, 4)


def norm_kernel(
    rows, slabs, spaces, capacity, message_ref, keys_ref, gathered_ref, small_ref, out_matrix_ref, conv_ref, other_ref,
    *send_refs
):
    columns = conv_ref.shape[2]
    half = columns // 2
    kept = rows // 2
    part = MOMENTS // 2
    slab, space, chan = [lax.axis_index(name) for name in PART]
    count = float(rows * columns)
    sums, ids = gathered_ref[:, :CHANNELS], gathered_ref[:, CHANNELS:]
    place = group_place()
    beside = (slab * spaces + space) * 2 + 1 - chan
    line = lax.broadcasted_iota(jnp.int32, (gathered_ref.shape[0], 1), 0)
    numbers = [
        message_ref[0:1, CHANNELS : CHANNELS + 1],
        jnp.sum(jnp.where(line == beside, gathered_ref[:, CHANNELS : CHANNELS + 1], 0.0), axis=0, keepdims=True),
        message_ref[0:1, CHANNELS + 2 : CHANNELS + 3],
    ]
    lines = []
    for number in numbers:
        mask = ids == number
        picked = jnp.sum(jnp.where(mask, sums, 0.0), axis=0, keepdims=True)
        pixels = jnp.where(place == 0, count, jnp.where(place == 2, 0.5 * count, 0.0))
        held = jnp.sum(jnp.where(mask, pixels, 0.0), axis=0, keepdims=True)
        lines += [jnp.where(place % 2 == n, picked, 0.0) for n in range(2)] + [held]
    totals = group_totals(jnp.concatenate(lines + [jnp.zeros((7, CHANNELS), F32)], axis=0))
    matrix = out_matrix_ref[pl.ds(pl.multiple_of(chan * part, part), part), :]

    def factors(first):
        size = float(CHANNELS // GROUPS)
        counts = totals[first + 2 : first + 3, :] * size
        mean = totals[first : first + 1, :] / counts
        var = totals[first + 1 : first + 2, :] / counts - mean * mean
        scale = lax.rsqrt(var + 1e-06) * small_ref[0:1, :]
        offset = small_ref[1:2, :] - mean * scale
        return [jnp.broadcast_to(0.5 * value, (CHANNELS, CHANNELS)).T for value in (scale, offset)]

    def project(source_ref, first, lines, scale, offset):
        images = []
        for r in range(first, first + lines, 2):
            pieces = []
            for i in range(2):
                for j in range(2):
                    value = source_ref[r + i, :, j * half : (j + 1) * half].astype(F32)
                    value = value * scale + offset
                    pieces.append((value + value * jnp.tanh(value)).astype(BF16))
            images.append(jnp.concatenate(pieces, axis=0))
        image = jnp.concatenate(images, axis=1)
        return jnp.dot(matrix, image, preferred_element_type=F32)

    own_keys = keys_ref[...]
    other_keys = other_ref[rows + kept, :ID_ROWS, :CHANNELS].astype(F32)

    def blocks(latent, keys, first):
        return [
            (keys[first + n : first + n + 1, :], latent[:, n * half : (n + 1) * half])
            for n in range(latent.shape[1] // half)
        ]

    def spread(groups, started):
        for d in range(slabs):
            owner = (slab ^ d if crossed(slabs) else jnp.int32(d)).astype(F32)
            for j in range(capacity):
                wanted = owner * float(capacity) + float(j + 1)
                for first, group in groups:
                    ref = send_refs[d].at[first + j] if crossed(slabs) else send_refs[0].at[d, first + j]
                    value = ref[...].astype(F32) if started else jnp.zeros((part, half), F32)
                    for key, block in group:
                        value = jnp.where(key == wanted, block, value)
                    ref[...] = value.astype(BF16)

    mine = project(conv_ref, 0, rows, *factors(0))
    others = project(other_ref, 0, rows, *factors(3))
    second = chan == 1
    now = blocks(jnp.where(second, mine, others), jnp.where(second, own_keys, other_keys[:8, :]), 0)
    following = blocks(jnp.where(second, others, mine), jnp.where(second, other_keys[:8, :], own_keys), 0)
    spread(((0, now), (capacity, following)), False)

    @pl.when(slab == 0)
    def _():
        scale, offset = factors(6)
        begin = []
        for ref, keys in ((conv_ref, own_keys), (other_ref, other_keys)):
            begin += blocks(project(ref, rows, kept, scale, offset), keys, kept)
        spread(((0, begin),), True)


def merge_kernel(slabs, capacity, *refs):
    sources, owned_ref = refs[:-1], refs[-1]
    slab = lax.axis_index("tm")

    def source(d):
        if crossed(slabs):
            return slab ^ d, sources[d]
        return d, sources[0].at[d]

    for d in range(slabs):
        block, ref = source(d)
        for j in range(capacity):
            owned_ref[block * capacity + j] = ref[j]
    for d in range(slabs):
        block, ref = source(d)

        inside = block + 1 < slabs
        first = jnp.minimum(block + 1, slabs - 1) * capacity
        for j in range(capacity):
            value = jnp.where(inside, ref[capacity + j].astype(F32), 0.0)
            owned_ref[first + j] = (owned_ref[first + j].astype(F32) + value).astype(BF16)


def shards(activations, frame_clip, conv_weight, norm_gain, norm_bias, out_weight, owner):
    half, frames, rows, columns = activations.shape
    sizes = tuple(lax.axis_size(name) for name in PART)
    slabs, spaces, chans = sizes
    assert (frames, chans, half * chans) == (2, 2, CHANNELS)
    parts = slabs * spaces * chans
    halos = 1 if spaces <= 2 else 2
    send_rows = frames * (rows // 2)
    capacity = max(2, 2 * send_rows // slabs)
    kept = rows // 2
    assert send_rows == SEND_ROWS
    payload = jax.ShapeDtypeStruct((rows * half, columns), BF16)
    pair = jax.ShapeDtypeStruct((2 * half, columns), BF16)
    cross, same, both, *edges = whole_call(
        lambda *refs: front_kernel(rows, *refs),
        (payload, payload, jax.ShapeDtypeStruct((2 * rows * half, columns), BF16)) + (pair,) * halos,
        (activations.reshape(half * frames * rows, columns),),
        flops=3000000000,
    )
    own_halos = [space_swap(edge, sizes, start) for start, edge in enumerate(edges)]
    late_own = slab_swap(same, sizes, False)
    late_other = slab_swap(cross, sizes, True)
    turn = [(0, 1), (1, 0)]
    local_weight, late_weight, sum_weight, small, out_matrix = whole_call(
        weights_kernel,
        (
            jax.ShapeDtypeStruct((3 * CHANNELS, 6 * CHANNELS), BF16),
            jax.ShapeDtypeStruct((2, 3 * CHANNELS, 3 * CHANNELS), BF16),
            jax.ShapeDtypeStruct((3 * CHANNELS, 3 * CHANNELS), BF16),
            jax.ShapeDtypeStruct((8, CHANNELS), F32),
            jax.ShapeDtypeStruct((MOMENTS, 4 * CHANNELS), BF16),
        ),
        (
            frame_clip.reshape(1, frames), owner.reshape(1, send_rows), norm_gain.reshape(1, CHANNELS),
            norm_bias.reshape(1, CHANNELS), out_weight.transpose(0, 1, 3, 2), conv_weight, both,
        ),
        [
            pltpu.VMEM((1, frames), jnp.int32),
            pltpu.VMEM((1, send_rows), jnp.int32),
            pltpu.VMEM((1, CHANNELS), F32),
            pltpu.VMEM((1, CHANNELS), F32),
            pltpu.VMEM((2, 2, MOMENTS, CHANNELS), BF16),
            pltpu.VMEM((3, 3, 3, CHANNELS, CHANNELS), BF16),
            pltpu.SemaphoreType.DMA((5,)),
        ],
        [pl.BlockSpec(memory_space=pl.ANY)] * 5 + [VMEM] * 2,
        4800000000,
    )
    other = lax.ppermute(both, "chan", turn)
    message_halo = jax.ShapeDtypeStruct((halos * half + ID_ROWS, columns), BF16)
    *own_halos, cross_halo, same_halo = whole_call(
        lambda *refs: halo_kernel(halos, capacity, *refs[: 1 + halos], *refs[2 + halos :]),
        (pair,) * halos + (jax.ShapeDtypeStruct((halos * half, columns), BF16), message_halo),
        (small, *own_halos, other),
    )
    other_halos = [lax.ppermute(halo, "chan", turn) for halo in own_halos]
    late_own_halo = slab_swap(same_halo, sizes, False)
    late_other_halo = slab_swap(cross_halo, sizes, True)
    here = (cross, same, other, *own_halos, *other_halos)
    part, extra, extra_sums = whole_call(
        lambda *refs: local_kernel(rows, halos, *refs),
        (
            jax.ShapeDtypeStruct((rows, CHANNELS, columns), F32),
            jax.ShapeDtypeStruct((rows // 2, CHANNELS, columns), BF16),
            jax.ShapeDtypeStruct((8, CHANNELS), F32),
        ),
        (local_weight, sum_weight, *here),
        [pltpu.VMEM((rows // 2 + 2, CHANNELS, columns), BF16)],
        flops=1000000,
    )
    conv, message, keys = whole_call(
        lambda *refs: late_kernel(rows, halos, slabs, *refs),
        (
            jax.ShapeDtypeStruct((rows + kept + 1, CHANNELS, columns), BF16),
            jax.ShapeDtypeStruct((parts, 2 * CHANNELS), F32),
            jax.ShapeDtypeStruct((8, CHANNELS), F32),
        ),
        (
            small, late_weight, part, extra, extra_sums, same_halo, *here, late_own, late_other, late_own_halo, late_other_halo,
        ),
        [pltpu.VMEM((rows + 2, CHANNELS, columns), BF16)],
        flops=1500000000,
    )
    conv_other = lax.ppermute(conv, "chan", turn)
    gathered = lax.all_to_all(message, PART, split_axis=0, concat_axis=0, tiled=True)
    part = MOMENTS // chans
    width = columns // 2
    blocks = (2 * capacity, part, width)
    if crossed(slabs):
        shapes = (jax.ShapeDtypeStruct(blocks, BF16),) * slabs
    else:
        shapes = (jax.ShapeDtypeStruct((slabs,) + blocks, BF16),)
    sends = whole_call(
        lambda *refs: norm_kernel(rows, slabs, spaces, capacity, *refs),
        shapes,
        (message, keys, gathered, small, out_matrix, conv, conv_other),
    )
    if crossed(slabs):
        received = [sends[0]]
        for d in range(1, slabs):
            received.append(lax.ppermute(sends[d], "tm", [(t, t ^ d) for t in range(slabs)]))
    else:
        received = [lax.all_to_all(sends[0], "tm", split_axis=0, concat_axis=0, tiled=True)]
    turns = list((0, 2, 1, 3)) if crossed(slabs) else [0]
    owned = pl.pallas_call(
        lambda *refs: merge_kernel(slabs, capacity, *[refs[turns.index(d)] for d in range(len(turns))], refs[-1]),
        out_shape=jax.ShapeDtypeStruct((slabs * capacity, part, width), BF16),
        in_specs=[VMEM] * len(received),
        out_specs=pl.BlockSpec((slabs * capacity, part, width), lambda: (0, 0, 0)),
        compiler_params=PARAMS,
    )(*[received[d] for d in turns])
    return owned[None]


def solution(mesh):
    placed = (
        P(("groups", "chan"), "tm", "space", None),
        P(("groups", "tm")),
        P(),
        P(),
        P(),
        P(),
        P(("groups", "space"), "tm", None),
    )
    return jax.shard_map(
        shards,
        mesh=mesh,
        in_specs=placed,
        out_specs=P(("groups", "space"), "tm", "chan", None),
        check_vma=False,
    )
```
